32 devices in a mesh: dom: 8 (over z, y), chan: 4 (over x, core).
Axes of the slice: x: 2, y: 2, z: 4, core: 2. Of those that a mesh axis runs over, the one named last changes fastest.
Arguments:
- features: bfloat16 [256, 8192], P('chan', 'dom'), may hold values from -6 to 6
- cotangent: bfloat16 [256, 8192], P('chan', 'dom'), may hold values from -6 to 6
- weights: bfloat16 [9, 256, 256], P(None, 'chan'), may hold values from -0.375 to 0.375
- tile_values: float32 [512, 128, 128], P('dom'), may hold values from -0.046875 to 0.046875
- tile_cols: int32 [8, 8, 8], P('dom'), may hold values from 0 to 11, as said below
- send_list: int32 [8, 4, 128], P('dom'), may hold values from 0 to 1023
Outputs:
- input_grad: float32 [256, 8192], P('chan', 'dom')
- weight_grad: float32 [9, 256, 256], P(None, None, 'chan')
The draws below stay inside these ranges and needn't reach their ends.
Inputs may be any that keep to these rules, and one draw needn't show every extreme that they name: `tile_cols`: values below 8 are blocks of the partition's own nodes; 8 + s is the block received from neighbour slot s. Tile 0 of row block r has column block r.
All inputs are finite; a program needn't handle non-finite values.
Results may differ from the reference program's by a relative error of at most 0.0003.
Values may be sent and summed in bfloat16 or wider, within the bound.
No kernel may reach another device: no remote copies, remote signals or barrier semaphores. Data moves between devices by JAX's collectives and lax.ppermute only.
A program may use at most 128 MiB of HBM per device.

```python
import jax
import jax.numpy as jnp
from jax import lax

C = 256
TILE = 128
ORDER = 8
TPR = 8
NB_DEV = 8
PARTITIONS = 8
NODES = 8192
TILES = 512


def draw_tile_cols(key, part):
    columns = jax.random.randint(key, (PARTITIONS, NB_DEV, TPR), 0, NB_DEV).astype(jnp.int32)
    row_ids = jnp.arange(NB_DEV, dtype=jnp.int32)[None, :]
    columns = columns.at[:, :, 0].set(row_ids)
    columns = columns.at[:, :, TPR - 2].set(NB_DEV + row_ids % 4)
    columns = columns.at[:, :, TPR - 1].set(NB_DEV + (row_ids + 2) % 4)
    return columns.astype(jnp.int32)


def set_ends(array, key, smallest, high):
    index_at = [jax.random.randint(jax.random.fold_in(key, axis), (), 0, length) for axis, length in enumerate(array.shape)]
    longest = array.shape.index(max(array.shape))
    beside = index_at[:longest] + [(index_at[longest] + 1) % array.shape[longest]] + index_at[longest + 1:]
    return array.at[tuple(index_at)].set(smallest).at[tuple(beside)].set(high)


def level_of(stream_key, extent, split, low, top_value):
    level, own = 1.0, jax.random.fold_in(stream_key, 6)
    for position, blocks in split:
        steps = jnp.exp(jax.random.uniform(jax.random.fold_in(own, position), (blocks,), jnp.float32, low / len(split), top_value / len(split)))
        level = level * jnp.repeat(steps, extent[position] // blocks).reshape([-1 if axis == position else 1 for axis in range(len(extent))])
    return level


def bell_draw(rng, shape, scale, bound, pieces=(), held_as=jnp.bfloat16):
    values = scale * jax.random.normal(rng, shape, jnp.float32)
    if pieces:
        values = values * level_of(rng, shape, pieces, -0.22, 0.18)
    return jnp.clip(values, -bound, bound).astype(held_as)


def setup_inputs(seed: int = 0) -> dict:
    key_list = jax.random.split(jax.random.key(seed), 7)
    return {
        "features": bell_draw(key_list[0], (C, NODES), 1.0, 6.0, ((0, 4), (1, 8))),
        "cotangent": bell_draw(key_list[1], (C, NODES), 1.0, 6.0, ((0, 4), (1, 8))),
        "weights": bell_draw(key_list[2], (ORDER + 1, C, C), C ** -0.5, 0.375, ((1, 4),)),
        "tile_values": bell_draw(key_list[3], (TILES, TILE, TILE), (16 * TPR * TILE) ** -0.5, 0.046875, ((0, 8),), jnp.float32),
        "tile_cols": draw_tile_cols(jax.random.fold_in(key_list[6], 71), 0),
        "send_list": set_ends(jax.random.randint(key_list[5], (PARTITIONS, 4, TILE), 0, NB_DEV * TILE), jax.random.fold_in(key_list[5], 1), 0, (NB_DEV * TILE) - 1).astype(jnp.int32),
    }


NEIGHBOUR_SHIFTS = (1, -1, 2, -2)


def take_rows(source_part, row_ids):
    return jnp.take(source_part, row_ids, axis=1)


def apply_operator(field_in, tile_values, tile_cols, send_list):
    channels = field_in.shape[0]
    local_nodes = NB_DEV * TILE
    by_part = field_in.reshape(channels, PARTITIONS, local_nodes).transpose(1, 0, 2)
    halos = []
    for slot_index, offset in enumerate(NEIGHBOUR_SHIFTS):
        source = jnp.roll(by_part, offset, axis=0)
        row_ids = jnp.roll(send_list[:, slot_index, :], offset, axis=0).astype(jnp.int32)
        halos.append(jax.vmap(take_rows)(source, row_ids))
    extended = jnp.concatenate([by_part] + halos, axis=2)
    tiles_part = tile_values.reshape(PARTITIONS, NB_DEV * TPR, TILE, TILE)
    cols_part = tile_cols.reshape(PARTITIONS, NB_DEV * TPR).astype(jnp.int32)

    def one_part(operands):
        ext_part, tile_part, col_part = operands
        blocks = ext_part.reshape(channels, NB_DEV + 4, TILE)
        picked = jnp.take(blocks, col_part, axis=1)
        product = jnp.einsum('ctj,tjk->ctk', picked, tile_part, precision=lax.Precision.HIGHEST)
        return product.reshape(channels, NB_DEV, TPR, TILE).sum(axis=2).reshape(channels, local_nodes)

    result = lax.map(one_part, (extended, tiles_part, cols_part))
    return result.transpose(1, 0, 2).reshape(channels, PARTITIONS * local_nodes)


def reference(features, cotangent, weights, tile_values, tile_cols, send_list):
    feat_wide = features.astype(jnp.float32)
    cot_wide = cotangent.astype(jnp.float32)

    def operator_on(field_in):
        return apply_operator(field_in, tile_values, tile_cols, send_list)

    def mixed_term(order_index):
        return jnp.dot(weights[order_index].astype(jnp.float32), cot_wide, precision=lax.Precision.HIGHEST)

    def grad_term(state):
        return lax.dot_general(feat_wide, state, (((1,), (1,)), ((), ())), precision=lax.Precision.HIGHEST)

    cheb_prev = cot_wide
    grad_terms = [grad_term(cheb_prev)]
    cheb_now = operator_on(cheb_prev)
    grad_terms.append(grad_term(cheb_now))
    for order_index in range(2, ORDER + 1):
        cheb_prev, cheb_now = cheb_now, 2.0 * operator_on(cheb_now) - cheb_prev
        grad_terms.append(grad_term(cheb_now))
    current = mixed_term(ORDER)
    clen_later = jnp.zeros_like(current)
    for order_index in range(ORDER - 1, 0, -1):
        current, clen_later = mixed_term(order_index) + 2.0 * operator_on(current) - clen_later, current
    input_grad = mixed_term(0) + operator_on(current) - clen_later
    weight_grad = jnp.stack(grad_terms) * (float(NODES) ** -0.5)
    return input_grad, weight_grad
```

```python
import functools

import jax
import jax.numpy as jnp
from jax import lax
from jax.experimental import pallas as pl
from jax.experimental.pallas import tpu as pltpu
from jax.sharding import PartitionSpec as P

F32, BF16 = jnp.float32, jnp.bfloat16
SLOTS = 4
WIDE = 256
MIB = 1 << 20


def dot(a, b, contract=(1, 0)):
    return lax.dot_general(
        a, b, (((contract[0],), (contract[1],)), ((), ())), preferred_element_type=F32
    )


def halves(x):
    high = x.astype(BF16)
    return high, (x - high.astype(F32)).astype(BF16)


def on_chip(x):
    return pltpu.with_memory_space_constraint(x, pltpu.VMEM)


def call(body, outs, ins, scratch=(), vmem=32, flops=0):
    specs, operands, moved = [], [], 0
    for x, place in ins:
        if place == "vmem":
            x = on_chip(x)
        spaces = {"smem": pltpu.SMEM, "any": pl.ANY}
        specs.append(pl.BlockSpec(memory_space=spaces.get(place, pltpu.VMEM)))
        operands.append(x)
    shapes = [
        pltpu.VMEM(shape, dtype) if kept else jax.ShapeDtypeStruct(shape, dtype)
        for shape, dtype, kept in outs
    ]
    return pl.pallas_call(
        body,
        out_shape=shapes,
        in_specs=specs,
        out_specs=[pl.BlockSpec(memory_space=pltpu.VMEM)] * len(outs),
        scratch_shapes=list(scratch),
        compiler_params=pltpu.CompilerParams(vmem_limit_bytes=vmem * MIB),
        cost_estimate=pl.CostEstimate(flops=flops, bytes_accessed=MIB, transcendentals=0),
    )(*operands)


def partners(size):
    pairs = [[], [], [], []]
    for p in range(size):
        odd, far = p % 2, (p // 2) % 2
        pairs[0].append((p, (p + 1) % size if odd else (p - 1) % size))
        pairs[1].append((p, (p - 1) % size if odd else (p + 1) % size))
        pairs[2].append((p, (p - 2) % size if far else (p + 2) % size))
        pairs[3].append((p, (p + 2) % size if far else (p - 2) % size))
    return pairs


def exchange(blocks):
    pairs = partners(lax.axis_size("dom"))
    return [lax.ppermute(block, "dom", route) for block, route in zip(blocks, pairs)]


def prepare(cols_ref, side_ref, lists_ref, tiles_ref, high_ref, low_ref, pick_ref, total, held, sems):
    count, tile, _ = held.shape
    nodes = pick_ref.shape[0]
    blocks = nodes // tile
    odd, far = side_ref[0], side_ref[1]
    per_row = count // blocks
    copies = [
        pltpu.make_async_copy(
            tiles_ref.at[pl.ds(r * per_row, per_row)], held.at[pl.ds(r * per_row, per_row)], sems.at[r]
        )
        for r in range(blocks)
    ]
    for copy in copies:
        copy.start()
    total[...] = jnp.zeros_like(total)
    lists = lists_ref[...]
    rows = lax.broadcasted_iota(jnp.int32, (nodes, tile), 0)
    near = [lists[0:1], lists[1:2]]
    away = [lists[2:3], lists[3:4]]
    order = [
        jnp.where(odd == 1, near[0], near[1]),
        jnp.where(odd == 1, near[1], near[0]),
        jnp.where(far == 1, away[1], away[0]),
        jnp.where(far == 1, away[0], away[1]),
    ]
    for k, wanted in enumerate(order):
        hit = rows == jnp.broadcast_to(wanted, rows.shape)
        pick_ref[:, k * tile : (k + 1) * tile] = hit.astype(F32).astype(BF16)
    for r, copy in enumerate(copies):
        copy.wait()
        here = slice(r * tile, (r + 1) * tile)
        for j in range(per_row):
            col = cols_ref[r * per_row + j]
            slot = col - blocks
            place = jnp.where(slot < 2, slot ^ odd, slot ^ (1 - far))
            col = jnp.where(slot >= 0, blocks + place, col)
            at = pl.ds(pl.multiple_of(col * tile, tile), tile)
            total[at, here] += held[r * per_row + j]
        high, low = halves(total[:, here])
        high_ref[:, here] = high
        low_ref[:, here] = low


def send_out(state, pick_ref, sends):
    rows = state.shape[0] // 2
    both = dot(state, pick_ref[...])
    picked = both[:rows] + both[rows:]
    width = sends[0].shape[1]
    for k, ref in enumerate(sends):
        ref[...] = picked[:, k * width : (k + 1) * width]


def begin(weight_ref, gathered_ref, own_ref, pick_ref, state_ref, halves_ref, *sends):
    local = own_ref.shape[0]
    first = dot(weight_ref[...], gathered_ref[...])
    own = own_ref[...].astype(F32)
    state = jnp.concatenate([first, own], axis=0)
    state_ref[...] = state
    high, low = halves(state)
    halves_ref[: 2 * local] = high
    halves_ref[2 * local :] = low
    send_out(halves_ref[...], pick_ref, sends)


def inner(scales, both_ref, before_ref, weight_ref, gathered_ref, feat_ref, high_ref, low_ref, out_ref, grad_ref):
    rows, nodes = before_ref.shape
    local = rows // 2
    for start in range(0, nodes, WIDE):
        here = slice(start, start + WIDE)
        both = dot(both_ref[...], high_ref[:nodes, here])
        total = both[:rows] + both[rows:] + dot(both_ref[:rows], low_ref[:nodes, here])
        before = before_ref[:, here]
        mixed = dot(weight_ref[...], gathered_ref[:, here])
        out_ref[:local, here] = scales[0] * total[:local] - before[:local] + mixed
        out_ref[local:, here] = scales[1] * total[local:] - before[local:]
    grad_ref[...] = dot(both_ref[local:rows], feat_ref[...], (1, 1)) + dot(
        both_ref[rows + local :], feat_ref[...], (1, 1)
    )


def outer(scales, part_ref, high_ref, low_ref, pick_ref, *refs):
    halos, (state_ref, halves_ref, *sends) = refs[:SLOTS], refs[SLOTS:]
    rows, nodes = part_ref.shape
    local = rows // 2
    high, low = halves(jnp.concatenate([ref[...] for ref in halos], axis=1))
    lhs = jnp.concatenate([high, low], axis=0)
    for start in range(0, nodes, WIDE):
        here = slice(start, start + WIDE)
        both = dot(lhs, high_ref[nodes:, here])
        total = both[:rows] + both[rows:] + dot(high, low_ref[nodes:, here])
        for chain in range(2):
            mine = slice(chain * local, (chain + 1) * local)
            state = part_ref[mine, here] + scales[chain] * total[mine]
            state_ref[mine, here] = state
            new_high, new_low = halves(state)
            halves_ref[mine, here] = new_high
            halves_ref[rows + chain * local : rows + (chain + 1) * local, here] = new_low
    send_out(halves_ref[...], pick_ref, sends)


def last(scales, part_ref, high_ref, low_ref, feat_ref, *refs):
    halos, (result_ref, grad_ref) = refs[:SLOTS], refs[SLOTS:]
    rows, nodes = part_ref.shape
    local = rows // 2
    high, low = halves(jnp.concatenate([ref[...] for ref in halos], axis=1))
    lhs = jnp.concatenate([high, low], axis=0)
    grad = jnp.zeros(grad_ref.shape, F32)
    for start in range(0, nodes, WIDE):
        here = slice(start, start + WIDE)
        both = dot(lhs, high_ref[nodes:, here])
        total = both[:rows] + both[rows:] + dot(high, low_ref[nodes:, here])
        result_ref[:, here] = part_ref[:local, here] + scales[0] * total[:local]
        state = part_ref[local:, here] + scales[1] * total[local:]
        new_high, new_low = halves(state)
        feat = feat_ref[:, here]
        grad += dot(new_high, feat, (1, 1)) + dot(new_low, feat, (1, 1))
    grad_ref[...] = grad


def local(features, cotangent, weights, tile_values, tile_cols, send_list):
    top = weights.shape[0] - 1
    channels, nodes = features.shape
    tile = tile_values.shape[-1]
    count = tile_values.shape[0]
    rows = 2 * channels
    wide = nodes + SLOTS * tile
    place = lax.axis_index("dom")
    side = jnp.stack([place % 2, (place // 2) % 2]).astype(jnp.int32)

    gathered = lax.all_gather(cotangent, "chan", axis=0, tiled=True)
    feat_all = lax.all_gather(features, "chan", axis=0, tiled=True)
    every = gathered.shape[0]

    high, low, pick = call(
        prepare,
        [((wide, nodes), BF16, True), ((wide, nodes), BF16, True), ((nodes, SLOTS * tile), BF16, True)],
        [(tile_cols.reshape(-1), "smem"), (side, "smem"), (send_list[0], ""), (tile_values, "any")],
        [
            pltpu.VMEM((wide, nodes), F32),
            pltpu.VMEM((count, tile, tile), F32),
            pltpu.SemaphoreType.DMA((nodes // tile,)),
        ],
    )
    state_outs = [((rows, nodes), F32, True), ((2 * rows, nodes), BF16, True)]
    sent = [((rows, tile), F32, False)] * SLOTS
    state, both, *sends = call(
        begin,
        state_outs + sent,
        [(weights[top], ""), (gathered, "vmem"), (cotangent, ""), (pick, "vmem")],
    )
    before = jnp.zeros((rows, nodes), F32)
    grads = []
    for step in range(1, top + 1):
        halos = exchange(sends)
        scales = (1.0 if step == top else 2.0, 1.0 if step == 1 else 2.0)
        part, grad = call(
            functools.partial(inner, scales),
            [((rows, nodes), F32, True), ((channels, every), F32, True)],
            [
                (both, "vmem"),
                (before, "vmem"),
                (weights[top - step], ""),
                (gathered, "vmem"),
                (feat_all, "vmem"),
                (high, "vmem"),
                (low, "vmem"),
            ],
            flops=2 * rows * nodes * nodes * 3,
        )
        grads.append(grad)
        operands = [(part, "vmem"), (high, "vmem"), (low, "vmem")]
        received = [(halo, "") for halo in halos]
        if step < top:
            before = state
            state, both, *sends = call(
                functools.partial(outer, scales), state_outs + sent, operands + [(pick, "vmem")] + received
            )
        else:
            input_grad, grad = call(
                functools.partial(last, scales),
                [((channels, nodes), F32, False), ((channels, every), F32, True)],
                operands + [(feat_all, "vmem")] + received,
            )
            grads.append(grad)
    summed = lax.psum(jnp.stack(grads), "dom")
    total_nodes = lax.axis_size("dom") * nodes
    return input_grad, jnp.swapaxes(summed, 1, 2) * float(total_nodes) ** (-0.5)


def solution(mesh):
    placed = (
        P("chan", "dom"),
        P("chan", "dom"),
        P(None, "chan", None),
        P("dom", None, None),
        P("dom", None, None),
        P("dom", None, None),
    )
    return jax.shard_map(
        local,
        mesh=mesh,
        in_specs=placed,
        out_specs=(P("chan", "dom"), P(None, None, "chan")),
        check_vma=False,
    )
```

```python
import types

import jax
import jax.numpy as jnp
from jax import lax
from jax.experimental import pallas as pl
from jax.experimental.pallas import tpu as pltpu
from jax.sharding import PartitionSpec as P

F32, BF16 = jnp.float32, jnp.bfloat16
SLOTS = 4
WIDE = 256
MIB = 1 << 20
RING = 8
KINDS = (2, 0, 3, 1)


def dot(a, b, contract=(1, 0)):
    return lax.dot_general(
        a, b, (((contract[0],), (contract[1],)), ((), ())), preferred_element_type=F32
    )


def halves(x):
    high = x.astype(BF16)
    return high, (x - high.astype(F32)).astype(BF16)


def call(body, ins, outs, scratch=(), flops=0):
    specs, operands = [], []
    for value in ins.values():
        x, place = value if isinstance(value, tuple) else (value, "vmem")
        if place == "vmem":
            x = pltpu.with_memory_space_constraint(x, pltpu.VMEM)
        specs.append(pl.BlockSpec(memory_space={"smem": pltpu.SMEM, "any": pl.ANY}.get(place, pltpu.VMEM)))
        operands.append(x)
    shapes = [
        pltpu.VMEM(shape, dtype) if kept else jax.ShapeDtypeStruct(shape, dtype)
        for shape, dtype, kept in outs.values()
    ]

    def kernel(*refs):
        n, m = len(ins), len(outs)
        i = types.SimpleNamespace(**dict(zip(ins, refs[:n])))
        o = types.SimpleNamespace(**dict(zip(outs, refs[n : n + m])))
        body(i, o, *refs[n + m :])

    got = pl.pallas_call(
        kernel,
        out_shape=shapes,
        in_specs=specs,
        out_specs=[pl.BlockSpec(memory_space=pltpu.VMEM)] * len(outs),
        scratch_shapes=list(scratch),
        compiler_params=pltpu.CompilerParams(vmem_limit_bytes=32 * MIB),
        cost_estimate=pl.CostEstimate(flops=flops, bytes_accessed=MIB, transcendentals=0),
    )(*operands)
    return dict(zip(outs, got))


def exchange(blocks):
    size = lax.axis_size("dom")
    pairs = [[], [], [], []]
    for p in range(size):
        odd, far = p % 2, (p // 2) % 2
        pairs[0].append((p, (p + 1) % size if odd else (p - 1) % size))
        pairs[1].append((p, (p - 1) % size if odd else (p + 1) % size))
        pairs[2].append((p, (p - 2) % size if far else (p + 2) % size))
        pairs[3].append((p, (p + 2) % size if far else (p - 2) % size))
    return [lax.ppermute(block, "dom", pairs[kind]) for block, kind in zip(blocks, KINDS)]


def dealt(side, forth1, back1, forth2, back2):
    odd, far = side[0] == 1, side[1] == 1
    kinds = [
        lambda: jnp.where(odd, forth1, back1),
        lambda: jnp.where(odd, back1, forth1),
        lambda: jnp.where(far, back2, forth2),
        lambda: jnp.where(far, forth2, back2),
    ]
    return [None if kind < 2 and forth1 is None else kinds[kind]() for kind in KINDS]


def undealt(side, got):
    odd, far = side[0] == 1, side[1] == 1
    k = [got[KINDS.index(kind)] for kind in range(SLOTS)]
    near = (None, None)
    if k[0] is not None:
        near = (jnp.where(odd, k[1], k[0]), jnp.where(odd, k[0], k[1]))
    return *near, jnp.where(far, k[2], k[3]), jnp.where(far, k[3], k[2])


def gather(x):
    size = lax.axis_size("chan")
    bit, blocks = size // 2, [x]
    while bit:
        blocks = blocks + [
            lax.ppermute(block, "chan", [(c, c ^ bit) for c in range(size)]) for block in blocks
        ]
        bit //= 2
    return blocks


def collect(place, blocks, out, base=0):
    masks, bit = [0], len(blocks) // 2
    while bit:
        masks = masks + [m ^ bit for m in masks]
        bit //= 2
    for mask, block in zip(masks, blocks):
        rows = block.shape[0]
        out[pl.ds(pl.multiple_of((place ^ mask) * rows, rows), rows), :] = block


def prepare(i, o, total, held, sems):
    count, tile, _ = held.shape
    nodes = o.pick.shape[0]
    blocks = nodes // tile
    odd, far = i.side[0], i.side[1]
    per_row = count // blocks
    copies = [
        pltpu.make_async_copy(
            i.tiles.at[pl.ds(r * per_row, per_row)], held.at[pl.ds(r * per_row, per_row)], sems.at[r]
        )
        for r in range(blocks)
    ]
    for copy in copies:
        copy.start()
    total[...] = jnp.zeros_like(total)
    rows = lax.broadcasted_iota(jnp.int32, (nodes, tile), 0)
    lists = i.lists[...]
    order = dealt(i.side, lists[0:1], lists[1:2], lists[2:3], lists[3:4])
    for k, wanted in enumerate(order):
        hit = rows == jnp.broadcast_to(wanted, rows.shape)
        o.pick[:, k * tile : (k + 1) * tile] = hit.astype(F32).astype(BF16)
    for r, copy in enumerate(copies):
        copy.wait()
        here = slice(r * tile, (r + 1) * tile)
        for j in range(per_row):
            col = i.cols[r * per_row + j]
            slot = col - blocks
            kind = jnp.where(slot < 2, slot ^ odd, slot ^ (1 - far))
            place = sum(jnp.where(kind == k, KINDS.index(k), 0) for k in range(SLOTS))
            col = jnp.where(slot >= 0, blocks + place, col)
            at = pl.ds(pl.multiple_of(col * tile, tile), tile)
            total[at, here] += held[r * per_row + j]
        high, low = halves(total[:, here])
        o.high[:, here] = high
        o.low[:, here] = low


def summed(both):
    rows = both.shape[0] // 2
    return both[:rows] + both[rows:]


def write_sends(sends, parts, extra=()):
    for k, ref in enumerate(sends):
        at, width = 0, ref.shape[1]
        for part in parts:
            ref[at : at + part.shape[0], :] = part[:, k * width : (k + 1) * width]
            at += part.shape[0]
        for blocks in extra:
            if blocks[k] is not None:
                ref[at : at + blocks[k].shape[0], :] = blocks[k]
                at += blocks[k].shape[0]


def back_halo(both, i, nodes):
    rows = both.shape[0] // 2
    return summed(dot(both, i.high[nodes:, :], (1, 1))) + dot(both[:rows], i.low[nodes:, :], (1, 1))


def correlate(u_high, u_low, g_high, g_low=None):
    total = dot(u_high, g_high, (1, 1))
    if u_low is not None:
        total += dot(u_low, g_high, (1, 1))
    if g_low is not None:
        total += dot(u_high, g_low, (1, 1))
    half = total.shape[1] // 2
    return jnp.concatenate([total[:, :half], total[:, half:]], axis=0)


def sends_of(o):
    return [getattr(o, f"send{k}") for k in range(SLOTS)]


def begin(i, o):
    local, nodes = i.own.shape
    blocks = [getattr(i, f"block{k}")[...] for k in range(len(vars(i)) - 7)]
    collect(i.side[3], [i.own[...]] + blocks, o.gathered)
    first = dot(i.weight[...], o.gathered[...])
    own = i.own[...].astype(F32)
    o.state[:local] = first
    o.state[local:] = own
    high, low = halves(first)
    o.both[:local] = high
    o.both[local : 2 * local] = i.own[...]
    o.both[2 * local : 3 * local] = low
    o.both[3 * local :] = jnp.zeros_like(low)
    feat = i.feat[...]
    back = dot(feat, i.high[nodes:, :], (1, 1)) + dot(feat, i.low[nodes:, :], (1, 1))
    write_sends(sends_of(o), [summed(dot(o.both[...], i.pick[...])), back])


def make_inner(step, top, chains):
    def inner(i, o):
        rows, nodes = o.part.shape
        local = rows // chains
        scale = 1.0 if step == top else 2.0
        width = i.both.shape[0] // 2
        lhs = jnp.concatenate([i.both[:rows], i.both[width : width + rows]], axis=0)
        for start in range(0, nodes, WIDE):
            here = slice(start, start + WIDE)
            total = summed(dot(lhs, i.high[:nodes, here])) + dot(lhs[:rows], i.low[:nodes, here])
            mixed = dot(i.weight[...], i.gathered[:, here])
            value = scale * total[:local] + mixed
            if step > 1:
                value -= i.before[:local, here]
            o.part[:local, here] = value
            if chains > 1:
                value = (1.0 if step == 1 else 2.0) * total[local:]
                if step > 1:
                    value -= i.before[local:, here]
                o.part[local:, here] = value
        if step == 1:
            feat = i.feat[...]
            for start in range(0, nodes, WIDE):
                here = slice(start, start + WIDE)
                o.fpart[:, here] = dot(feat, i.high[here, :], (1, 1)) + dot(feat, i.low[here, :], (1, 1))
        if step == 2:
            for start in range(0, nodes, WIDE):
                here = slice(start, start + WIDE)
                total = summed(dot(i.fboth[...], i.high[here, :], (1, 1)))
                total += dot(i.fboth[:local], i.low[here, :], (1, 1))
                o.fpart[:, here] = 2.0 * total - i.feat[:, here].astype(F32)

    return inner


def halo_product(i, lhs, rows, here, nodes):
    return summed(dot(lhs, i.high[nodes:, here])) + dot(lhs[:rows], i.low[nodes:, here])


def split_halos(i, rows):
    got = [getattr(i, f"halo{k}") for k in range(SLOTS)]
    high, low = halves(jnp.concatenate([ref[:rows, :] for ref in got], axis=1))
    return jnp.concatenate([high, low], axis=0)


def payload(i, at, rows, near=True):
    return undealt(
        i.side,
        [
            getattr(i, f"halo{k}")[at : at + rows, :] if near or kind >= 2 else None
            for k, kind in enumerate(KINDS)
        ],
    )


def make_outer(step, chains, following, ring):
    def outer(i, o):
        rows, nodes = i.part.shape
        local = rows // chains
        lhs = split_halos(i, rows)
        for start in range(0, nodes, WIDE):
            here = slice(start, start + WIDE)
            total = halo_product(i, lhs, rows, here, nodes)
            for chain in range(chains):
                mine = slice(chain * local, (chain + 1) * local)
                state = i.part[mine, here] + (1.0 if chain == 1 and step == 1 else 2.0) * total[mine]
                o.state[mine, here] = state
                high, low = halves(state)
                o.both[mine, here] = high
                o.both[rows + chain * local : rows + (chain + 1) * local, here] = low
        live = following * local
        moving = o.both[...]
        if following < chains:
            moving = jnp.concatenate([o.both[:live], o.both[rows : rows + live]], axis=0)
        parts, extra = [summed(dot(moving, i.pick[...]))], []
        if step <= 2:
            got = [getattr(i, f"halo{k}")[rows : rows + local, :] for k in range(SLOTS)]
            high, low = halves(jnp.concatenate(got, axis=1))
            lhs = jnp.concatenate([high, low], axis=0)
            for start in range(0, nodes, WIDE):
                here = slice(start, start + WIDE)
                total = summed(dot(lhs, i.pick[here, :], (1, 1)))
                high, low = halves(i.fpart[:, here] + (1.0 if step == 1 else 2.0) * total)
                o.fboth[:local, here] = high
                o.fboth[local:, here] = low
            if step == 1:
                parts.append(back_halo(o.fboth[...], i, nodes))
        if ring:
            unit = i.side[2]
            size = o.send0.shape[1]
            half = size // 2

            def at(offset):
                return (unit + offset + RING) % RING

            def newest(old):
                return 2.0 * correlate(
                    o.both[local : 2 * local], o.both[rows + local :], i.g_high[...], i.g_low[...]
                ) - old

            if step == 4:
                o.stack[0:4] = i.early[0:4]
                o.stack[4] = correlate(o.both[local : 2 * local], o.both[rows + local :], i.feat_all[...])
                o.stack[5] = i.early[4]
                o.stack[6] = newest(i.early[2])
                o.stack[7] = jnp.zeros_like(o.stack[7])
                forth = jnp.concatenate([o.stack[at(3)], o.stack[at(4), :half]], axis=0)
                back = jnp.concatenate([o.stack[at(-3)], o.stack[at(4), half:]], axis=0)
                extra.append(dealt(i.side, None, None, forth, back))
            if step == 5:
                _, _, m2, p2 = payload(i, rows, size + half, near=False)
                o.seven[...] = newest(i.stack[3])
                to_forth = i.stack[at(2)]
                to_back = i.stack[at(-2)]
                extra.append(
                    dealt(
                        i.side,
                        i.stack[at(1)] + m2[:size],
                        i.stack[at(-1)] + p2[:size],
                        jnp.concatenate([to_forth[:half] + m2[size:], to_forth[half:]], axis=0),
                        jnp.concatenate([to_back[:half], to_back[half:] + p2[size:]], axis=0),
                    )
                )
                extra.append([o.seven[...]] * SLOTS)
            if step == 6:
                m1, p1, m2, p2 = payload(i, rows, size)
                o.done[...] = i.stack[at(0)] + m1 + p1 + m2 + p2
                extra.append([o.done[...]] * SLOTS)
                m1, p1, m2, p2 = payload(i, rows + size, size)
                o.seven[...] = i.seven[...] + m1 + p1 + m2 + p2
                o.eight[...] = newest(i.stack[4])
                extra.append([o.eight[...]] * SLOTS)
                extra.append(dealt(i.side, None, None, m1, p1 + p2))
            if step == 7:
                m1, p1, m2, p2 = payload(i, rows, size)
                o.found[0] = i.done[...]
                for slot, value in enumerate((m1, p1, m2, p2)):
                    o.found[1 + slot] = value
                extra.append(dealt(i.side, m2, p2, m2[:half], p2[half:]))
                m1, p1, m2, p2 = payload(i, rows + size, size)
                o.eight[...] = i.eight[...] + m1 + p1 + m2 + p2
                extra.append(dealt(i.side, None, None, m1, p1 + p2))
                _, _, m2, p2 = payload(i, rows + 2 * size, size, near=False)
                o.seven[...] = i.seven[...] + m2 + p2
        write_sends(sends_of(o), parts, extra)

    return outer


def early(i, o):
    local = i.both1.shape[0] // 4
    o.early[0] = correlate(i.own[...], None, i.feat_all[...])
    for k in range(1, 4):
        ref = getattr(i, f"both{k}")
        o.early[k] = correlate(ref[local : 2 * local], ref[3 * local :], i.feat_all[...])
    o.early[4] = 2.0 * correlate(
        i.both3[local : 2 * local], i.both3[3 * local :], i.g_high[...], i.g_low[...]
    ) - o.early[1]


def make_last(scale):
    def last(i, o):
        rows, nodes = i.part.shape
        lhs = split_halos(i, rows)
        for start in range(0, nodes, WIDE):
            here = slice(start, start + WIDE)
            o.result[:, here] = i.part[:, here] + halo_product(i, lhs, rows, here, nodes)
        if not hasattr(i, "found"):
            return
        size = i.halo0.shape[1]
        half = size // 2

        def put(k, chunk):
            for h in range(2):
                o.grads[k, h * size : (h + 1) * size, :] = scale * chunk[h * half : (h + 1) * half].T

        unit = i.side[2]
        for slot, offset in enumerate((0, -1, 1, -2, 2)):
            where = (unit + offset + RING) % RING

            @pl.when(where < 7)
            def _():
                put(where, i.found[slot])

        m1, p1, _, _ = payload(i, rows, size)
        from_two = []
        for k, kind in enumerate(KINDS):
            ref = getattr(i, f"halo{k}")
            start = rows + (size if kind < 2 else 0)
            from_two.append(None if kind < 2 else ref[rows : rows + half, :])
        _, _, m2, p2 = undealt(i.side, from_two)
        for offset, chunk in ((-3, m1), (3, p1), (4, jnp.concatenate([m2, p2], axis=0))):
            where = (unit + offset + RING) % RING

            @pl.when(where < 7)
            def _():
                put(where, chunk)

        _, _, m2, p2 = payload(i, rows + half, size, near=False)
        put(7, i.seven[...])
        put(8, i.eight[...] + m2 + p2)

    return last


def after(x, marker):
    return lax.optimization_barrier((x, marker))


def local(features, cotangent, weights, tile_values, tile_cols, send_list):
    top = weights.shape[0] - 1
    channels, nodes = features.shape
    count, tile = tile_values.shape[0], tile_values.shape[-1]
    every = weights.shape[2]
    wide = nodes + SLOTS * tile
    parts = lax.axis_size("dom")
    ring = parts == RING and top == RING and channels * every == tile * tile
    place = lax.axis_index("dom")
    side = jnp.stack([place % 2, (place // 2) % 2, place, lax.axis_index("chan")]).astype(jnp.int32)
    side = (side, "smem")
    scale = float(parts * nodes) ** (-0.5)

    blocks = gather(cotangent)
    ready = call(
        prepare,
        dict(
            cols=(tile_cols.reshape(-1), "smem"), side=side, lists=(send_list[0], ""), tiles=(tile_values, "any")
        ),
        dict(
            high=((wide, nodes), BF16, True),
            low=((wide, nodes), BF16, True),
            pick=((nodes, SLOTS * tile), BF16, True),
        ),
        [
            pltpu.VMEM((wide, nodes), F32),
            pltpu.VMEM((count, tile, tile), F32),
            pltpu.SemaphoreType.DMA((nodes // tile,)),
        ],
    )
    matrix = dict(high=ready["high"], low=ready["low"])
    pick = dict(pick=ready["pick"])

    def messages(rows, extra=(0, 0)):
        return {
            f"send{k}": ((rows + extra[0 if kind < 2 else 1], tile), F32, False)
            for k, kind in enumerate(KINDS)
        }

    def state_outs(chains):
        rows = chains * channels
        return dict(state=((rows, nodes), F32, True), both=((2 * rows, nodes), BF16, True))

    got = call(
        begin,
        dict(
            side=side,
            own=(cotangent, ""),
            feat=(features, ""),
            weight=(weights[top], ""),
            **matrix,
            **pick,
            **{f"block{k}": (block, "") for k, block in enumerate(blocks[1:])},
        ),
        dict(gathered=((every, nodes), BF16, True), **state_outs(2), **messages(3 * channels)),
    )
    gathered = got["gathered"]
    chunk = ((tile, tile), F32, True)
    extras = {4: (0, tile + tile // 2), 5: (2 * tile, 2 * tile), 6: (2 * tile, 3 * tile), 7: (tile, tile // 2 + tile)}
    kept, before, boths = {}, None, {}
    result = None
    for step in range(1, top + 1):
        chains = 2 if step <= top - 2 else 1
        following = 2 if step + 1 <= top - 2 else 1
        halos = {f"halo{k}": (x, "") for k, x in enumerate(exchange([got[f"send{k}"] for k in range(SLOTS)]))}
        ins = dict(both=got["both"], weight=(weights[top - step], ""), gathered=gathered, **matrix)
        outs = dict(part=((chains * channels, nodes), F32, True))
        if step > 1:
            ins["before"] = before
        if step <= 2:
            ins["feat"] = (features, "")
            outs["fpart"] = ((channels, nodes), F32, True)
        if step == 2:
            ins["fboth"] = got["fboth"]
        inside = call(
            make_inner(step, top, chains), ins, outs, flops=2 * chains * channels * nodes * nodes * 3
        )
        part = inside["part"]
        if step == 1:
            feat, part = after(features, part)
            feat_blocks = gather(feat)
        if step == 3:
            back, part = after(got["fboth"], part)
            back_blocks = gather(back)
        if step == 4:

            def settle(i, o):
                n = len(feat_blocks)
                collect(i.side[3], [getattr(i, f"f{k}")[...] for k in range(n)], o.feat_all)
                rows = channels
                back = [getattr(i, f"b{k}") for k in range(n)]
                collect(i.side[3], [ref[:rows] for ref in back], o.g_high)
                collect(i.side[3], [ref[rows:] for ref in back], o.g_low)

            whole = ((every, nodes), BF16, True)
            kept = call(
                settle,
                dict(
                    side=side,
                    **{f"f{k}": (x, "") for k, x in enumerate(feat_blocks)},
                    **{f"b{k}": (x, "") for k, x in enumerate(back_blocks)},
                ),
                dict(feat_all=whole, g_high=whole, g_low=whole),
            )
            first = call(
                early,
                dict(own=(cotangent, ""), **kept, **{f"both{k}": boths[k] for k in (1, 2, 3)}),
                dict(early=((5, tile, tile), F32, True)),
            )
        if step == top:
            ins = dict(part=part, side=side, **matrix, **halos)
            outs = dict(result=((channels, nodes), F32, False))
            if ring:
                ins.update(found=got["found"], seven=got["seven"], eight=got["eight"])
                outs["grads"] = ((top + 1, every, channels), F32, False)
            final = call(make_last(scale), ins, outs)
            result = final["result"]
            break
        ins = dict(part=part, side=side, **matrix, **pick, **halos)
        outs = state_outs(chains)
        if step <= 2:
            ins["fpart"] = inside["fpart"]
            outs["fboth"] = ((2 * channels, nodes), BF16, True)
        extra = (0, 0)
        if ring and step >= 4:
            extra = extras[step]
            if step <= 6:
                ins.update(g_high=kept["g_high"], g_low=kept["g_low"])
            if step == 4:
                ins.update(feat_all=kept["feat_all"], early=first["early"])
                outs["stack"] = ((RING, tile, tile), F32, True)
            if step in (5, 6):
                ins["stack"] = stack
            if step >= 5:
                outs["seven"] = chunk
            if step >= 6:
                ins["seven"] = got["seven"]
                outs["eight"] = chunk
            if step == 6:
                outs["done"] = chunk
            if step == 7:
                ins.update(done=got["done"], eight=got["eight"])
                outs["found"] = ((5, tile, tile), F32, True)
        sent = following + (1 if step == 1 else 0)
        outs.update(messages(sent * channels, extra))
        before = got["state"]
        got = call(make_outer(step, chains, following, ring and step >= 4), ins, outs)
        boths[step] = got["both"]
        if step == 4 and ring:
            stack = got["stack"]
    if ring:
        return result, final["grads"]

    def rest(i, o):
        o.out[0:4] = i.early[0:4]
        o.out[5] = i.early[4]
        for k in (4, 5, 6):
            ref = getattr(i, f"both{k}")
            high, low = ref[channels : 2 * channels], ref[3 * channels :]
            if k == 4:
                o.out[4] = correlate(high, low, i.feat_all[...])
            o.out[k + 2] = 2.0 * correlate(high, low, i.g_high[...], i.g_low[...]) - o.out[k - 2]

    grads = call(
        rest,
        dict(early=first["early"], **kept, **{f"both{k}": boths[k] for k in (4, 5, 6)}),
        dict(out=((top + 1, 2 * channels, every // 2), F32, True)),
    )["out"]
    grads = lax.psum(grads, "dom").reshape(top + 1, 2, channels, every // 2)
    return result, grads.transpose(0, 1, 3, 2).reshape(top + 1, every, channels) * scale


def solution(mesh):
    placed = (
        P("chan", "dom"),
        P("chan", "dom"),
        P(None, "chan", None),
        P("dom", None, None),
        P("dom", None, None),
        P("dom", None, None),
    )
    return jax.shard_map(
        local,
        mesh=mesh,
        in_specs=placed,
        out_specs=(P("chan", "dom"), P(None, None, "chan")),
        check_vma=False,
    )
```

```python
import types

import jax
import jax.numpy as jnp
from jax import lax
from jax.experimental import pallas as pl
from jax.experimental.pallas import tpu as pltpu
from jax.sharding import PartitionSpec as P

F32, BF16 = jnp.float32, jnp.bfloat16
SLOTS = 4
WIDE = 256
MIB = 1 << 20
RING = 8
KINDS = (2, 0, 3, 1)


def dot(a, b, contract=(1, 0)):
    return lax.dot_general(
        a, b, (((contract[0],), (contract[1],)), ((), ())), preferred_element_type=F32
    )


def halves(x):
    high = x.astype(BF16)
    return high, (x - high.astype(F32)).astype(BF16)


def call(body, ins, outs, scratch=(), flops=0):
    specs, operands = [], []
    for value in ins.values():
        x, place = value if isinstance(value, tuple) else (value, "vmem")
        if place:
            x = pltpu.with_memory_space_constraint(x, pltpu.VMEM if place == "vmem" else pltpu.HBM)
        specs.append(pl.BlockSpec(memory_space={"smem": pltpu.SMEM, "hbm": pltpu.HBM}.get(place, pltpu.VMEM)))
        operands.append(x)
    shapes = [
        pltpu.VMEM(shape, dtype) if kept else jax.ShapeDtypeStruct(shape, dtype)
        for shape, dtype, kept in outs.values()
    ]

    def kernel(*refs):
        n, m = len(ins), len(outs)
        i = types.SimpleNamespace(**dict(zip(ins, refs[:n])))
        o = types.SimpleNamespace(**dict(zip(outs, refs[n : n + m])))
        body(i, o, *refs[n + m :])

    got = pl.pallas_call(
        kernel,
        out_shape=shapes,
        in_specs=specs,
        out_specs=[pl.BlockSpec(memory_space=pltpu.VMEM)] * len(outs),
        scratch_shapes=list(scratch),
        compiler_params=pltpu.CompilerParams(vmem_limit_bytes=32 * MIB),
        cost_estimate=pl.CostEstimate(flops=flops, bytes_accessed=MIB, transcendentals=0),
    )(*operands)
    return dict(zip(outs, got))


def exchange(blocks):
    size = lax.axis_size("dom")
    pairs = [[], [], [], []]
    for p in range(size):
        odd, far = p % 2, (p // 2) % 2
        pairs[0].append((p, (p + 1) % size if odd else (p - 1) % size))
        pairs[1].append((p, (p - 1) % size if odd else (p + 1) % size))
        pairs[2].append((p, (p - 2) % size if far else (p + 2) % size))
        pairs[3].append((p, (p + 2) % size if far else (p - 2) % size))
    return [lax.ppermute(block, "dom", pairs[kind]) for block, kind in zip(blocks, KINDS)]


def sides():
    me = lax.axis_index("dom")
    return lax.rem(me, 2), lax.rem(lax.div(me, 2), 2)


def pairs_of_two(forth, back):
    far = sides()[1] == 1
    return {2: jnp.where(far, back, forth), 3: jnp.where(far, forth, back)}


def from_pairs(got):
    odd, far = sides()
    odd, far = odd == 1, far == 1
    near = (None, None)
    if 0 in got:
        near = (jnp.where(odd, got[1], got[0]), jnp.where(odd, got[0], got[1]))
    return *near, jnp.where(far, got[2], got[3]), jnp.where(far, got[3], got[2])


LAYOUT = {
    4: {1: (256,)},
    5: {1: (192,), 2: (128,), 3: (128,)},
    6: {1: (128,), 2: (128, 96), 3: (128, 96)},
    7: {0: (128,), 1: (256, 128), 2: (96, 64, 128), 3: (96, 64, 128)},
    8: {1: (192,), 2: (64, 128), 3: (64, 128)},
}


def carried(i, step, base, kind, index):
    rows = LAYOUT[step][kind]
    start = base + sum(rows[:index])
    return getattr(i, f"halo{KINDS.index(kind)}")[start : start + rows[index], :]


def parted(group):
    odd = sides()[0] == 1
    half = group.shape[0] // 2
    return jnp.where(odd, group[half:], group[:half]), jnp.where(odd, group[:half], group[half:])


def joined(own, other):
    odd = sides()[0] == 1
    return jnp.concatenate([jnp.where(odd, other, own), jnp.where(odd, own, other)], axis=0)


def added(rows, first, second):
    half = rows.shape[0] // 2
    return jnp.concatenate([rows[:half] + first, rows[half:] + second], axis=0)


def gather(x, hold=lambda block: block):
    size = lax.axis_size("chan")
    bit, blocks = size // 2, [x]
    while bit:
        blocks = blocks + [
            lax.ppermute(block, "chan", [(c, c ^ bit) for c in range(size)]) for block in blocks
        ]
        if bit == size // 2:
            blocks[1] = hold(blocks[1])
        bit //= 2
    return blocks


def collect(blocks, out):
    masks, bit = [0], len(blocks) // 2
    while bit:
        masks = masks + [m ^ bit for m in masks]
        bit //= 2
    place = lax.axis_index("chan")
    for mask, block in zip(masks, blocks):
        rows = block.shape[0]
        out[pl.ds(pl.multiple_of((place ^ mask) * rows, rows), rows), :] = block


def stack(i, o, sems):
    local = i.upper.shape[0]
    copies = [
        pltpu.make_async_copy(i.upper, o.both.at[pl.ds(0, local)], sems.at[0]),
        pltpu.make_async_copy(i.lower, o.both.at[pl.ds(local, local)], sems.at[1]),
    ]
    for copy in copies:
        copy.start()
    for copy in copies:
        copy.wait()


def prepare(i, o, total, held, sems):
    count, tile, _ = held.shape
    nodes = o.pick.shape[0]
    blocks = nodes // tile
    per_row = count // blocks
    copies = [
        pltpu.make_async_copy(
            i.tiles.at[pl.ds(r * per_row, per_row)], held.at[pl.ds(r * per_row, per_row)], sems.at[r]
        )
        for r in range(blocks)
    ]
    for copy in copies:
        copy.start()
    odd, far = sides()
    rows = lax.broadcasted_iota(jnp.int32, (nodes, tile), 0)
    lists = i.lists[0]
    near = jnp.where(odd == 1, lists[0:1], lists[1:2]), jnp.where(odd == 1, lists[1:2], lists[0:1])
    order = [*near, *pairs_of_two(lists[2:3], lists[3:4]).values()]
    for k, kind in enumerate(KINDS):
        hit = rows == jnp.broadcast_to(order[kind], rows.shape)
        o.pick[:, k * tile : (k + 1) * tile] = hit.astype(F32).astype(BF16)
    total[...] = jnp.zeros_like(total)
    for r, copy in enumerate(copies):
        copy.wait()
        here = slice(r * tile, (r + 1) * tile)
        for j in range(per_row):
            col = i.cols[0, r, j]
            slot = col - blocks
            kind = jnp.where(slot < 2, slot ^ odd, slot ^ (1 - far))
            place = sum(jnp.where(kind == k, KINDS.index(k), 0) for k in range(SLOTS))
            col = jnp.where(slot >= 0, blocks + place, col)
            at = pl.ds(pl.multiple_of(col * tile, tile), tile)
            total[at, here] += held[r * per_row + j]
        high, low = halves(total[:, here])
        o.high[:, here] = high
        o.low[:, here] = low
    channels = i.stacked.shape[0] // 2
    feat = i.stacked[channels:]
    o.back[...] = dot(feat, o.high[nodes:, :], (1, 1)) + dot(feat, o.low[nodes:, :], (1, 1))
    o.sent[...] = dot(i.stacked[:channels], o.pick[...])


def summed(both):
    rows = both.shape[0] // 2
    return both[:rows] + both[rows:]


def write_sends(o, parts, extra=None):
    for k, kind in enumerate(KINDS):
        ref = getattr(o, f"send{k}")
        at, width = 0, ref.shape[1]
        for part in parts:
            ref[at : at + part.shape[0], :] = part[:, k * width : (k + 1) * width]
            at += part.shape[0]
        for block in (extra or {}).get(kind, ()):
            ref[at : at + block.shape[0], :] = block
            at += block.shape[0]


def back_halo(both, i, nodes):
    rows = both.shape[0] // 2
    return summed(dot(both, i.high[nodes:, :], (1, 1))) + dot(both[:rows], i.low[nodes:, :], (1, 1))


def correlate(u_high, u_low, g_high, g_low=None):
    if u_low is None:
        total = dot(u_high, g_high)
    else:
        total = summed(dot(jnp.concatenate([u_high, u_low], axis=0), g_high))
    if g_low is not None:
        total += dot(u_high, g_low)
    half = total.shape[1] // 2
    return jnp.concatenate([total[:, :half], total[:, half:]], axis=0)


def transposed(x):
    return x.astype(F32).T.astype(BF16)


def begin(i, o):
    local = i.weight.shape[0]
    own = i.stacked[:local]
    collect([own] + [ref[:local, :] for name, ref in vars(i).items() if name.startswith("block")], o.gathered)
    first = dot(i.weight[...], o.gathered[...])
    o.state[:local] = first
    o.state[local:] = own.astype(F32)
    high, low = halves(first)
    o.both[:local] = high
    o.both[local : 2 * local] = own
    o.both[2 * local : 3 * local] = low
    o.both[3 * local :] = jnp.zeros_like(low)
    parts = summed(dot(jnp.concatenate([high, low], axis=0), i.pick[...])), i.sent[...], i.back[...]
    write_sends(o, parts)


def make_inner(step, top, chains):
    def inner(i, o):
        rows, nodes = o.part.shape
        local = rows // chains
        scale = 1.0 if step == top else 2.0
        width = i.both.shape[0] // 2
        lhs = jnp.concatenate([i.both[:rows], i.both[width : width + rows]], axis=0)
        for start in range(0, nodes, WIDE):
            here = slice(start, start + WIDE)
            total = summed(dot(lhs, i.high[:nodes, here])) + dot(lhs[:rows], i.low[:nodes, here])
            mixed = dot(i.weight[...], i.gathered[:, here])
            value = scale * total[:local] + mixed
            if step > 1:
                value -= i.before[:local, here]
            o.part[:local, here] = value
            if chains > 1:
                value = (1.0 if step == 1 else 2.0) * total[local:]
                if step > 1:
                    value -= i.before[local:, here]
                o.part[local:, here] = value
        if step == 1:
            feat = i.stacked[local:]
            for start in range(0, nodes, WIDE):
                here = slice(start, start + WIDE)
                o.fpart[:, here] = dot(feat, i.high[here, :], (1, 1)) + dot(feat, i.low[here, :], (1, 1))
        if step == 2:
            for start in range(0, nodes, WIDE):
                here = slice(start, start + WIDE)
                total = summed(dot(i.fboth[...], i.high[here, :], (1, 1)))
                total += dot(i.fboth[:local], i.low[here, :], (1, 1))
                o.fpart[:, here] = 2.0 * total - i.stacked[local:, here].astype(F32)
        if step <= 3:
            u_low = None if step == 1 else i.both[width + local : width + 2 * local]
            o.grad[...] = correlate(i.both[local : 2 * local], u_low, i.feat_t[...])

    return inner


def halo_product(i, lhs, rows, here, nodes):
    return summed(dot(lhs, i.high[nodes:, here])) + dot(lhs[:rows], i.low[nodes:, here])


def split_halos(i, rows):
    got = [getattr(i, f"halo{k}") for k in range(SLOTS)]
    high, low = halves(jnp.concatenate([ref[:rows, :] for ref in got], axis=1))
    return jnp.concatenate([high, low], axis=0)


def make_outer(step, chains, following, ring):
    def outer(i, o):
        rows, nodes = i.part.shape
        local = rows // chains
        lhs = split_halos(i, rows)
        for start in range(0, nodes, WIDE):
            here = slice(start, start + WIDE)
            total = halo_product(i, lhs, rows, here, nodes)
            for chain in range(chains):
                mine = slice(chain * local, (chain + 1) * local)
                state = i.part[mine, here] + (1.0 if chain == 1 and step == 1 else 2.0) * total[mine]
                o.state[mine, here] = state
                high, low = halves(state)
                o.both[mine, here] = high
                o.both[rows + chain * local : rows + (chain + 1) * local, here] = low
        live = following * local
        moving = o.both[...]
        if following < chains:
            moving = jnp.concatenate([o.both[:live], o.both[rows : rows + live]], axis=0)
        parts, extra = [summed(dot(moving, i.pick[...]))], []
        if step <= 2:
            got = [getattr(i, f"halo{k}")[rows : rows + local, :] for k in range(SLOTS)]
            high, low = halves(jnp.concatenate(got, axis=1))
            lhs = jnp.concatenate([high, low], axis=0)
            for start in range(0, nodes, WIDE):
                here = slice(start, start + WIDE)
                total = summed(dot(lhs, i.pick[here, :], (1, 1)))
                high, low = halves(i.fpart[:, here] + (1.0 if step == 1 else 2.0) * total)
                o.fboth[:local, here] = high
                o.fboth[local:, here] = low
            if step == 1:
                parts.append(back_halo(o.fboth[...], i, nodes))
        extra = None
        if ring:
            if chains > 1:
                state = o.both[local : 2 * local], o.both[rows + local : rows + 2 * local]

            def got(kind, index):
                return carried(i, step, rows, kind, index)

            def newest(old):
                return 2.0 * correlate(*state, i.g_high[...], i.g_low[...]) - old

            if step == 3:
                o.third[...] = correlate(*state, i.feat_t[...])
                group = jnp.concatenate([i.grad0[...], i.grad1[...], i.grad2[...], o.third[...]], axis=0)
                o.one[...], away = parted(group)
                extra = {1: [away]}
            if step == 4:
                one = i.one[...] + got(1, 0)
                half = one.shape[0] // 2
                o.one[...] = one
                o.fourth[...] = correlate(*state, i.feat_t[...])
                group = jnp.concatenate([o.fourth[...], i.fifth[...], newest(i.grad2[...])], axis=0)
                o.two[...], away = parted(group)
                extra = {1: [away], 2: [one[:half]], 3: [one[half:]]}
            if step == 5:
                one = added(i.one[...], got(2, 0), got(3, 0))
                two = i.two[...] + got(1, 0)
                half, quarter = one.shape[0] // 2, two.shape[0] // 2
                o.one[...], o.two[...] = one, two
                o.seven[...] = newest(i.third[...])
                extra = {1: [o.seven[...]], 2: [one[half:], two[:quarter]], 3: [one[:half], two[quarter:]]}
            if step == 6:
                one = added(i.one[...], got(3, 0), got(2, 0))
                two = added(i.two[...], got(2, 1), got(3, 1))
                seven = i.seven[...] + got(1, 0)
                eight = newest(i.fourth[...])
                half, quarter = seven.shape[0] // 2, two.shape[0] // 2
                o.one[...], o.two[...], o.seven[...], o.eight[...] = one, two, seven, eight
                extra = {
                    0: [eight],
                    1: [one, eight],
                    2: [two[quarter:], seven[:half], eight],
                    3: [two[:quarter], seven[half:], eight],
                }
            if step == 7:
                o.one[...] = joined(i.one[...], got(1, 0))
                two = added(i.two[...], got(3, 0), got(2, 0))
                seven = added(i.seven[...], got(2, 1), got(3, 1))
                m1, p1, m2, p2 = from_pairs({0: got(0, 0), 1: got(1, 1), 2: got(2, 2), 3: got(3, 2)})
                half = seven.shape[0] // 2
                o.two[...], o.seven[...] = two, seven
                o.eight[...] = i.eight[...] + m1 + p1 + m2 + p2
                on = pairs_of_two(m1, p1 + p2)
                extra = {1: [two], 2: [seven[half:], on[2]], 3: [seven[:half], on[3]]}
        write_sends(o, parts, extra)

    return outer


def settle(i, o):
    blocks = [ref for name, ref in vars(i).items() if name.startswith("block")]
    rows = blocks[0].shape[0] // 2
    for half, out in ((slice(0, rows), o.g_high), (slice(rows, None), o.g_low)):
        collect([ref[half, :] for ref in blocks], o.whole)
        out[...] = transposed(o.whole[...])
    local = i.both.shape[0] // 4
    o.fifth[...] = 2.0 * correlate(
        i.both[local : 2 * local], i.both[3 * local :], o.g_high[...], o.g_low[...]
    ) - i.grad1[...]


def make_last(step, scale, ring):
    def last(i, o):
        rows, nodes = i.part.shape
        lhs = split_halos(i, rows)
        for start in range(0, nodes, WIDE):
            here = slice(start, start + WIDE)
            o.result[:, here] = i.part[:, here] + halo_product(i, lhs, rows, here, nodes)
        if not ring:
            return

        def got(kind, index):
            return carried(i, step, rows, kind, index)

        def put(k, chunk):
            size = chunk.shape[0] // 2
            o.grads[k] = scale * jnp.concatenate([chunk[:size], chunk[size:]], axis=1)

        size = i.eight.shape[0]
        one, two = i.one[...], joined(i.two[...], got(1, 0))
        for k in range(4):
            put(k, one[k * size : (k + 1) * size])
        for k in range(3):
            put(4 + k, two[k * size : (k + 1) * size])
        put(7, added(i.seven[...], got(3, 0), got(2, 0)))
        _, _, m2, p2 = from_pairs({2: got(2, 1), 3: got(3, 1)})
        put(8, i.eight[...] + m2 + p2)

    return last


def after(x, marker):
    return lax.optimization_barrier((x, marker))


def local(features, cotangent, weights, tile_values, tile_cols, send_list):
    top = weights.shape[0] - 1
    channels, nodes = features.shape
    tile = tile_values.shape[-1]
    every = weights.shape[2]
    wide = nodes + SLOTS * tile
    parts = lax.axis_size("dom")
    ring = parts == RING and top == RING and channels * every == tile * tile and tile == 128
    scale = float(parts * nodes) ** (-0.5)
    sent_shape = ((channels, SLOTS * tile), F32, True)
    whole = ((every, nodes), BF16, True)
    turned = ((nodes, every), BF16, True)
    chunk = ((2 * channels, every // 2), F32, True)

    stacked = call(
        stack,
        dict(upper=(cotangent, "hbm"), lower=(features, "hbm")),
        dict(both=((2 * channels, nodes), BF16, True)),
        [pltpu.SemaphoreType.DMA((2,))],
    )["both"]
    ready = call(
        prepare,
        dict(
            cols=(tile_cols, "smem"),
            lists=(send_list, "load"),
            tiles=(tile_values, "hbm"),
            stacked=stacked,
        ),
        dict(
            high=((wide, nodes), BF16, True),
            low=((wide, nodes), BF16, True),
            pick=((nodes, SLOTS * tile), BF16, True),
            back=sent_shape,
            sent=sent_shape,
        ),
        [
            pltpu.VMEM((wide, nodes), F32),
            pltpu.VMEM(tile_values.shape, F32),
            pltpu.SemaphoreType.DMA((nodes // tile,)),
        ],
        flops=10**10,
    )
    matrix = dict(high=ready["high"], low=ready["low"])
    pick = dict(pick=ready["pick"])
    blocks = gather(stacked, lambda block: after(block, ready["back"])[0])

    def messages(rows, step):
        extra = LAYOUT.get(step, {}) if ring else {}
        return {
            f"send{k}": ((rows + sum(extra.get(kind, ())), tile), F32, False) for k, kind in enumerate(KINDS)
        }

    def state_outs(chains):
        rows = chains * channels
        return dict(state=((rows, nodes), F32, True), both=((2 * rows, nodes), BF16, True))

    named = {f"block{k}": (block, "") for k, block in enumerate(blocks[1:])}
    got = call(
        begin,
        dict(
            stacked=stacked,
            weight=(weights[top], ""),
            **pick,
            sent=ready["sent"],
            back=ready["back"],
            **named,
        ),
        dict(gathered=whole, **state_outs(2), **messages(3 * channels, 1)),
    )
    gathered = got["gathered"]

    def turn(i, o):
        rows = [ref[channels:, :] for name, ref in vars(i).items() if name.startswith("block")]
        collect([i.stacked[channels:]] + rows, o.whole)
        o.feat_t[...] = transposed(o.whole[...])

    feat_t = call(turn, dict(stacked=stacked, **named), dict(whole=whole, feat_t=turned))["feat_t"]
    before, boths, grads, back = None, {}, {}, None
    for step in range(1, top + 1):
        chains = 2 if step <= top - 2 else 1
        following = 2 if step + 1 <= top - 2 else 1
        halos = {f"halo{k}": (x, "") for k, x in enumerate(exchange([got[f"send{k}"] for k in range(SLOTS)]))}
        ins = dict(both=got["both"], weight=(weights[top - step], ""), gathered=gathered, **matrix)
        outs = dict(part=((chains * channels, nodes), F32, True))
        if step > 1:
            ins["before"] = before
        if step <= 2:
            ins["stacked"] = stacked
            outs["fpart"] = ((channels, nodes), F32, True)
        if step == 2:
            ins["fboth"] = got["fboth"]
        if step <= 3:
            ins["feat_t"] = feat_t
            outs["grad"] = chunk
        inside = call(
            make_inner(step, top, chains), ins, outs, flops=2 * chains * channels * nodes * nodes * 3
        )
        part = inside["part"]
        if step <= 3:
            grads[step - 1] = inside["grad"]
        if step == 3:
            back_blocks = gather(got["fboth"])
        if step == 4:
            back = call(
                settle,
                dict(
                    **{f"block{k}": (x, "") for k, x in enumerate(back_blocks)}, both=boths[3], grad1=grads[1]
                ),
                dict(g_high=turned, g_low=turned, whole=whole, fifth=chunk),
            )
        ins = dict(part=part, **matrix, **halos)
        if step == top:
            outs = dict(result=((channels, nodes), F32, False))
            if ring:
                ins.update({k: got[k] for k in ("one", "two", "seven", "eight")})
                outs["grads"] = ((top + 1, channels, every), F32, False)
            got = call(make_last(step, scale, ring), ins, outs)
            break
        ins.update(pick)
        outs = state_outs(chains)
        if step <= 2:
            ins["fpart"] = inside["fpart"]
            outs["fboth"] = ((2 * channels, nodes), BF16, True)
        if ring and step >= 3:
            one = ((4 * channels, every // 2), F32, True)
            two = ((3 * channels, every // 2), F32, True)
            if step in (3, 4):
                ins["feat_t"] = feat_t
            if step in (4, 5, 6):
                ins.update(g_high=back["g_high"], g_low=back["g_low"])
            if step == 3:
                ins.update({f"grad{k}": grads[k] for k in range(3)})
                outs.update(one=one, third=chunk)
            if step == 4:
                grads[3] = got["third"]
                ins.update(one=got["one"], grad2=grads[2], fifth=back["fifth"])
                outs.update(one=one, two=two, fourth=chunk)
            if step == 5:
                grads[4] = got["fourth"]
                ins.update(one=got["one"], two=got["two"], third=grads[3])
                outs.update(one=one, two=two, seven=chunk)
            if step == 6:
                ins.update({k: got[k] for k in ("one", "two", "seven")}, fourth=grads[4])
                outs.update(one=one, two=two, seven=chunk, eight=chunk)
            if step == 7:
                ins.update({k: got[k] for k in ("one", "two", "seven", "eight")})
                outs.update(one=((8 * channels, every // 2), F32, True), two=two, seven=chunk, eight=chunk)
        sent = following + (1 if step == 1 else 0)
        outs.update(messages(sent * channels, step + 1))
        before = got["state"]
        got = call(make_outer(step, chains, following, ring and step >= 3), ins, outs)
        boths[step] = got["both"]
    if ring:
        return got["result"], jnp.swapaxes(got["grads"], 1, 2)

    def rest(i, o):
        for k in range(3):
            o.out[k] = getattr(i, f"grad{k}")[...]
        o.out[5] = i.fifth[...]
        for k in range(3, 7):
            ref = getattr(i, f"both{k}")
            state = ref[channels : 2 * channels], ref[3 * channels :]
            if k <= 4:
                o.out[k] = correlate(*state, i.feat_t[...])
            if k >= 4:
                o.out[k + 2] = 2.0 * correlate(*state, i.g_high[...], i.g_low[...]) - o.out[k - 2]

    total = call(
        rest,
        dict(
            feat_t=feat_t,
            fifth=back["fifth"],
            g_high=back["g_high"],
            g_low=back["g_low"],
            **{f"grad{k}": grads[k] for k in range(3)},
            **{f"both{k}": boths[k] for k in range(3, 7)},
        ),
        dict(out=((top + 1, 2 * channels, every // 2), F32, True)),
    )["out"]
    total = lax.psum(total, "dom").reshape(top + 1, 2, channels, every // 2)
    return got["result"], total.transpose(0, 1, 3, 2).reshape(top + 1, every, channels) * scale


def solution(mesh):
    placed = (
        P("chan", "dom"),
        P("chan", "dom"),
        P(None, "chan", None),
        P("dom", None, None),
        P("dom", None, None),
        P("dom", None, None),
    )
    return jax.shard_map(
        local,
        mesh=mesh,
        in_specs=placed,
        out_specs=(P("chan", "dom"), P(None, None, "chan")),
        check_vma=False,
    )
```

```python
import types

import jax
import jax.numpy as jnp
from jax import lax
from jax.experimental import pallas as pl
from jax.experimental.pallas import tpu as pltpu
from jax.sharding import PartitionSpec as P

F32, BF16 = jnp.float32, jnp.bfloat16
SLOTS = 4
WIDE = 256
MIB = 1 << 20
RING = 8
KINDS = (2, 0, 3, 1)


def dot(a, b, contract=(1, 0)):
    return lax.dot_general(
        a, b, (((contract[0],), (contract[1],)), ((), ())), preferred_element_type=F32
    )


def halves(x):
    high = x.astype(BF16)
    return high, (x - high.astype(F32)).astype(BF16)


def call(body, ins, outs, scratch=(), flops=0):
    specs, operands = [], []
    for value in ins.values():
        x, place = value if isinstance(value, tuple) else (value, "vmem")
        if place:
            x = pltpu.with_memory_space_constraint(x, pltpu.VMEM if place == "vmem" else pltpu.HBM)
        specs.append(pl.BlockSpec(memory_space={"smem": pltpu.SMEM, "hbm": pltpu.HBM}.get(place, pltpu.VMEM)))
        operands.append(x)
    shapes = [
        pltpu.VMEM(shape, dtype) if kept else jax.ShapeDtypeStruct(shape, dtype)
        for shape, dtype, kept in outs.values()
    ]

    def kernel(*refs):
        n, m = len(ins), len(outs)
        i = types.SimpleNamespace(**dict(zip(ins, refs[:n])))
        o = types.SimpleNamespace(**dict(zip(outs, refs[n : n + m])))
        body(i, o, *refs[n + m :])

    got = pl.pallas_call(
        kernel,
        out_shape=shapes,
        in_specs=specs,
        out_specs=[pl.BlockSpec(memory_space=pltpu.VMEM)] * len(outs),
        scratch_shapes=list(scratch),
        compiler_params=pltpu.CompilerParams(vmem_limit_bytes=32 * MIB),
        cost_estimate=pl.CostEstimate(flops=flops, bytes_accessed=MIB, transcendentals=0),
    )(*operands)
    return dict(zip(outs, got))


def exchange(blocks):
    size = lax.axis_size("dom")
    pairs = [[], [], [], []]
    for p in range(size):
        odd, far = p % 2, (p // 2) % 2
        pairs[0].append((p, (p + 1) % size if odd else (p - 1) % size))
        pairs[1].append((p, (p - 1) % size if odd else (p + 1) % size))
        pairs[2].append((p, (p - 2) % size if far else (p + 2) % size))
        pairs[3].append((p, (p + 2) % size if far else (p - 2) % size))
    return [lax.ppermute(block, "dom", pairs[kind]) for block, kind in zip(blocks, KINDS)]


def sides():
    me = lax.axis_index("dom")
    return lax.rem(me, 2), lax.rem(lax.div(me, 2), 2)


def pairs_of_two(forth, back):
    far = sides()[1] == 1
    return {2: jnp.where(far, back, forth), 3: jnp.where(far, forth, back)}


def from_pairs(got):
    odd, far = sides()
    odd, far = odd == 1, far == 1
    near = (None, None)
    if 0 in got:
        near = (jnp.where(odd, got[1], got[0]), jnp.where(odd, got[0], got[1]))
    return *near, jnp.where(far, got[2], got[3]), jnp.where(far, got[3], got[2])


LAYOUT = {
    4: {1: (256,)},
    5: {1: (192,), 2: (128,), 3: (128,)},
    6: {1: (128,), 2: (128, 96), 3: (128, 96)},
    7: {0: (128,), 1: (128,), 2: (96, 64, 128), 3: (96, 64, 128)},
    8: {1: (192, 256), 2: (64, 128), 3: (64, 128)},
}


def carried(i, step, base, kind, index):
    rows = LAYOUT[step][kind]
    start = base + sum(rows[:index])
    return getattr(i, f"halo{KINDS.index(kind)}")[start : start + rows[index], :]


def parted(group):
    odd = sides()[0] == 1
    half = group.shape[0] // 2
    return jnp.where(odd, group[half:], group[:half]), jnp.where(odd, group[:half], group[half:])


def joined(own, other):
    odd = sides()[0] == 1
    return jnp.concatenate([jnp.where(odd, other, own), jnp.where(odd, own, other)], axis=0)


def added(rows, first, second):
    half = rows.shape[0] // 2
    return jnp.concatenate([rows[:half] + first, rows[half:] + second], axis=0)


def hop(block, bit):
    return lax.ppermute(block, "chan", [(c, c ^ bit) for c in range(lax.axis_size("chan"))])


def gather(blocks, marker):
    bit = lax.axis_size("chan") // 4
    blocks = [*lax.optimization_barrier((*blocks, marker))[:2]]
    while bit:
        blocks = blocks + [hop(block, bit) for block in blocks]
        bit //= 2
    return blocks


def collect(blocks, out):
    masks, bit = [0], len(blocks) // 2
    while bit:
        masks = masks + [m ^ bit for m in masks]
        bit //= 2
    place = lax.axis_index("chan")
    for mask, block in zip(masks, blocks):
        rows = block.shape[0]
        out[pl.ds(pl.multiple_of((place ^ mask) * rows, rows), rows), :] = block


def stack(i, o, sems):
    local = i.upper.shape[0]
    copies = [
        pltpu.make_async_copy(i.upper, o.both.at[pl.ds(0, local)], sems.at[0]),
        pltpu.make_async_copy(i.lower, o.both.at[pl.ds(local, local)], sems.at[1]),
    ]
    for copy in copies:
        copy.start()
    for copy in copies:
        copy.wait()


def prepare(i, o, total, held, sems):
    count, tile, _ = held.shape
    nodes = o.pick.shape[0]
    blocks = nodes // tile
    per_row = count // blocks
    copies = [
        pltpu.make_async_copy(
            i.tiles.at[pl.ds(r * per_row, per_row)], held.at[pl.ds(r * per_row, per_row)], sems.at[r]
        )
        for r in range(blocks)
    ]
    for copy in copies:
        copy.start()
    odd, far = sides()
    rows = lax.broadcasted_iota(jnp.int32, (nodes, tile), 0)
    lists = i.lists[0]
    near = jnp.where(odd == 1, lists[0:1], lists[1:2]), jnp.where(odd == 1, lists[1:2], lists[0:1])
    order = [*near, *pairs_of_two(lists[2:3], lists[3:4]).values()]
    for k, kind in enumerate(KINDS):
        hit = rows == jnp.broadcast_to(order[kind], rows.shape)
        o.pick[:, k * tile : (k + 1) * tile] = hit.astype(F32).astype(BF16)
    total[...] = jnp.zeros_like(total)
    for r, copy in enumerate(copies):
        copy.wait()
        here = slice(r * tile, (r + 1) * tile)
        for j in range(per_row):
            col = i.cols[0, r, j]
            slot = col - blocks
            kind = jnp.where(slot < 2, slot ^ odd, slot ^ (1 - far))
            place = sum(jnp.where(kind == k, KINDS.index(k), 0) for k in range(SLOTS))
            col = jnp.where(slot >= 0, blocks + place, col)
            at = pl.ds(pl.multiple_of(col * tile, tile), tile)
            total[at, here] += held[r * per_row + j]
        high, low = halves(total[:, here])
        o.high[:, here] = high
        o.low[:, here] = low
    channels = i.stacked.shape[0] // 2
    feat = i.stacked[channels:]
    o.back[...] = dot(feat, o.high[nodes:, :], (1, 1)) + dot(feat, o.low[nodes:, :], (1, 1))
    o.sent[...] = dot(i.stacked[:channels], o.pick[...])


def summed(both):
    rows = both.shape[0] // 2
    return both[:rows] + both[rows:]


def write_sends(o, parts, extra=None):
    for k, kind in enumerate(KINDS):
        ref = getattr(o, f"send{k}")
        at, width = 0, ref.shape[1]
        for part in parts:
            ref[at : at + part.shape[0], :] = part[:, k * width : (k + 1) * width]
            at += part.shape[0]
        for block in (extra or {}).get(kind, ()):
            ref[at : at + block.shape[0], :] = block
            at += block.shape[0]


def back_halo(both, i, nodes):
    rows = both.shape[0] // 2
    return summed(dot(both, i.high[nodes:, :], (1, 1))) + dot(both[:rows], i.low[nodes:, :], (1, 1))


def correlate(u_high, u_low, g_high, g_low=None):
    if u_low is None:
        total = dot(u_high, g_high)
    else:
        total = summed(dot(jnp.concatenate([u_high, u_low], axis=0), g_high))
    if g_low is not None:
        total += dot(u_high, g_low)
    half = total.shape[1] // 2
    return jnp.concatenate([total[:, :half], total[:, half:]], axis=0)


def transposed(x):
    return x.astype(F32).T.astype(BF16)


def begin(i, o):
    local = i.weight.shape[0]
    own = i.stacked[:local]
    collect([own] + [ref[:local, :] for name, ref in vars(i).items() if name.startswith("block")], o.gathered)
    first = dot(i.weight[...], o.gathered[...])
    o.state[:local] = first
    o.state[local:] = own.astype(F32)
    high, low = halves(first)
    o.both[:local] = high
    o.both[local : 2 * local] = own
    o.both[2 * local : 3 * local] = low
    o.both[3 * local :] = jnp.zeros_like(low)
    parts = summed(dot(jnp.concatenate([high, low], axis=0), i.pick[...])), i.sent[...], i.back[...]
    write_sends(o, parts)


def make_inner(step, top, chains):
    def inner(i, o):
        rows, nodes = o.part.shape
        local = rows // chains
        scale = 1.0 if step == top else 2.0
        width = i.both.shape[0] // 2
        lhs = jnp.concatenate([i.both[:rows], i.both[width : width + rows]], axis=0)
        for start in range(0, nodes, WIDE):
            here = slice(start, start + WIDE)
            total = summed(dot(lhs, i.high[:nodes, here])) + dot(lhs[:rows], i.low[:nodes, here])
            mixed = dot(i.weight[...], i.gathered[:, here])
            value = scale * total[:local] + mixed
            if step > 1:
                value -= i.before[:local, here]
            o.part[:local, here] = value
            if chains > 1:
                value = (1.0 if step == 1 else 2.0) * total[local:]
                if step > 1:
                    value -= i.before[local:, here]
                o.part[local:, here] = value
        if step == 1:
            feat = i.stacked[local:]
            for start in range(0, nodes, WIDE):
                here = slice(start, start + WIDE)
                o.fpart[:, here] = dot(feat, i.high[here, :], (1, 1)) + dot(feat, i.low[here, :], (1, 1))
        if step == 2:
            for start in range(0, nodes, WIDE):
                here = slice(start, start + WIDE)
                total = summed(dot(i.fboth[...], i.high[here, :], (1, 1)))
                total += dot(i.fboth[:local], i.low[here, :], (1, 1))
                o.fpart[:, here] = 2.0 * total - i.stacked[local:, here].astype(F32)
        if step <= 3:
            u_low = None if step == 1 else i.both[width + local : width + 2 * local]
            o.grad[...] = correlate(i.both[local : 2 * local], u_low, i.feat_t[...])

    return inner


def halo_product(i, lhs, rows, here, nodes):
    return summed(dot(lhs, i.high[nodes:, here])) + dot(lhs[:rows], i.low[nodes:, here])


def split_halos(i, rows):
    got = [getattr(i, f"halo{k}") for k in range(SLOTS)]
    high, low = halves(jnp.concatenate([ref[:rows, :] for ref in got], axis=1))
    return jnp.concatenate([high, low], axis=0)


def make_outer(step, chains, following, ring):
    def outer(i, o):
        rows, nodes = i.part.shape
        local = rows // chains
        lhs = split_halos(i, rows)
        for start in range(0, nodes, WIDE):
            here = slice(start, start + WIDE)
            total = halo_product(i, lhs, rows, here, nodes)
            for chain in range(chains):
                mine = slice(chain * local, (chain + 1) * local)
                state = i.part[mine, here] + (1.0 if chain == 1 and step == 1 else 2.0) * total[mine]
                o.state[mine, here] = state
                high, low = halves(state)
                o.both[mine, here] = high
                o.both[rows + chain * local : rows + (chain + 1) * local, here] = low
        live = following * local
        moving = o.both[...]
        if following < chains:
            moving = jnp.concatenate([o.both[:live], o.both[rows : rows + live]], axis=0)
        parts, extra = [summed(dot(moving, i.pick[...]))], []
        if step <= 2:
            got = [getattr(i, f"halo{k}")[rows : rows + local, :] for k in range(SLOTS)]
            high, low = halves(jnp.concatenate(got, axis=1))
            lhs = jnp.concatenate([high, low], axis=0)
            for start in range(0, nodes, WIDE):
                here = slice(start, start + WIDE)
                total = summed(dot(lhs, i.pick[here, :], (1, 1)))
                high, low = halves(i.fpart[:, here] + (1.0 if step == 1 else 2.0) * total)
                o.fboth[:local, here] = high
                o.fboth[local:, here] = low
            if step == 1:
                parts.append(back_halo(o.fboth[...], i, nodes))
        extra = None
        if ring:
            if chains > 1:
                state = o.both[local : 2 * local], o.both[rows + local : rows + 2 * local]

            def got(kind, index):
                return carried(i, step, rows, kind, index)

            def newest(old):
                return 2.0 * correlate(*state, i.g_high[...], i.g_low[...]) - old

            if step == 3:
                o.third[...] = correlate(*state, i.feat_t[...])
                group = jnp.concatenate([i.grad0[...], i.grad1[...], i.grad2[...], o.third[...]], axis=0)
                o.one[...], away = parted(group)
                extra = {1: [away]}
            if step == 4:
                one = i.one[...] + got(1, 0)
                half = one.shape[0] // 2
                o.one[...] = one
                o.fourth[...] = correlate(*state, i.feat_t[...])
                group = jnp.concatenate([o.fourth[...], i.fifth[...], newest(i.grad2[...])], axis=0)
                o.two[...], away = parted(group)
                extra = {1: [away], 2: [one[:half]], 3: [one[half:]]}
            if step == 5:
                one = added(i.one[...], got(2, 0), got(3, 0))
                two = i.two[...] + got(1, 0)
                half, quarter = one.shape[0] // 2, two.shape[0] // 2
                o.one[...], o.two[...] = one, two
                o.seven[...] = newest(i.third[...])
                extra = {1: [o.seven[...]], 2: [one[half:], two[:quarter]], 3: [one[:half], two[quarter:]]}
            if step == 6:
                one = added(i.one[...], got(3, 0), got(2, 0))
                two = added(i.two[...], got(2, 1), got(3, 1))
                seven = i.seven[...] + got(1, 0)
                eight = newest(i.fourth[...])
                half, quarter = seven.shape[0] // 2, two.shape[0] // 2
                o.one[...], o.two[...], o.seven[...], o.eight[...] = one, two, seven, eight
                extra = {
                    0: [eight],
                    1: [eight],
                    2: [two[quarter:], seven[:half], eight],
                    3: [two[:quarter], seven[half:], eight],
                }
            if step == 7:
                o.one[...] = i.one[...]
                two = added(i.two[...], got(3, 0), got(2, 0))
                seven = added(i.seven[...], got(2, 1), got(3, 1))
                m1, p1, m2, p2 = from_pairs({0: got(0, 0), 1: got(1, 0), 2: got(2, 2), 3: got(3, 2)})
                half = seven.shape[0] // 2
                o.two[...], o.seven[...] = two, seven
                o.eight[...] = i.eight[...] + m1 + p1 + m2 + p2
                on = pairs_of_two(m1, p1 + p2)
                extra = {1: [two, i.one[...]], 2: [seven[half:], on[2]], 3: [seven[:half], on[3]]}
        write_sends(o, parts, extra)

    return outer


def settle(i, o):
    blocks = [ref for name, ref in vars(i).items() if name.startswith("block")]
    rows = blocks[0].shape[0] // 2
    for half, out in ((slice(0, rows), o.g_high), (slice(rows, None), o.g_low)):
        collect([ref[half, :] for ref in blocks], o.whole)
        out[...] = transposed(o.whole[...])
    local = i.both.shape[0] // 4
    o.fifth[...] = 2.0 * correlate(
        i.both[local : 2 * local], i.both[3 * local :], o.g_high[...], o.g_low[...]
    ) - i.grad1[...]


def make_last(step, scale, ring):
    def last(i, o):
        rows, nodes = i.part.shape
        lhs = split_halos(i, rows)
        for start in range(0, nodes, WIDE):
            here = slice(start, start + WIDE)
            o.result[:, here] = i.part[:, here] + halo_product(i, lhs, rows, here, nodes)
        if not ring:
            return

        def got(kind, index):
            return carried(i, step, rows, kind, index)

        def put(k, chunk):
            size = chunk.shape[0] // 2
            o.grads[k] = scale * jnp.concatenate([chunk[:size], chunk[size:]], axis=1)

        size = i.eight.shape[0]
        one, two = joined(i.one[...], got(1, 1)), joined(i.two[...], got(1, 0))
        for k in range(4):
            put(k, one[k * size : (k + 1) * size])
        for k in range(3):
            put(4 + k, two[k * size : (k + 1) * size])
        put(7, added(i.seven[...], got(3, 0), got(2, 0)))
        _, _, m2, p2 = from_pairs({2: got(2, 1), 3: got(3, 1)})
        put(8, i.eight[...] + m2 + p2)

    return last


def local(features, cotangent, weights, tile_values, tile_cols, send_list):
    top = weights.shape[0] - 1
    channels, nodes = features.shape
    tile = tile_values.shape[-1]
    every = weights.shape[2]
    wide = nodes + SLOTS * tile
    parts = lax.axis_size("dom")
    ring = parts == RING and top == RING and channels * every == tile * tile and tile == 128
    scale = float(parts * nodes) ** (-0.5)
    sent_shape = ((channels, SLOTS * tile), F32, True)
    whole = ((every, nodes), BF16, True)
    turned = ((nodes, every), BF16, True)
    chunk = ((2 * channels, every // 2), F32, True)

    stacked = call(
        stack,
        dict(upper=(cotangent, "hbm"), lower=(features, "hbm")),
        dict(both=((2 * channels, nodes), BF16, True)),
        [pltpu.SemaphoreType.DMA((2,))],
    )["both"]
    ready = call(
        prepare,
        dict(
            cols=(tile_cols, "smem"),
            lists=(send_list, "load"),
            tiles=(tile_values, "hbm"),
            stacked=stacked,
        ),
        dict(
            high=((wide, nodes), BF16, True),
            low=((wide, nodes), BF16, True),
            pick=((nodes, SLOTS * tile), BF16, True),
            back=sent_shape,
            sent=sent_shape,
        ),
        [
            pltpu.VMEM((wide, nodes), F32),
            pltpu.VMEM(tile_values.shape, F32),
            pltpu.SemaphoreType.DMA((nodes // tile,)),
        ],
        flops=10**10,
    )
    matrix = dict(high=ready["high"], low=ready["low"])
    pick = dict(pick=ready["pick"])
    blocks = gather((stacked, hop(stacked, lax.axis_size("chan") // 2)), ready["back"])

    def messages(rows, step):
        extra = LAYOUT.get(step, {}) if ring else {}
        return {
            f"send{k}": ((rows + sum(extra.get(kind, ())), tile), F32, False) for k, kind in enumerate(KINDS)
        }

    def state_outs(chains):
        rows = chains * channels
        return dict(state=((rows, nodes), F32, True), both=((2 * rows, nodes), BF16, True))

    named = {f"block{k}": (block, "") for k, block in enumerate(blocks[1:])}
    got = call(
        begin,
        dict(
            stacked=stacked,
            weight=(weights[top], ""),
            **pick,
            sent=ready["sent"],
            back=ready["back"],
            **named,
        ),
        dict(gathered=whole, **state_outs(2), **messages(3 * channels, 1)),
    )
    gathered = got["gathered"]

    def turn(i, o):
        rows = [ref[channels:, :] for name, ref in vars(i).items() if name.startswith("block")]
        collect([i.stacked[channels:]] + rows, o.whole)
        o.feat_t[...] = transposed(o.whole[...])

    feat_t = call(turn, dict(stacked=stacked, **named), dict(whole=whole, feat_t=turned))["feat_t"]
    before, boths, grads, back = None, {}, {}, None
    for step in range(1, top + 1):
        chains = 2 if step <= top - 2 else 1
        following = 2 if step + 1 <= top - 2 else 1
        halos = {f"halo{k}": (x, "") for k, x in enumerate(exchange([got[f"send{k}"] for k in range(SLOTS)]))}
        ins = dict(both=got["both"], weight=(weights[top - step], ""), gathered=gathered, **matrix)
        outs = dict(part=((chains * channels, nodes), F32, True))
        if step > 1:
            ins["before"] = before
        if step <= 2:
            ins["stacked"] = stacked
            outs["fpart"] = ((channels, nodes), F32, True)
        if step == 2:
            ins["fboth"] = got["fboth"]
        if step <= 3:
            ins["feat_t"] = feat_t
            outs["grad"] = chunk
        inside = call(
            make_inner(step, top, chains), ins, outs, flops=2 * chains * channels * nodes * nodes * 3
        )
        part = inside["part"]
        if step <= 3:
            grads[step - 1] = inside["grad"]
        if step == 3:
            back_blocks = got["fboth"], hop(got["fboth"], lax.axis_size("chan") // 2)
        if step == 4:
            back = call(
                settle,
                dict(
                    **{f"block{k}": (x, "") for k, x in enumerate(gather(back_blocks, got["send0"]))}, both=boths[3], grad1=grads[1]
                ),
                dict(g_high=turned, g_low=turned, whole=whole, fifth=chunk),
            )
        ins = dict(part=part, **matrix, **halos)
        if step == top:
            outs = dict(result=((channels, nodes), F32, False))
            if ring:
                ins.update({k: got[k] for k in ("one", "two", "seven", "eight")})
                outs["grads"] = ((top + 1, channels, every), F32, False)
            got = call(make_last(step, scale, ring), ins, outs)
            break
        ins.update(pick)
        outs = state_outs(chains)
        if step <= 2:
            ins["fpart"] = inside["fpart"]
            outs["fboth"] = ((2 * channels, nodes), BF16, True)
        if ring and step >= 3:
            one = ((4 * channels, every // 2), F32, True)
            two = ((3 * channels, every // 2), F32, True)
            if step in (3, 4):
                ins["feat_t"] = feat_t
            if step in (4, 5, 6):
                ins.update(g_high=back["g_high"], g_low=back["g_low"])
            if step == 3:
                ins.update({f"grad{k}": grads[k] for k in range(3)})
                outs.update(one=one, third=chunk)
            if step == 4:
                grads[3] = got["third"]
                ins.update(one=got["one"], grad2=grads[2], fifth=back["fifth"])
                outs.update(one=one, two=two, fourth=chunk)
            if step == 5:
                grads[4] = got["fourth"]
                ins.update(one=got["one"], two=got["two"], third=grads[3])
                outs.update(one=one, two=two, seven=chunk)
            if step == 6:
                ins.update({k: got[k] for k in ("one", "two", "seven")}, fourth=grads[4])
                outs.update(one=one, two=two, seven=chunk, eight=chunk)
            if step == 7:
                ins.update({k: got[k] for k in ("one", "two", "seven", "eight")})
                outs.update(one=one, two=two, seven=chunk, eight=chunk)
        sent = following + (1 if step == 1 else 0)
        outs.update(messages(sent * channels, step + 1))
        before = got["state"]
        got = call(make_outer(step, chains, following, ring and step >= 3), ins, outs)
        boths[step] = got["both"]
    if ring:
        return got["result"], jnp.swapaxes(got["grads"], 1, 2)

    def rest(i, o):
        for k in range(3):
            o.out[k] = getattr(i, f"grad{k}")[...]
        o.out[5] = i.fifth[...]
        for k in range(3, 7):
            ref = getattr(i, f"both{k}")
            state = ref[channels : 2 * channels], ref[3 * channels :]
            if k <= 4:
                o.out[k] = correlate(*state, i.feat_t[...])
            if k >= 4:
                o.out[k + 2] = 2.0 * correlate(*state, i.g_high[...], i.g_low[...]) - o.out[k - 2]

    total = call(
        rest,
        dict(
            feat_t=feat_t,
            fifth=back["fifth"],
            g_high=back["g_high"],
            g_low=back["g_low"],
            **{f"grad{k}": grads[k] for k in range(3)},
            **{f"both{k}": boths[k] for k in range(3, 7)},
        ),
        dict(out=((top + 1, 2 * channels, every // 2), F32, True)),
    )["out"]
    total = lax.psum(total, "dom").reshape(top + 1, 2, channels, every // 2)
    return got["result"], total.transpose(0, 1, 3, 2).reshape(top + 1, every, channels) * scale


def solution(mesh):
    placed = (
        P("chan", "dom"),
        P("chan", "dom"),
        P(None, "chan", None),
        P("dom", None, None),
        P("dom", None, None),
        P("dom", None, None),
    )
    return jax.shard_map(
        local,
        mesh=mesh,
        in_specs=placed,
        out_specs=(P("chan", "dom"), P(None, None, "chan")),
        check_vma=False,
    )
```

```python
import types

import jax
import jax.numpy as jnp
from jax import lax
from jax.experimental import pallas as pl
from jax.experimental.pallas import tpu as pltpu
from jax.sharding import PartitionSpec as P

F32, BF16 = jnp.float32, jnp.bfloat16
SLOTS = 4
WIDE = 256
MIB = 1 << 20
RING = 8
QUICK = (1, 2, 7)
KINDS = (2, 0, 3, 1)


def dot(a, b, contract=(1, 0)):
    return lax.dot_general(
        a, b, (((contract[0],), (contract[1],)), ((), ())), preferred_element_type=F32
    )


def halves(x):
    high = x.astype(BF16)
    return high, (x - high.astype(F32)).astype(BF16)


def call(body, ins, outs, scratch=(), flops=0):
    specs, operands = [], []
    for value in ins.values():
        x, place = value if isinstance(value, tuple) else (value, "vmem")
        if place:
            x = pltpu.with_memory_space_constraint(x, pltpu.VMEM if place == "vmem" else pltpu.HBM)
        specs.append(pl.BlockSpec(memory_space={"smem": pltpu.SMEM, "hbm": pltpu.HBM}.get(place, pltpu.VMEM)))
        operands.append(x)
    shapes = [
        pltpu.VMEM(shape, dtype) if kept else jax.ShapeDtypeStruct(shape, dtype)
        for shape, dtype, kept in outs.values()
    ]

    def kernel(*refs):
        n, m = len(ins), len(outs)
        i = types.SimpleNamespace(**dict(zip(ins, refs[:n])))
        o = types.SimpleNamespace(**dict(zip(outs, refs[n : n + m])))
        body(i, o, *refs[n + m :])

    got = pl.pallas_call(
        kernel,
        out_shape=shapes,
        in_specs=specs,
        out_specs=[pl.BlockSpec(memory_space=pltpu.VMEM)] * len(outs),
        scratch_shapes=list(scratch),
        compiler_params=pltpu.CompilerParams(vmem_limit_bytes=32 * MIB),
        cost_estimate=pl.CostEstimate(flops=flops, bytes_accessed=MIB, transcendentals=0),
    )(*operands)
    return dict(zip(outs, got))


def exchange(blocks):
    size = lax.axis_size("dom")
    pairs = [[], [], [], []]
    for p in range(size):
        odd, far = p % 2, (p // 2) % 2
        pairs[0].append((p, (p + 1) % size if odd else (p - 1) % size))
        pairs[1].append((p, (p - 1) % size if odd else (p + 1) % size))
        pairs[2].append((p, (p - 2) % size if far else (p + 2) % size))
        pairs[3].append((p, (p + 2) % size if far else (p - 2) % size))
    return [lax.ppermute(block, "dom", pairs[kind]) for block, kind in zip(blocks, KINDS)]


def sides():
    me = lax.axis_index("dom")
    return lax.rem(me, 2), lax.rem(lax.div(me, 2), 2)


def pairs_of_two(forth, back):
    far = sides()[1] == 1
    return {2: jnp.where(far, back, forth), 3: jnp.where(far, forth, back)}


def from_pairs(got):
    odd, far = sides()
    odd, far = odd == 1, far == 1
    near = (None, None)
    if 0 in got:
        near = (jnp.where(odd, got[1], got[0]), jnp.where(odd, got[0], got[1]))
    return *near, jnp.where(far, got[2], got[3]), jnp.where(far, got[3], got[2])


LAYOUT = {
    4: {1: (256,)},
    5: {1: (192,), 2: (128,), 3: (128,)},
    6: {1: (128,), 2: (128, 96), 3: (128, 96)},
    7: {0: (128,), 1: (128,), 2: (96, 64, 128), 3: (96, 64, 128)},
    8: {1: (192, 256), 2: (64, 128), 3: (64, 128)},
}


def carried(i, step, base, kind, index):
    rows = LAYOUT[step][kind]
    start = base + sum(rows[:index])
    return getattr(i, f"halo{KINDS.index(kind)}")[start : start + rows[index], :]


def parted(group):
    odd = sides()[0] == 1
    half = group.shape[0] // 2
    return jnp.where(odd, group[half:], group[:half]), jnp.where(odd, group[:half], group[half:])


def joined(own, other):
    odd = sides()[0] == 1
    return jnp.concatenate([jnp.where(odd, other, own), jnp.where(odd, own, other)], axis=0)


def added(rows, first, second):
    half = rows.shape[0] // 2
    return jnp.concatenate([rows[:half] + first, rows[half:] + second], axis=0)


def hop(block, bit):
    return lax.ppermute(block, "chan", [(c, c ^ bit) for c in range(lax.axis_size("chan"))])


def gather(blocks, marker):
    bit = lax.axis_size("chan") // 4
    blocks = [*lax.optimization_barrier((*blocks, marker))[:2]]
    while bit:
        blocks = blocks + [hop(block, bit) for block in blocks]
        bit //= 2
    return blocks


def collect(blocks, out):
    masks, bit = [0], len(blocks) // 2
    while bit:
        masks = masks + [m ^ bit for m in masks]
        bit //= 2
    place = lax.axis_index("chan")
    for mask, block in zip(masks, blocks):
        rows = block.shape[0]
        out[pl.ds(pl.multiple_of((place ^ mask) * rows, rows), rows), :] = block


def stack(i, o, sems):
    local = i.upper.shape[0]
    copies = [
        pltpu.make_async_copy(i.upper, o.both.at[pl.ds(0, local)], sems.at[0]),
        pltpu.make_async_copy(i.lower, o.both.at[pl.ds(local, local)], sems.at[1]),
    ]
    for copy in copies:
        copy.start()
    for copy in copies:
        copy.wait()


def prepare(i, o, total, held, sems):
    count, tile, _ = held.shape
    nodes = o.pick.shape[0]
    blocks = nodes // tile
    per_row = count // blocks
    copies = [
        pltpu.make_async_copy(
            i.tiles.at[pl.ds(r * per_row, per_row)], held.at[pl.ds(r * per_row, per_row)], sems.at[r]
        )
        for r in range(blocks)
    ]
    for copy in copies:
        copy.start()
    odd, far = sides()
    rows = lax.broadcasted_iota(jnp.int32, (nodes, tile), 0)
    lists = i.lists[0]
    near = jnp.where(odd == 1, lists[0:1], lists[1:2]), jnp.where(odd == 1, lists[1:2], lists[0:1])
    order = [*near, *pairs_of_two(lists[2:3], lists[3:4]).values()]
    for k, kind in enumerate(KINDS):
        hit = rows == jnp.broadcast_to(order[kind], rows.shape)
        o.pick[:, k * tile : (k + 1) * tile] = hit.astype(F32).astype(BF16)
    total[...] = jnp.zeros_like(total)
    for r, copy in enumerate(copies):
        copy.wait()
        here = slice(r * tile, (r + 1) * tile)
        for j in range(per_row):
            col = i.cols[0, r, j]
            slot = col - blocks
            kind = jnp.where(slot < 2, slot ^ odd, slot ^ (1 - far))
            place = sum(jnp.where(kind == k, KINDS.index(k), 0) for k in range(SLOTS))
            col = jnp.where(slot >= 0, blocks + place, col)
            at = pl.ds(pl.multiple_of(col * tile, tile), tile)
            total[at, here] += held[r * per_row + j]
        high, low = halves(total[:, here])
        o.high[:, here] = high
        o.low[:, here] = low
    channels = i.stacked.shape[0] // 2
    feat = i.stacked[channels:]
    o.back[...] = dot(feat, o.high[nodes:, :], (1, 1)) + dot(feat, o.low[nodes:, :], (1, 1))
    o.sent[...] = dot(i.stacked[:channels], o.pick[...])


def summed(both):
    rows = both.shape[0] // 2
    return both[:rows] + both[rows:]


def write_sends(o, parts, extra=None):
    for k, kind in enumerate(KINDS):
        ref = getattr(o, f"send{k}")
        at, width = 0, ref.shape[1]
        for part in parts:
            ref[at : at + part.shape[0], :] = part[:, k * width : (k + 1) * width]
            at += part.shape[0]
        for block in (extra or {}).get(kind, ()):
            ref[at : at + block.shape[0], :] = block
            at += block.shape[0]


def back_halo(both, i, nodes):
    rows = both.shape[0] // 2
    return summed(dot(both, i.high[nodes:, :], (1, 1))) + dot(both[:rows], i.low[nodes:, :], (1, 1))


def correlate(u_high, u_low, g_high, g_low=None):
    if u_low is None:
        total = dot(u_high, g_high)
    else:
        total = summed(dot(jnp.concatenate([u_high, u_low], axis=0), g_high))
    if g_low is not None:
        total += dot(u_high, g_low)
    half = total.shape[1] // 2
    return jnp.concatenate([total[:, :half], total[:, half:]], axis=0)


def transposed(x):
    return x.astype(F32).T.astype(BF16)


def begin(i, o):
    local = i.weight.shape[0]
    own = i.stacked[:local]
    collect([own] + [ref[:local, :] for name, ref in vars(i).items() if name.startswith("block")], o.gathered)
    first = dot(i.weight[...], o.gathered[...])
    o.state[:local] = first
    o.state[local:] = own.astype(F32)
    high, low = halves(first)
    o.both[:local] = high
    o.both[local : 2 * local] = own
    o.both[2 * local : 3 * local] = low
    o.both[3 * local :] = jnp.zeros_like(low)
    parts = summed(dot(jnp.concatenate([high, low], axis=0), i.pick[...])), i.sent[...], i.back[...]
    write_sends(o, parts)


def make_inner(step, top, chains):
    def inner(i, o):
        rows, nodes = o.part.shape
        local = rows // chains
        scale = 1.0 if step == top else 2.0
        width = i.both.shape[0] // 2
        lhs = jnp.concatenate([i.both[:rows], i.both[width : width + rows]], axis=0)
        for start in range(0, nodes, WIDE):
            here = slice(start, start + WIDE)
            total = summed(dot(lhs, i.high[:nodes, here])) + dot(lhs[:rows], i.low[:nodes, here])
            mixed = dot(i.weight[...], i.gathered[:, here])
            value = scale * total[:local] + mixed
            if step > 1:
                value -= i.before[:local, here]
            o.part[:local, here] = value
            if chains > 1:
                value = (1.0 if step == 1 else 2.0) * total[local:]
                if step > 1:
                    value -= i.before[local:, here]
                o.part[local:, here] = value
        if step == 1:
            feat = i.stacked[local:]
            for start in range(0, nodes, WIDE):
                here = slice(start, start + WIDE)
                o.fpart[:, here] = dot(feat, i.high[here, :], (1, 1)) + dot(feat, i.low[here, :], (1, 1))
        if step == 2:
            for start in range(0, nodes, WIDE):
                here = slice(start, start + WIDE)
                total = summed(dot(i.fboth[...], i.high[here, :], (1, 1)))
                total += dot(i.fboth[:local], i.low[here, :], (1, 1))
                o.fpart[:, here] = 2.0 * total - i.stacked[local:, here].astype(F32)
        if step in QUICK:
            o.picked[...] = summed(dot(jnp.concatenate(halves(o.part[...]), axis=0), i.pick[...]))
        if step == 1:
            o.back[...] = back_halo(jnp.concatenate(halves(o.fpart[...]), axis=0), i, nodes)

    return inner


def make_quick(step, ring):
    def quick(i, o):
        rows = i.picked.shape[0]
        both = split_halos(i, rows)
        total = summed(dot(both, i.through_high[...])) + dot(both[:rows], i.through_low[...])
        if step == 1:
            half = rows // 2
            total = jnp.concatenate([2.0 * total[:half], total[half:]], axis=0)
        else:
            total = 2.0 * total
        parts = [i.picked[...] + total]
        if step == 1:
            local = i.back.shape[0]
            got = [getattr(i, f"halo{k}")[rows : rows + local, :] for k in range(SLOTS)]
            both = jnp.concatenate(halves(jnp.concatenate(got, axis=1)), axis=0)
            total = summed(dot(both, i.through_high[...], (1, 1)))
            parts.append(i.back[...] + total + dot(both[:local], i.through_low[...], (1, 1)))
        extra = None
        if step == 7 and ring:

            def got(kind, index):
                return carried(i, step, rows, kind, index)

            two = added(i.two[...], got(3, 0), got(2, 0))
            seven = added(i.seven[...], got(2, 1), got(3, 1))
            m1, p1, m2, p2 = from_pairs({0: got(0, 0), 1: got(1, 0), 2: got(2, 2), 3: got(3, 2)})
            half = seven.shape[0] // 2
            o.two[...], o.seven[...] = two, seven
            o.eight[...] = i.eight[...] + m1 + p1 + m2 + p2
            on = pairs_of_two(m1, p1 + p2)
            extra = {1: [two, i.one[...]], 2: [seven[half:], on[2]], 3: [seven[:half], on[3]]}
        write_sends(o, parts, extra)

    return quick


def halo_product(i, lhs, rows, here, nodes):
    return summed(dot(lhs, i.high[nodes:, here])) + dot(lhs[:rows], i.low[nodes:, here])


def split_halos(i, rows):
    got = [getattr(i, f"halo{k}") for k in range(SLOTS)]
    high, low = halves(jnp.concatenate([ref[:rows, :] for ref in got], axis=1))
    return jnp.concatenate([high, low], axis=0)


def make_outer(step, chains, following, ring):
    def outer(i, o):
        rows, nodes = i.part.shape
        local = rows // chains
        lhs = split_halos(i, rows)
        for start in range(0, nodes, WIDE):
            here = slice(start, start + WIDE)
            total = halo_product(i, lhs, rows, here, nodes)
            for chain in range(chains):
                mine = slice(chain * local, (chain + 1) * local)
                state = i.part[mine, here] + (1.0 if chain == 1 and step == 1 else 2.0) * total[mine]
                o.state[mine, here] = state
                high, low = halves(state)
                o.both[mine, here] = high
                o.both[rows + chain * local : rows + (chain + 1) * local, here] = low
        live = following * local
        moving = o.both[...]
        if following < chains:
            moving = jnp.concatenate([o.both[:live], o.both[rows : rows + live]], axis=0)
        if step not in QUICK:
            parts = [summed(dot(moving, i.pick[...]))]
        if step <= 2:
            got = [getattr(i, f"halo{k}")[rows : rows + local, :] for k in range(SLOTS)]
            high, low = halves(jnp.concatenate(got, axis=1))
            lhs = jnp.concatenate([high, low], axis=0)
            for start in range(0, nodes, WIDE):
                here = slice(start, start + WIDE)
                total = summed(dot(lhs, i.pick[here, :], (1, 1)))
                high, low = halves(i.fpart[:, here] + (1.0 if step == 1 else 2.0) * total)
                o.fboth[:local, here] = high
                o.fboth[local:, here] = low
        if step in QUICK:
            return
        extra = None
        if ring:
            if chains > 1:
                state = o.both[local : 2 * local], o.both[rows + local : rows + 2 * local]

            def got(kind, index):
                return carried(i, step, rows, kind, index)

            def newest(old):
                return 2.0 * correlate(*state, i.g_high[...], i.g_low[...]) - old

            if step == 3:
                o.third[...] = correlate(*state, i.feat_t[...])
                group = jnp.concatenate([i.grad0[...], i.grad1[...], i.grad2[...], o.third[...]], axis=0)
                o.one[...], away = parted(group)
                extra = {1: [away]}
            if step == 4:
                one = i.one[...] + got(1, 0)
                half = one.shape[0] // 2
                o.one[...] = one
                o.fourth[...] = correlate(*state, i.feat_t[...])
                group = jnp.concatenate([o.fourth[...], i.fifth[...], newest(i.grad2[...])], axis=0)
                o.two[...], away = parted(group)
                extra = {1: [away], 2: [one[:half]], 3: [one[half:]]}
            if step == 5:
                one = added(i.one[...], got(2, 0), got(3, 0))
                two = i.two[...] + got(1, 0)
                half, quarter = one.shape[0] // 2, two.shape[0] // 2
                o.one[...], o.two[...] = one, two
                o.seven[...] = newest(i.third[...])
                extra = {1: [o.seven[...]], 2: [one[half:], two[:quarter]], 3: [one[:half], two[quarter:]]}
            if step == 6:
                one = added(i.one[...], got(3, 0), got(2, 0))
                two = added(i.two[...], got(2, 1), got(3, 1))
                seven = i.seven[...] + got(1, 0)
                eight = newest(i.fourth[...])
                half, quarter = seven.shape[0] // 2, two.shape[0] // 2
                o.one[...], o.two[...], o.seven[...], o.eight[...] = one, two, seven, eight
                extra = {
                    0: [eight],
                    1: [eight],
                    2: [two[quarter:], seven[:half], eight],
                    3: [two[:quarter], seven[half:], eight],
                }
        write_sends(o, parts, extra)

    return outer


def settle(i, o):
    blocks = [ref for name, ref in vars(i).items() if name.startswith("block")]
    rows = blocks[0].shape[0] // 2
    for half, out in ((slice(0, rows), o.g_high), (slice(rows, None), o.g_low)):
        collect([ref[half, :] for ref in blocks], o.whole)
        out[...] = transposed(o.whole[...])
    local = i.both.shape[0] // 4
    o.fifth[...] = 2.0 * correlate(
        i.both[local : 2 * local], i.both[3 * local :], o.g_high[...], o.g_low[...]
    ) - i.grad1[...]


def make_last(step, scale, ring):
    def last(i, o):
        rows, nodes = i.part.shape
        lhs = split_halos(i, rows)
        for start in range(0, nodes, WIDE):
            here = slice(start, start + WIDE)
            o.result[:, here] = i.part[:, here] + halo_product(i, lhs, rows, here, nodes)
        if not ring:
            return

        def got(kind, index):
            return carried(i, step, rows, kind, index)

        def put(k, chunk):
            size = chunk.shape[0] // 2
            o.grads[k] = scale * jnp.concatenate([chunk[:size], chunk[size:]], axis=1)

        size = i.eight.shape[0]
        one, two = joined(i.one[...], got(1, 1)), joined(i.two[...], got(1, 0))
        for k in range(4):
            put(k, one[k * size : (k + 1) * size])
        for k in range(3):
            put(4 + k, two[k * size : (k + 1) * size])
        put(7, added(i.seven[...], got(3, 0), got(2, 0)))
        _, _, m2, p2 = from_pairs({2: got(2, 1), 3: got(3, 1)})
        put(8, i.eight[...] + m2 + p2)

    return last


def local(features, cotangent, weights, tile_values, tile_cols, send_list):
    top = weights.shape[0] - 1
    channels, nodes = features.shape
    tile = tile_values.shape[-1]
    every = weights.shape[2]
    wide = nodes + SLOTS * tile
    parts = lax.axis_size("dom")
    ring = parts == RING and top == RING and channels * every == tile * tile and tile == 128
    scale = float(parts * nodes) ** (-0.5)
    sent_shape = ((channels, SLOTS * tile), F32, True)
    whole = ((every, nodes), BF16, True)
    turned = ((nodes, every), BF16, True)
    chunk = ((2 * channels, every // 2), F32, True)

    stacked = call(
        stack,
        dict(upper=(cotangent, "hbm"), lower=(features, "hbm")),
        dict(both=((2 * channels, nodes), BF16, True)),
        [pltpu.SemaphoreType.DMA((2,))],
    )["both"]
    ready = call(
        prepare,
        dict(
            cols=(tile_cols, "smem"),
            lists=(send_list, "load"),
            tiles=(tile_values, "hbm"),
            stacked=stacked,
        ),
        dict(
            high=((wide, nodes), BF16, True),
            low=((wide, nodes), BF16, True),
            pick=((nodes, SLOTS * tile), BF16, True),
            back=sent_shape,
            sent=sent_shape,
        ),
        [
            pltpu.VMEM((wide, nodes), F32),
            pltpu.VMEM(tile_values.shape, F32),
            pltpu.SemaphoreType.DMA((nodes // tile,)),
        ],
        flops=10**10,
    )
    matrix = dict(high=ready["high"], low=ready["low"])
    pick = dict(pick=ready["pick"])
    blocks = gather((stacked, hop(stacked, lax.axis_size("chan") // 2)), ready["back"])

    def messages(rows, step):
        extra = LAYOUT.get(step, {}) if ring else {}
        return {
            f"send{k}": ((rows + sum(extra.get(kind, ())), tile), F32, False) for k, kind in enumerate(KINDS)
        }

    def state_outs(chains):
        rows = chains * channels
        return dict(state=((rows, nodes), F32, True), both=((2 * rows, nodes), BF16, True))

    named = {f"block{k}": (block, "") for k, block in enumerate(blocks[1:])}
    got = call(
        begin,
        dict(
            stacked=stacked,
            weight=(weights[top], ""),
            **pick,
            sent=ready["sent"],
            back=ready["back"],
            **named,
        ),
        dict(gathered=whole, **state_outs(2), **messages(3 * channels, 1)),
    )
    gathered = got["gathered"]

    def pass_through(i, o):
        for matrix, out in ((i.high, o.through_high), (i.low, o.through_low)):
            out[...] = dot(matrix[nodes:, :], i.pick[...]).astype(BF16)

    through = ((SLOTS * tile, SLOTS * tile), BF16, True)
    through = call(pass_through, dict(**matrix, **pick), dict(through_high=through, through_low=through))

    def opening(i, o):
        rows = [ref[channels:, :] for name, ref in vars(i).items() if name.startswith("block")]
        collect([i.stacked[channels:]] + rows, o.whole)
        o.feat_t[...] = transposed(o.whole[...])
        o.grad0[...] = correlate(i.stacked[:channels], None, o.feat_t[...])
        for ref, out in ((i.both1, o.grad1), (i.both2, o.grad2)):
            out[...] = correlate(ref[channels : 2 * channels], ref[3 * channels :], o.feat_t[...])

    before, boths, grads, back = None, {}, {}, None
    for step in range(1, top + 1):
        chains = 2 if step <= top - 2 else 1
        following = 2 if step + 1 <= top - 2 else 1
        halos = {f"halo{k}": (x, "") for k, x in enumerate(exchange([got[f"send{k}"] for k in range(SLOTS)]))}
        ins = dict(both=got["both"], weight=(weights[top - step], ""), gathered=gathered, **matrix)
        outs = dict(part=((chains * channels, nodes), F32, True))
        if step > 1:
            ins["before"] = before
        if step in QUICK:
            ins.update(pick)
            outs["picked"] = ((chains * channels, SLOTS * tile), F32, True)
        if step == 1:
            outs["back"] = sent_shape
        if step <= 2:
            ins["stacked"] = stacked
            outs["fpart"] = ((channels, nodes), F32, True)
        if step == 2:
            ins["fboth"] = got["fboth"]
        inside = call(
            make_inner(step, top, chains), ins, outs, flops=2 * chains * channels * nodes * nodes * 3
        )
        part = inside["part"]
        if step == 3:
            opened = call(
                opening,
                dict(stacked=stacked, **named, both1=boths[1], both2=boths[2]),
                dict(whole=whole, feat_t=turned, **{f"grad{k}": chunk for k in range(3)}),
            )
            feat_t, grads = opened["feat_t"], {k: opened[f"grad{k}"] for k in range(3)}
        if step == 3:
            back_blocks = got["fboth"], hop(got["fboth"], lax.axis_size("chan") // 2)
        if step == 4:
            back = call(
                settle,
                dict(
                    **{f"block{k}": (x, "") for k, x in enumerate(gather(back_blocks, got["send0"]))}, both=boths[3], grad1=grads[1]
                ),
                dict(g_high=turned, g_low=turned, whole=whole, fifth=chunk),
            )
        ins = dict(part=part, **matrix, **halos)
        if step == top:
            outs = dict(result=((channels, nodes), F32, False))
            if ring:
                ins.update({k: got[k] for k in ("one", "two", "seven", "eight")})
                outs["grads"] = ((top + 1, channels, every), F32, False)
            got = call(make_last(step, scale, ring), ins, outs)
            break
        ins.update(pick)
        outs = state_outs(chains)
        if step <= 2:
            ins["fpart"] = inside["fpart"]
            outs["fboth"] = ((2 * channels, nodes), BF16, True)
        if ring and step >= 3:
            one = ((4 * channels, every // 2), F32, True)
            two = ((3 * channels, every // 2), F32, True)
            if step in (3, 4):
                ins["feat_t"] = feat_t
            if step in (4, 5, 6):
                ins.update(g_high=back["g_high"], g_low=back["g_low"])
            if step == 3:
                ins.update({f"grad{k}": grads[k] for k in range(3)})
                outs.update(one=one, third=chunk)
            if step == 4:
                grads[3] = got["third"]
                ins.update(one=got["one"], grad2=grads[2], fifth=back["fifth"])
                outs.update(one=one, two=two, fourth=chunk)
            if step == 5:
                grads[4] = got["fourth"]
                ins.update(one=got["one"], two=got["two"], third=grads[3])
                outs.update(one=one, two=two, seven=chunk)
            if step == 6:
                ins.update({k: got[k] for k in ("one", "two", "seven")}, fourth=grads[4])
                outs.update(one=one, two=two, seven=chunk, eight=chunk)
        sent = following + (1 if step == 1 else 0)
        sends = messages(sent * channels, step + 1)
        ready = {}
        if step in QUICK:
            told = dict(picked=inside["picked"], **through, **halos)
            if step == 1:
                told["back"] = inside["back"]
            if step == 7 and ring:
                told.update({k: got[k] for k in ("one", "two", "seven", "eight")})
                sends.update(two=two, seven=chunk, eight=chunk)
                ready["one"] = got["one"]
            ready.update(call(make_quick(step, ring), told, sends))
        else:
            outs.update(sends)
        before = got["state"]
        got = call(make_outer(step, chains, following, ring and step >= 3), ins, outs)
        got.update(ready)
        boths[step] = got["both"]
    if ring:
        return got["result"], jnp.swapaxes(got["grads"], 1, 2)

    def rest(i, o):
        for k in range(3):
            o.out[k] = getattr(i, f"grad{k}")[...]
        o.out[5] = i.fifth[...]
        for k in range(3, 7):
            ref = getattr(i, f"both{k}")
            state = ref[channels : 2 * channels], ref[3 * channels :]
            if k <= 4:
                o.out[k] = correlate(*state, i.feat_t[...])
            if k >= 4:
                o.out[k + 2] = 2.0 * correlate(*state, i.g_high[...], i.g_low[...]) - o.out[k - 2]

    total = call(
        rest,
        dict(
            feat_t=feat_t,
            fifth=back["fifth"],
            g_high=back["g_high"],
            g_low=back["g_low"],
            **{f"grad{k}": grads[k] for k in range(3)},
            **{f"both{k}": boths[k] for k in range(3, 7)},
        ),
        dict(out=((top + 1, 2 * channels, every // 2), F32, True)),
    )["out"]
    total = lax.psum(total, "dom").reshape(top + 1, 2, channels, every // 2)
    return got["result"], total.transpose(0, 1, 3, 2).reshape(top + 1, every, channels) * scale


def solution(mesh):
    placed = (
        P("chan", "dom"),
        P("chan", "dom"),
        P(None, "chan", None),
        P("dom", None, None),
        P("dom", None, None),
        P("dom", None, None),
    )
    return jax.shard_map(
        local,
        mesh=mesh,
        in_specs=placed,
        out_specs=(P("chan", "dom"), P(None, None, "chan")),
        check_vma=False,
    )
```

```python
import types

import jax
import jax.numpy as jnp
from jax import lax
from jax.experimental import pallas as pl
from jax.experimental.pallas import tpu as pltpu
from jax.sharding import PartitionSpec as P

F32, BF16 = jnp.float32, jnp.bfloat16
SLOTS = 4
WIDE = 256
MIB = 1 << 20
RING = 8
QUICK = (1, 2, 4, 5, 6, 7)
BESIDE = ("base4", "base6", "fifth", "f_through_high", "f_through_low")
KINDS = (2, 0, 3, 1)


def dot(a, b, contract=(1, 0)):
    return lax.dot_general(
        a, b, (((contract[0],), (contract[1],)), ((), ())), preferred_element_type=F32
    )


def halves(x):
    high = x.astype(BF16)
    return high, (x - high.astype(F32)).astype(BF16)


def call(body, ins, outs, scratch=(), flops=0):
    specs, operands = [], []
    for value in ins.values():
        x, place = value if isinstance(value, tuple) else (value, "vmem")
        if place:
            x = pltpu.with_memory_space_constraint(x, pltpu.VMEM if place == "vmem" else pltpu.HBM)
        specs.append(pl.BlockSpec(memory_space={"smem": pltpu.SMEM, "hbm": pltpu.HBM}.get(place, pltpu.VMEM)))
        operands.append(x)
    shapes = [
        pltpu.VMEM(shape, dtype) if kept else jax.ShapeDtypeStruct(shape, dtype)
        for shape, dtype, kept in outs.values()
    ]

    def kernel(*refs):
        n, m = len(ins), len(outs)
        i = types.SimpleNamespace(**dict(zip(ins, refs[:n])))
        o = types.SimpleNamespace(**dict(zip(outs, refs[n : n + m])))
        body(i, o, *refs[n + m :])

    got = pl.pallas_call(
        kernel,
        out_shape=shapes,
        in_specs=specs,
        out_specs=[pl.BlockSpec(memory_space=pltpu.VMEM)] * len(outs),
        scratch_shapes=list(scratch),
        compiler_params=pltpu.CompilerParams(vmem_limit_bytes=32 * MIB),
        cost_estimate=pl.CostEstimate(flops=flops, bytes_accessed=MIB, transcendentals=0),
    )(*operands)
    return dict(zip(outs, got))


def exchange(blocks):
    size = lax.axis_size("dom")
    pairs = [[], [], [], []]
    for p in range(size):
        odd, far = p % 2, (p // 2) % 2
        pairs[0].append((p, (p + 1) % size if odd else (p - 1) % size))
        pairs[1].append((p, (p - 1) % size if odd else (p + 1) % size))
        pairs[2].append((p, (p - 2) % size if far else (p + 2) % size))
        pairs[3].append((p, (p + 2) % size if far else (p - 2) % size))
    return [lax.ppermute(block, "dom", pairs[kind]) for block, kind in zip(blocks, KINDS)]


def sides():
    me = lax.axis_index("dom")
    return lax.rem(me, 2), lax.rem(lax.div(me, 2), 2)


def pairs_of_two(forth, back):
    far = sides()[1] == 1
    return {2: jnp.where(far, back, forth), 3: jnp.where(far, forth, back)}


def from_pairs(got):
    odd, far = sides()
    odd, far = odd == 1, far == 1
    near = (None, None)
    if 0 in got:
        near = (jnp.where(odd, got[1], got[0]), jnp.where(odd, got[0], got[1]))
    return *near, jnp.where(far, got[2], got[3]), jnp.where(far, got[3], got[2])


LAYOUT = {
    4: {1: (256,)},
    5: {1: (192,), 2: (128,), 3: (128,)},
    6: {1: (128,), 2: (128, 96), 3: (128, 96)},
    7: {0: (128,), 1: (128,), 2: (96, 64, 128), 3: (96, 64, 128)},
    8: {1: (192, 256), 2: (64, 128), 3: (64, 128)},
}


def carried(i, step, base, kind, index):
    rows = LAYOUT[step][kind]
    start = base + sum(rows[:index])
    return getattr(i, f"halo{KINDS.index(kind)}")[start : start + rows[index], :]


def parted(group):
    odd = sides()[0] == 1
    half = group.shape[0] // 2
    return jnp.where(odd, group[half:], group[:half]), jnp.where(odd, group[:half], group[half:])


def joined(own, other):
    odd = sides()[0] == 1
    return jnp.concatenate([jnp.where(odd, other, own), jnp.where(odd, own, other)], axis=0)


def added(rows, first, second):
    half = rows.shape[0] // 2
    return jnp.concatenate([rows[:half] + first, rows[half:] + second], axis=0)


def hop(block, bit):
    return lax.ppermute(block, "chan", [(c, c ^ bit) for c in range(lax.axis_size("chan"))])


def gather(blocks, marker):
    bit = lax.axis_size("chan") // 4
    blocks = [*lax.optimization_barrier((*blocks, marker))[:2]]
    while bit:
        blocks = blocks + [hop(block, bit) for block in blocks]
        bit //= 2
    return blocks


def collect(blocks, out):
    masks, bit = [0], len(blocks) // 2
    while bit:
        masks = masks + [m ^ bit for m in masks]
        bit //= 2
    place = lax.axis_index("chan")
    for mask, block in zip(masks, blocks):
        rows = block.shape[0]
        out[pl.ds(pl.multiple_of((place ^ mask) * rows, rows), rows), :] = block


def stack(i, o, sems):
    local = i.upper.shape[0]
    copies = [
        pltpu.make_async_copy(i.upper, o.both.at[pl.ds(0, local)], sems.at[0]),
        pltpu.make_async_copy(i.lower, o.both.at[pl.ds(local, local)], sems.at[1]),
    ]
    for copy in copies:
        copy.start()
    for copy in copies:
        copy.wait()


def prepare(i, o, total, held, sems):
    count, tile, _ = held.shape
    nodes = o.pick.shape[0]
    blocks = nodes // tile
    per_row = count // blocks
    copies = [
        pltpu.make_async_copy(
            i.tiles.at[pl.ds(r * per_row, per_row)], held.at[pl.ds(r * per_row, per_row)], sems.at[r]
        )
        for r in range(blocks)
    ]
    for copy in copies:
        copy.start()
    odd, far = sides()
    rows = lax.broadcasted_iota(jnp.int32, (nodes, tile), 0)
    lists = i.lists[0]
    near = jnp.where(odd == 1, lists[0:1], lists[1:2]), jnp.where(odd == 1, lists[1:2], lists[0:1])
    order = [*near, *pairs_of_two(lists[2:3], lists[3:4]).values()]
    for k, kind in enumerate(KINDS):
        hit = rows == jnp.broadcast_to(order[kind], rows.shape)
        o.pick[:, k * tile : (k + 1) * tile] = hit.astype(F32).astype(BF16)
    total[...] = jnp.zeros_like(total)
    for r, copy in enumerate(copies):
        copy.wait()
        here = slice(r * tile, (r + 1) * tile)
        for j in range(per_row):
            col = i.cols[0, r, j]
            slot = col - blocks
            kind = jnp.where(slot < 2, slot ^ odd, slot ^ (1 - far))
            place = sum(jnp.where(kind == k, KINDS.index(k), 0) for k in range(SLOTS))
            col = jnp.where(slot >= 0, blocks + place, col)
            at = pl.ds(pl.multiple_of(col * tile, tile), tile)
            total[at, here] += held[r * per_row + j]
        high, low = halves(total[:, here])
        o.high[:, here] = high
        o.low[:, here] = low
    channels = i.stacked.shape[0] // 2
    feat = i.stacked[channels:]
    o.back[...] = dot(feat, o.high[nodes:, :], (1, 1)) + dot(feat, o.low[nodes:, :], (1, 1))
    o.sent[...] = dot(i.stacked[:channels], o.pick[...])


def summed(both):
    rows = both.shape[0] // 2
    return both[:rows] + both[rows:]


def write_sends(o, parts, extra=None):
    for k, kind in enumerate(KINDS):
        ref = getattr(o, f"send{k}")
        at, width = 0, ref.shape[1]
        for part in parts:
            ref[at : at + part.shape[0], :] = part[:, k * width : (k + 1) * width]
            at += part.shape[0]
        for block in (extra or {}).get(kind, ()):
            ref[at : at + block.shape[0], :] = block
            at += block.shape[0]


def back_halo(both, i, nodes):
    rows = both.shape[0] // 2
    return summed(dot(both, i.high[nodes:, :], (1, 1))) + dot(both[:rows], i.low[nodes:, :], (1, 1))


def correlate(u_high, u_low, g_high, g_low=None):
    if u_low is None:
        total = dot(u_high, g_high)
    else:
        total = summed(dot(jnp.concatenate([u_high, u_low], axis=0), g_high))
    if g_low is not None:
        total += dot(u_high, g_low)
    half = total.shape[1] // 2
    return jnp.concatenate([total[:, :half], total[:, half:]], axis=0)


def transposed(x):
    return x.astype(F32).T.astype(BF16)


def begin(i, o):
    local = i.weight.shape[0]
    own = i.stacked[:local]
    collect([own] + [ref[:local, :] for name, ref in vars(i).items() if name.startswith("block")], o.gathered)
    first = dot(i.weight[...], o.gathered[...])
    o.state[:local] = first
    o.state[local:] = own.astype(F32)
    high, low = halves(first)
    o.both[:local] = high
    o.both[local : 2 * local] = own
    o.both[2 * local : 3 * local] = low
    o.both[3 * local :] = jnp.zeros_like(low)
    parts = summed(dot(jnp.concatenate([high, low], axis=0), i.pick[...])), i.sent[...], i.back[...]
    write_sends(o, parts)


def make_inner(step, top, chains):
    def inner(i, o):
        rows, nodes = o.part.shape
        local = rows // chains
        scale = 1.0 if step == top else 2.0
        width = i.both.shape[0] // 2
        lhs = jnp.concatenate([i.both[:rows], i.both[width : width + rows]], axis=0)
        for start in range(0, nodes, WIDE):
            here = slice(start, start + WIDE)
            total = summed(dot(lhs, i.high[:nodes, here])) + dot(lhs[:rows], i.low[:nodes, here])
            mixed = dot(i.weight[...], i.gathered[:, here])
            value = scale * total[:local] + mixed
            if step > 1:
                value -= i.before[:local, here]
            o.part[:local, here] = value
            if chains > 1:
                value = (1.0 if step == 1 else 2.0) * total[local:]
                if step > 1:
                    value -= i.before[local:, here]
                o.part[local:, here] = value
        if step == 1:
            feat = i.stacked[local:]
            for start in range(0, nodes, WIDE):
                here = slice(start, start + WIDE)
                o.fpart[:, here] = dot(feat, i.high[here, :], (1, 1)) + dot(feat, i.low[here, :], (1, 1))
        if step == 2:
            for start in range(0, nodes, WIDE):
                here = slice(start, start + WIDE)
                total = summed(dot(i.fboth[...], i.high[here, :], (1, 1)))
                total += dot(i.fboth[:local], i.low[here, :], (1, 1))
                o.fpart[:, here] = 2.0 * total - i.stacked[local:, here].astype(F32)
        if step in QUICK:
            o.picked[...] = summed(dot(jnp.concatenate(halves(o.part[...]), axis=0), i.pick[...]))
        if step == 1:
            o.back[...] = back_halo(jnp.concatenate(halves(o.fpart[...]), axis=0), i, nodes)
        if step in (5, 6):
            o.base[...] = correlate(*halves(o.part[local:, :]), i.g_high[...], i.g_low[...])

    return inner


def make_quick(step, chains, following, ring):
    def quick(i, o):
        rows = i.picked.shape[0]
        local = rows // chains
        both = split_halos(i, rows)
        total = summed(dot(both, i.through_high[...])) + dot(both[:rows], i.through_low[...])
        if step == 1:
            total = jnp.concatenate([2.0 * total[:local], total[local:]], axis=0)
        else:
            total = 2.0 * total
        parts = [(i.picked[...] + total)[: following * local]]
        if step == 1:
            got = [getattr(i, f"halo{k}")[rows : rows + local, :] for k in range(SLOTS)]
            back = jnp.concatenate(halves(jnp.concatenate(got, axis=1)), axis=0)
            total = summed(dot(back, i.through_high[...], (1, 1)))
            parts.append(i.back[...] + total + dot(back[:local], i.through_low[...], (1, 1)))
        if not ring or step <= 2:
            write_sends(o, parts)
            return
        if chains > 1:
            arrived = both[local : 2 * local], both[rows + local :]

        def got(kind, index):
            return carried(i, step, rows, kind, index)

        def newest(base, old):
            return 2.0 * (base + 2.0 * correlate(*arrived, i.g_through_high[...], i.g_through_low[...])) - old

        if step == 4:
            one = i.one[...] + got(1, 0)
            half = one.shape[0] // 2
            o.one[...] = one
            o.fourth[...] = i.base4[...] + 2.0 * correlate(*arrived, i.f_through_high[...], i.f_through_low[...])
            group = [o.fourth[...], i.fifth[...], newest(i.base6[...], i.grad2[...])]
            o.two[...], away = parted(jnp.concatenate(group, axis=0))
            extra = {1: [away], 2: [one[:half]], 3: [one[half:]]}
        if step == 5:
            one = added(i.one[...], got(2, 0), got(3, 0))
            two = i.two[...] + got(1, 0)
            half, quarter = one.shape[0] // 2, two.shape[0] // 2
            o.one[...], o.two[...] = one, two
            o.seven[...] = newest(i.base[...], i.third[...])
            extra = {1: [o.seven[...]], 2: [one[half:], two[:quarter]], 3: [one[:half], two[quarter:]]}
        if step == 6:
            one = added(i.one[...], got(3, 0), got(2, 0))
            two = added(i.two[...], got(2, 1), got(3, 1))
            seven = i.seven[...] + got(1, 0)
            eight = newest(i.base[...], i.fourth[...])
            half, quarter = seven.shape[0] // 2, two.shape[0] // 2
            o.one[...], o.two[...], o.seven[...], o.eight[...] = one, two, seven, eight
            extra = {
                0: [eight],
                1: [eight],
                2: [two[quarter:], seven[:half], eight],
                3: [two[:quarter], seven[half:], eight],
            }
        if step == 7:
            two = added(i.two[...], got(3, 0), got(2, 0))
            seven = added(i.seven[...], got(2, 1), got(3, 1))
            m1, p1, m2, p2 = from_pairs({0: got(0, 0), 1: got(1, 0), 2: got(2, 2), 3: got(3, 2)})
            half = seven.shape[0] // 2
            o.two[...], o.seven[...] = two, seven
            o.eight[...] = i.eight[...] + m1 + p1 + m2 + p2
            on = pairs_of_two(m1, p1 + p2)
            extra = {1: [two, i.one[...]], 2: [seven[half:], on[2]], 3: [seven[:half], on[3]]}
        write_sends(o, parts, extra)

    return quick


def halo_product(i, lhs, rows, here, nodes):
    return summed(dot(lhs, i.high[nodes:, here])) + dot(lhs[:rows], i.low[nodes:, here])


def split_halos(i, rows):
    got = [getattr(i, f"halo{k}") for k in range(SLOTS)]
    high, low = halves(jnp.concatenate([ref[:rows, :] for ref in got], axis=1))
    return jnp.concatenate([high, low], axis=0)


def make_outer(step, chains, following, ring):
    def outer(i, o):
        rows, nodes = i.part.shape
        local = rows // chains
        lhs = split_halos(i, rows)
        for start in range(0, nodes, WIDE):
            here = slice(start, start + WIDE)
            total = halo_product(i, lhs, rows, here, nodes)
            for chain in range(chains):
                mine = slice(chain * local, (chain + 1) * local)
                state = i.part[mine, here] + (1.0 if chain == 1 and step == 1 else 2.0) * total[mine]
                o.state[mine, here] = state
                high, low = halves(state)
                o.both[mine, here] = high
                o.both[rows + chain * local : rows + (chain + 1) * local, here] = low
        live = following * local
        moving = o.both[...]
        if following < chains:
            moving = jnp.concatenate([o.both[:live], o.both[rows : rows + live]], axis=0)
        if step not in QUICK:
            parts = [summed(dot(moving, i.pick[...]))]
        if step <= 2:
            got = [getattr(i, f"halo{k}")[rows : rows + local, :] for k in range(SLOTS)]
            high, low = halves(jnp.concatenate(got, axis=1))
            lhs = jnp.concatenate([high, low], axis=0)
            for start in range(0, nodes, WIDE):
                here = slice(start, start + WIDE)
                total = summed(dot(lhs, i.pick[here, :], (1, 1)))
                high, low = halves(i.fpart[:, here] + (1.0 if step == 1 else 2.0) * total)
                o.fboth[:local, here] = high
                o.fboth[local:, here] = low
        if step in QUICK:
            return
        extra = None
        if ring:
            if chains > 1:
                state = o.both[local : 2 * local], o.both[rows + local : rows + 2 * local]

            def got(kind, index):
                return carried(i, step, rows, kind, index)

            def newest(old):
                return 2.0 * correlate(*state, i.g_high[...], i.g_low[...]) - old

            if step == 3:
                o.third[...] = correlate(*state, i.feat_t[...])
                group = jnp.concatenate([i.grad0[...], i.grad1[...], i.grad2[...], o.third[...]], axis=0)
                o.one[...], away = parted(group)
                extra = {1: [away]}
        write_sends(o, parts, extra)

    return outer


def settle(i, o):
    blocks = [ref for name, ref in vars(i).items() if name.startswith("block")]
    rows = blocks[0].shape[0] // 2
    for half, out in ((slice(0, rows), o.g_high), (slice(rows, None), o.g_low)):
        collect([ref[half, :] for ref in blocks], o.whole)
        out[...] = transposed(o.whole[...])
    local = i.both.shape[0] // 4
    o.fifth[...] = 2.0 * correlate(
        i.both[local : 2 * local], i.both[3 * local :], o.g_high[...], o.g_low[...]
    ) - i.grad1[...]
    nodes = i.part.shape[1]
    part = halves(i.part[local:, :])
    o.base4[...] = correlate(*part, i.feat_t[...])
    o.base6[...] = correlate(*part, o.g_high[...], o.g_low[...])
    high, low = i.high[nodes:, :], i.low[nodes:, :]
    product = dot(high, i.feat_t[...]) + dot(low, i.feat_t[...])
    o.f_through_high[...], o.f_through_low[...] = halves(product)
    product = dot(high, o.g_high[...]) + dot(high, o.g_low[...]) + dot(low, o.g_high[...])
    o.g_through_high[...], o.g_through_low[...] = halves(product)


def make_last(step, scale, ring):
    def last(i, o):
        rows, nodes = i.part.shape
        lhs = split_halos(i, rows)
        for start in range(0, nodes, WIDE):
            here = slice(start, start + WIDE)
            o.result[:, here] = i.part[:, here] + halo_product(i, lhs, rows, here, nodes)
        if not ring:
            return

        def got(kind, index):
            return carried(i, step, rows, kind, index)

        def put(k, chunk):
            size = chunk.shape[0] // 2
            o.grads[k] = scale * jnp.concatenate([chunk[:size], chunk[size:]], axis=1)

        size = i.eight.shape[0]
        one, two = joined(i.one[...], got(1, 1)), joined(i.two[...], got(1, 0))
        for k in range(4):
            put(k, one[k * size : (k + 1) * size])
        for k in range(3):
            put(4 + k, two[k * size : (k + 1) * size])
        put(7, added(i.seven[...], got(3, 0), got(2, 0)))
        _, _, m2, p2 = from_pairs({2: got(2, 1), 3: got(3, 1)})
        put(8, i.eight[...] + m2 + p2)

    return last


def local(features, cotangent, weights, tile_values, tile_cols, send_list):
    top = weights.shape[0] - 1
    channels, nodes = features.shape
    tile = tile_values.shape[-1]
    every = weights.shape[2]
    wide = nodes + SLOTS * tile
    parts = lax.axis_size("dom")
    ring = parts == RING and top == RING and channels * every == tile * tile and tile == 128
    scale = float(parts * nodes) ** (-0.5)
    sent_shape = ((channels, SLOTS * tile), F32, True)
    whole = ((every, nodes), BF16, True)
    turned = ((nodes, every), BF16, True)
    chunk = ((2 * channels, every // 2), F32, True)
    along = ((SLOTS * tile, every), BF16, True)

    stacked = call(
        stack,
        dict(upper=(cotangent, "hbm"), lower=(features, "hbm")),
        dict(both=((2 * channels, nodes), BF16, True)),
        [pltpu.SemaphoreType.DMA((2,))],
    )["both"]
    ready = call(
        prepare,
        dict(
            cols=(tile_cols, "smem"),
            lists=(send_list, "load"),
            tiles=(tile_values, "hbm"),
            stacked=stacked,
        ),
        dict(
            high=((wide, nodes), BF16, True),
            low=((wide, nodes), BF16, True),
            pick=((nodes, SLOTS * tile), BF16, True),
            back=sent_shape,
            sent=sent_shape,
        ),
        [
            pltpu.VMEM((wide, nodes), F32),
            pltpu.VMEM(tile_values.shape, F32),
            pltpu.SemaphoreType.DMA((nodes // tile,)),
        ],
        flops=10**10,
    )
    matrix = dict(high=ready["high"], low=ready["low"])
    pick = dict(pick=ready["pick"])
    blocks = gather((stacked, hop(stacked, lax.axis_size("chan") // 2)), ready["back"])

    def messages(rows, step):
        extra = LAYOUT.get(step, {}) if ring else {}
        return {
            f"send{k}": ((rows + sum(extra.get(kind, ())), tile), F32, False) for k, kind in enumerate(KINDS)
        }

    def state_outs(chains):
        rows = chains * channels
        return dict(state=((rows, nodes), F32, True), both=((2 * rows, nodes), BF16, True))

    named = {f"block{k}": (block, "") for k, block in enumerate(blocks[1:])}
    got = call(
        begin,
        dict(
            stacked=stacked,
            weight=(weights[top], ""),
            **pick,
            sent=ready["sent"],
            back=ready["back"],
            **named,
        ),
        dict(gathered=whole, **state_outs(2), **messages(3 * channels, 1)),
    )
    gathered = got["gathered"]

    def pass_through(i, o):
        for matrix, out in ((i.high, o.through_high), (i.low, o.through_low)):
            out[...] = dot(matrix[nodes:, :], i.pick[...]).astype(BF16)

    through = ((SLOTS * tile, SLOTS * tile), BF16, True)
    through = call(pass_through, dict(**matrix, **pick), dict(through_high=through, through_low=through))

    def opening(i, o):
        rows = [ref[channels:, :] for name, ref in vars(i).items() if name.startswith("block")]
        collect([i.stacked[channels:]] + rows, o.whole)
        o.feat_t[...] = transposed(o.whole[...])
        o.grad0[...] = correlate(i.stacked[:channels], None, o.feat_t[...])
        for ref, out in ((i.both1, o.grad1), (i.both2, o.grad2)):
            out[...] = correlate(ref[channels : 2 * channels], ref[3 * channels :], o.feat_t[...])

    before, boths, grads, back = None, {}, {}, None
    for step in range(1, top + 1):
        chains = 2 if step <= top - 2 else 1
        following = 2 if step + 1 <= top - 2 else 1
        halos = {f"halo{k}": (x, "") for k, x in enumerate(exchange([got[f"send{k}"] for k in range(SLOTS)]))}
        ins = dict(both=got["both"], weight=(weights[top - step], ""), gathered=gathered, **matrix)
        outs = dict(part=((chains * channels, nodes), F32, True))
        if step > 1:
            ins["before"] = before
        if step in QUICK:
            ins.update(pick)
            outs["picked"] = ((chains * channels, SLOTS * tile), F32, True)
        if step in (5, 6):
            ins.update(g_high=back["g_high"], g_low=back["g_low"])
            outs["base"] = chunk
        if step == 1:
            outs["back"] = sent_shape
        if step <= 2:
            ins["stacked"] = stacked
            outs["fpart"] = ((channels, nodes), F32, True)
        if step == 2:
            ins["fboth"] = got["fboth"]
        inside = call(
            make_inner(step, top, chains), ins, outs, flops=2 * chains * channels * nodes * nodes * 3
        )
        part = inside["part"]
        if step == 3:
            opened = call(
                opening,
                dict(stacked=stacked, **named, both1=boths[1], both2=boths[2]),
                dict(whole=whole, feat_t=turned, **{f"grad{k}": chunk for k in range(3)}),
            )
            feat_t, grads = opened["feat_t"], {k: opened[f"grad{k}"] for k in range(3)}
        if step == 3:
            back_blocks = got["fboth"], hop(got["fboth"], lax.axis_size("chan") // 2)
        if step == 4:
            back = call(
                settle,
                dict(
                    **{f"block{k}": (x, "") for k, x in enumerate(gather(back_blocks, got["send0"]))}, both=boths[3],
                    grad1=grads[1],
                    part=part,
                    feat_t=feat_t,
                    **matrix,
                ),
                dict(
                    g_high=turned, g_low=turned, whole=whole, fifth=chunk, base4=chunk, base6=chunk,
                    **{f"{name}_through_{half}": along for name in "fg" for half in ("high", "low")},
                ),
            )
        ins = dict(part=part, **matrix, **halos)
        if step == top:
            outs = dict(result=((channels, nodes), F32, False))
            if ring:
                ins.update({k: got[k] for k in ("one", "two", "seven", "eight")})
                outs["grads"] = ((top + 1, channels, every), F32, False)
            got = call(make_last(step, scale, ring), ins, outs)
            break
        ins.update(pick)
        outs = state_outs(chains)
        if step <= 2:
            ins["fpart"] = inside["fpart"]
            outs["fboth"] = ((2 * channels, nodes), BF16, True)
        if ring and step == 3:
            ins.update(feat_t=feat_t, **{f"grad{k}": grads[k] for k in range(3)})
            outs.update(one=((4 * channels, every // 2), F32, True), third=chunk)
        sent = following + (1 if step == 1 else 0)
        sends = messages(sent * channels, step + 1)
        ready = {}
        if step in QUICK:
            told = dict(picked=inside["picked"], **through, **halos)
            if step == 1:
                told["back"] = inside["back"]
            if ring and step >= 4:
                told["one"] = got["one"]
                if step < 7:
                    sends["one"] = ((4 * channels, every // 2), F32, True)
                else:
                    ready["one"] = got["one"]
                sends["two"] = ((3 * channels, every // 2), F32, True)
                if step >= 5:
                    told["two"] = got["two"]
                    sends["seven"] = chunk
                if step >= 6:
                    told["seven"] = got["seven"]
                    sends["eight"] = chunk
                if step in (4, 5, 6):
                    told.update({k: back[k] for k in ("g_through_high", "g_through_low")})
                if step == 4:
                    told.update(grad2=grads[2], **{k: x for k, x in back.items() if k in BESIDE})
                    sends["fourth"] = chunk
                if step == 5:
                    told.update(base=inside["base"], third=third)
                if step == 6:
                    told.update(base=inside["base"], fourth=fourth)
                if step == 7:
                    told["eight"] = got["eight"]
            ready.update(call(make_quick(step, chains, following, ring), told, sends))
        else:
            outs.update(sends)
        before = got["state"]
        weight = 2 * chains * channels * nodes * nodes * 3 if step in QUICK else 0
        got = call(make_outer(step, chains, following, ring and step == 3), ins, outs, flops=weight)
        got.update(ready)
        if ring and step == 3:
            third = got["third"]
        if ring and step == 4:
            fourth = got["fourth"]
        boths[step] = got["both"]
    if ring:
        return got["result"], jnp.swapaxes(got["grads"], 1, 2)

    def rest(i, o):
        for k in range(3):
            o.out[k] = getattr(i, f"grad{k}")[...]
        o.out[5] = i.fifth[...]
        for k in range(3, 7):
            ref = getattr(i, f"both{k}")
            state = ref[channels : 2 * channels], ref[3 * channels :]
            if k <= 4:
                o.out[k] = correlate(*state, i.feat_t[...])
            if k >= 4:
                o.out[k + 2] = 2.0 * correlate(*state, i.g_high[...], i.g_low[...]) - o.out[k - 2]

    total = call(
        rest,
        dict(
            feat_t=feat_t,
            fifth=back["fifth"],
            g_high=back["g_high"],
            g_low=back["g_low"],
            **{f"grad{k}": grads[k] for k in range(3)},
            **{f"both{k}": boths[k] for k in range(3, 7)},
        ),
        dict(out=((top + 1, 2 * channels, every // 2), F32, True)),
    )["out"]
    total = lax.psum(total, "dom").reshape(top + 1, 2, channels, every // 2)
    return got["result"], total.transpose(0, 1, 3, 2).reshape(top + 1, every, channels) * scale


def solution(mesh):
    placed = (
        P("chan", "dom"),
        P("chan", "dom"),
        P(None, "chan", None),
        P("dom", None, None),
        P("dom", None, None),
        P("dom", None, None),
    )
    return jax.shard_map(
        local,
        mesh=mesh,
        in_specs=placed,
        out_specs=(P("chan", "dom"), P(None, None, "chan")),
        check_vma=False,
    )
```

```python
import types

import jax
import jax.numpy as jnp
from jax import lax
from jax.experimental import pallas as pl
from jax.experimental.pallas import tpu as pltpu
from jax.sharding import PartitionSpec as P

F32, BF16 = jnp.float32, jnp.bfloat16
SLOTS = 4
WIDE = 256
MIB = 1 << 20
RING = 8
QUICK = (1, 2, 4, 5, 6, 7)
BESIDE = ("base4", "base6", "fifth", "f_through_high", "f_through_low")
KINDS = (2, 0, 3, 1)


def dot(a, b, contract=(1, 0)):
    return lax.dot_general(
        a, b, (((contract[0],), (contract[1],)), ((), ())), preferred_element_type=F32
    )


def halves(x):
    high = x.astype(BF16)
    return high, (x - high.astype(F32)).astype(BF16)


def call(body, ins, outs, scratch=(), flops=0):
    specs, operands = [], []
    for value in ins.values():
        x, place = value if isinstance(value, tuple) else (value, "vmem")
        if place:
            x = pltpu.with_memory_space_constraint(x, pltpu.VMEM if place == "vmem" else pltpu.HBM)
        specs.append(pl.BlockSpec(memory_space={"smem": pltpu.SMEM, "hbm": pltpu.HBM}.get(place, pltpu.VMEM)))
        operands.append(x)
    shapes = [
        pltpu.VMEM(shape, dtype) if kept else jax.ShapeDtypeStruct(shape, dtype)
        for shape, dtype, kept in outs.values()
    ]

    def kernel(*refs):
        n, m = len(ins), len(outs)
        i = types.SimpleNamespace(**dict(zip(ins, refs[:n])))
        o = types.SimpleNamespace(**dict(zip(outs, refs[n : n + m])))
        body(i, o, *refs[n + m :])

    got = pl.pallas_call(
        kernel,
        out_shape=shapes,
        in_specs=specs,
        out_specs=[pl.BlockSpec(memory_space=pltpu.VMEM)] * len(outs),
        scratch_shapes=list(scratch),
        compiler_params=pltpu.CompilerParams(vmem_limit_bytes=32 * MIB),
        cost_estimate=pl.CostEstimate(flops=flops, bytes_accessed=MIB, transcendentals=0),
    )(*operands)
    return dict(zip(outs, got))


def exchange(blocks):
    size = lax.axis_size("dom")
    pairs = [[], [], [], []]
    for p in range(size):
        odd, far = p % 2, (p // 2) % 2
        pairs[0].append((p, (p + 1) % size if odd else (p - 1) % size))
        pairs[1].append((p, (p - 1) % size if odd else (p + 1) % size))
        pairs[2].append((p, (p - 2) % size if far else (p + 2) % size))
        pairs[3].append((p, (p + 2) % size if far else (p - 2) % size))
    return [lax.ppermute(block, "dom", pairs[kind]) for block, kind in zip(blocks, KINDS)]


def sides():
    me = lax.axis_index("dom")
    return lax.rem(me, 2), lax.rem(lax.div(me, 2), 2)


def pairs_of_two(forth, back):
    far = sides()[1] == 1
    return {2: jnp.where(far, back, forth), 3: jnp.where(far, forth, back)}


def from_pairs(got):
    far = sides()[1] == 1
    return jnp.where(far, got[2], got[3]), jnp.where(far, got[3], got[2])


LAYOUT = {
    4: {1: (256,)},
    5: {1: (192,), 2: (128,), 3: (128,)},
    6: {1: (128,), 2: (128, 96), 3: (128, 96)},
    7: {1: (128,), 2: (96, 64, 128), 3: (96, 64, 128)},
    8: {0: (128,), 1: (192, 256), 2: (64, 128), 3: (64, 128)},
}


def carried(i, step, base, kind, index):
    rows = LAYOUT[step][kind]
    start = base + sum(rows[:index])
    return getattr(i, f"halo{KINDS.index(kind)}")[start : start + rows[index], :]


def parted(group):
    odd = sides()[0] == 1
    half = group.shape[0] // 2
    return jnp.where(odd, group[half:], group[:half]), jnp.where(odd, group[:half], group[half:])


def joined(own, other):
    odd = sides()[0] == 1
    return jnp.concatenate([jnp.where(odd, other, own), jnp.where(odd, own, other)], axis=0)


def added(rows, first, second):
    half = rows.shape[0] // 2
    return jnp.concatenate([rows[:half] + first, rows[half:] + second], axis=0)


def hop(block, bit):
    return lax.ppermute(block, "chan", [(c, c ^ bit) for c in range(lax.axis_size("chan"))])


def gather(blocks, marker):
    bit = lax.axis_size("chan") // 4
    blocks = [*lax.optimization_barrier((*blocks, marker))[:2]]
    while bit:
        blocks = blocks + [hop(block, bit) for block in blocks]
        bit //= 2
    return blocks


def collect(blocks, out):
    masks, bit = [0], len(blocks) // 2
    while bit:
        masks = masks + [m ^ bit for m in masks]
        bit //= 2
    place = lax.axis_index("chan")
    for mask, block in zip(masks, blocks):
        rows = block.shape[0]
        out[pl.ds(pl.multiple_of((place ^ mask) * rows, rows), rows), :] = block


def stack(i, o, sems):
    local = i.upper.shape[0]
    copies = [
        pltpu.make_async_copy(i.upper, o.both.at[pl.ds(0, local)], sems.at[0]),
        pltpu.make_async_copy(i.lower, o.both.at[pl.ds(local, local)], sems.at[1]),
    ]
    for copy in copies:
        copy.start()
    for copy in copies:
        copy.wait()


def prepare(i, o, total, held, sems):
    count, tile, _ = held.shape
    nodes = o.pick.shape[0]
    blocks = nodes // tile
    per_row = count // blocks
    copies = [
        pltpu.make_async_copy(
            i.tiles.at[pl.ds(r * per_row, per_row)], held.at[pl.ds(r * per_row, per_row)], sems.at[r]
        )
        for r in range(blocks)
    ]
    for copy in copies:
        copy.start()
    odd, far = sides()
    rows = lax.broadcasted_iota(jnp.int32, (nodes, tile), 0)
    lists = i.lists[0]
    near = jnp.where(odd == 1, lists[0:1], lists[1:2]), jnp.where(odd == 1, lists[1:2], lists[0:1])
    order = [*near, *pairs_of_two(lists[2:3], lists[3:4]).values()]
    for k, kind in enumerate(KINDS):
        hit = rows == jnp.broadcast_to(order[kind], rows.shape)
        o.pick[:, k * tile : (k + 1) * tile] = hit.astype(F32).astype(BF16)
    total[...] = jnp.zeros_like(total)
    for r, copy in enumerate(copies):
        copy.wait()
        here = slice(r * tile, (r + 1) * tile)
        for j in range(per_row):
            col = i.cols[0, r, j]
            slot = col - blocks
            kind = jnp.where(slot < 2, slot ^ odd, slot ^ (1 - far))
            place = sum(jnp.where(kind == k, KINDS.index(k), 0) for k in range(SLOTS))
            col = jnp.where(slot >= 0, blocks + place, col)
            at = pl.ds(pl.multiple_of(col * tile, tile), tile)
            total[at, here] += held[r * per_row + j]
        high, low = halves(total[:, here])
        o.high[:, here] = high
        o.low[:, here] = low
    channels = i.stacked.shape[0] // 2
    feat = i.stacked[channels:]
    o.back[...] = dot(feat, o.high[nodes:, :], (1, 1)) + dot(feat, o.low[nodes:, :], (1, 1))
    o.sent[...] = dot(i.stacked[:channels], o.pick[...])


def summed(both):
    rows = both.shape[0] // 2
    return both[:rows] + both[rows:]


def write_sends(o, parts, extra=None):
    for k, kind in enumerate(KINDS):
        ref = getattr(o, f"send{k}")
        at, width = 0, ref.shape[1]
        for part in parts:
            ref[at : at + part.shape[0], :] = part[:, k * width : (k + 1) * width]
            at += part.shape[0]
        for block in (extra or {}).get(kind, ()):
            ref[at : at + block.shape[0], :] = block
            at += block.shape[0]


def back_halo(both, i, nodes):
    rows = both.shape[0] // 2
    return summed(dot(both, i.high[nodes:, :], (1, 1))) + dot(both[:rows], i.low[nodes:, :], (1, 1))


def correlate(u_high, u_low, g_high, g_low=None):
    if u_low is None:
        total = dot(u_high, g_high)
    else:
        total = summed(dot(jnp.concatenate([u_high, u_low], axis=0), g_high))
    if g_low is not None:
        total += dot(u_high, g_low)
    half = total.shape[1] // 2
    return jnp.concatenate([total[:, :half], total[:, half:]], axis=0)


def transposed(x):
    return x.astype(F32).T.astype(BF16)


def begin(i, o):
    local = i.weight.shape[0]
    own = i.stacked[:local]
    collect([own] + [ref[:local, :] for name, ref in vars(i).items() if name.startswith("block")], o.gathered)
    first = dot(i.weight[...], o.gathered[...])
    o.state[:local] = first
    o.state[local:] = own.astype(F32)
    high, low = halves(first)
    o.both[:local] = high
    o.both[local : 2 * local] = own
    o.both[2 * local : 3 * local] = low
    o.both[3 * local :] = jnp.zeros_like(low)
    parts = summed(dot(jnp.concatenate([high, low], axis=0), i.pick[...])), i.sent[...], i.back[...]
    write_sends(o, parts)


def make_inner(step, top, chains):
    def inner(i, o):
        rows, nodes = o.part.shape
        local = rows // chains
        scale = 1.0 if step == top else 2.0
        width = i.both.shape[0] // 2
        lhs = jnp.concatenate([i.both[:rows], i.both[width : width + rows]], axis=0)
        for start in range(0, nodes, WIDE):
            here = slice(start, start + WIDE)
            total = summed(dot(lhs, i.high[:nodes, here])) + dot(lhs[:rows], i.low[:nodes, here])
            mixed = dot(i.weight[...], i.gathered[:, here])
            value = scale * total[:local] + mixed
            if step > 1:
                value -= i.before[:local, here]
            o.part[:local, here] = value
            if chains > 1:
                value = (1.0 if step == 1 else 2.0) * total[local:]
                if step > 1:
                    value -= i.before[local:, here]
                o.part[local:, here] = value
        if step == 1:
            feat = i.stacked[local:]
            for start in range(0, nodes, WIDE):
                here = slice(start, start + WIDE)
                o.fpart[:, here] = dot(feat, i.high[here, :], (1, 1)) + dot(feat, i.low[here, :], (1, 1))
        if step == 2:
            for start in range(0, nodes, WIDE):
                here = slice(start, start + WIDE)
                total = summed(dot(i.fboth[...], i.high[here, :], (1, 1)))
                total += dot(i.fboth[:local], i.low[here, :], (1, 1))
                o.fpart[:, here] = 2.0 * total - i.stacked[local:, here].astype(F32)
        if step in QUICK:
            o.picked[...] = summed(dot(jnp.concatenate(halves(o.part[...]), axis=0), i.pick[...]))
        if step == 1:
            o.back[...] = back_halo(jnp.concatenate(halves(o.fpart[...]), axis=0), i, nodes)
        if step in (5, 6):
            o.base[...] = correlate(*halves(o.part[local:, :]), i.g_high[...], i.g_low[...])

    return inner


def make_quick(step, chains, following, ring):
    def quick(i, o):
        rows = i.picked.shape[0]
        local = rows // chains
        both = split_halos(i, rows)
        total = summed(dot(both, i.through_high[...])) + dot(both[:rows], i.through_low[...])
        if step == 1:
            total = jnp.concatenate([2.0 * total[:local], total[local:]], axis=0)
        else:
            total = 2.0 * total
        parts = [(i.picked[...] + total)[: following * local]]
        if step == 1:
            got = [getattr(i, f"halo{k}")[rows : rows + local, :] for k in range(SLOTS)]
            back = jnp.concatenate(halves(jnp.concatenate(got, axis=1)), axis=0)
            total = summed(dot(back, i.through_high[...], (1, 1)))
            parts.append(i.back[...] + total + dot(back[:local], i.through_low[...], (1, 1)))
        if not ring or step <= 2:
            write_sends(o, parts)
            return
        if chains > 1:
            arrived = both[local : 2 * local], both[rows + local :]

        def got(kind, index):
            return carried(i, step, rows, kind, index)

        def newest(base, old):
            return 2.0 * (base + 2.0 * correlate(*arrived, i.g_through_high[...], i.g_through_low[...])) - old

        if step == 4:
            one = i.one[...] + got(1, 0)
            half = one.shape[0] // 2
            o.one[...] = one
            o.fourth[...] = i.base4[...] + 2.0 * correlate(*arrived, i.f_through_high[...], i.f_through_low[...])
            group = [o.fourth[...], i.fifth[...], newest(i.base6[...], i.grad2[...])]
            o.two[...], away = parted(jnp.concatenate(group, axis=0))
            extra = {1: [away], 2: [one[:half]], 3: [one[half:]]}
        if step == 5:
            one = added(i.one[...], got(2, 0), got(3, 0))
            two = i.two[...] + got(1, 0)
            half, quarter = one.shape[0] // 2, two.shape[0] // 2
            o.one[...], o.two[...] = one, two
            o.seven[...] = newest(i.base[...], i.third[...])
            extra = {1: [o.seven[...]], 2: [one[half:], two[:quarter]], 3: [one[:half], two[quarter:]]}
        if step == 6:
            one = added(i.one[...], got(3, 0), got(2, 0))
            two = added(i.two[...], got(2, 1), got(3, 1))
            seven = i.seven[...] + got(1, 0)
            eight = newest(i.base[...], i.fourth[...])
            half, quarter = seven.shape[0] // 2, two.shape[0] // 2
            o.one[...], o.two[...], o.seven[...], o.eight[...] = one, two, seven, eight
            extra = {
                1: [eight],
                2: [two[quarter:], seven[:half], eight],
                3: [two[:quarter], seven[half:], eight],
            }
        if step == 7:
            two = added(i.two[...], got(3, 0), got(2, 0))
            seven = added(i.seven[...], got(2, 1), got(3, 1))
            near, (m2, p2) = got(1, 0), from_pairs({2: got(2, 2), 3: got(3, 2)})
            half = seven.shape[0] // 2
            o.two[...], o.seven[...] = two, seven
            o.eight[...] = i.eight[...] + near + m2 + p2
            on = pairs_of_two(near, near + p2)
            across = jnp.where(sides()[0] == 1, m2, p2)
            extra = {0: [across], 1: [two, i.one[...]], 2: [seven[half:], on[2]], 3: [seven[:half], on[3]]}
        write_sends(o, parts, extra)

    return quick


def halo_product(i, lhs, rows, here, nodes):
    return summed(dot(lhs, i.high[nodes:, here])) + dot(lhs[:rows], i.low[nodes:, here])


def split_halos(i, rows):
    got = [getattr(i, f"halo{k}") for k in range(SLOTS)]
    high, low = halves(jnp.concatenate([ref[:rows, :] for ref in got], axis=1))
    return jnp.concatenate([high, low], axis=0)


def make_outer(step, chains, following, ring):
    def outer(i, o):
        rows, nodes = i.part.shape
        local = rows // chains
        lhs = split_halos(i, rows)
        for start in range(0, nodes, WIDE):
            here = slice(start, start + WIDE)
            total = halo_product(i, lhs, rows, here, nodes)
            for chain in range(chains):
                mine = slice(chain * local, (chain + 1) * local)
                state = i.part[mine, here] + (1.0 if chain == 1 and step == 1 else 2.0) * total[mine]
                o.state[mine, here] = state
                high, low = halves(state)
                o.both[mine, here] = high
                o.both[rows + chain * local : rows + (chain + 1) * local, here] = low
        live = following * local
        moving = o.both[...]
        if following < chains:
            moving = jnp.concatenate([o.both[:live], o.both[rows : rows + live]], axis=0)
        if step not in QUICK:
            parts = [summed(dot(moving, i.pick[...]))]
        if step <= 2:
            got = [getattr(i, f"halo{k}")[rows : rows + local, :] for k in range(SLOTS)]
            high, low = halves(jnp.concatenate(got, axis=1))
            lhs = jnp.concatenate([high, low], axis=0)
            for start in range(0, nodes, WIDE):
                here = slice(start, start + WIDE)
                total = summed(dot(lhs, i.pick[here, :], (1, 1)))
                high, low = halves(i.fpart[:, here] + (1.0 if step == 1 else 2.0) * total)
                o.fboth[:local, here] = high
                o.fboth[local:, here] = low
        if step in QUICK:
            return
        extra = None
        if ring:
            if chains > 1:
                state = o.both[local : 2 * local], o.both[rows + local : rows + 2 * local]

            def got(kind, index):
                return carried(i, step, rows, kind, index)

            def newest(old):
                return 2.0 * correlate(*state, i.g_high[...], i.g_low[...]) - old

            if step == 3:
                o.third[...] = correlate(*state, i.feat_t[...])
                group = jnp.concatenate([i.grad0[...], i.grad1[...], i.grad2[...], o.third[...]], axis=0)
                o.one[...], away = parted(group)
                extra = {1: [away]}
        write_sends(o, parts, extra)

    return outer


def settle(i, o):
    blocks = [ref for name, ref in vars(i).items() if name.startswith("block")]
    rows = blocks[0].shape[0] // 2
    for half, out in ((slice(0, rows), o.g_high), (slice(rows, None), o.g_low)):
        collect([ref[half, :] for ref in blocks], o.whole)
        out[...] = transposed(o.whole[...])
    local = i.both.shape[0] // 4
    o.fifth[...] = 2.0 * correlate(
        i.both[local : 2 * local], i.both[3 * local :], o.g_high[...], o.g_low[...]
    ) - i.grad1[...]
    nodes = i.part.shape[1]
    part = halves(i.part[local:, :])
    o.base4[...] = correlate(*part, i.feat_t[...])
    o.base6[...] = correlate(*part, o.g_high[...], o.g_low[...])
    high, low = i.high[nodes:, :], i.low[nodes:, :]
    product = dot(high, i.feat_t[...]) + dot(low, i.feat_t[...])
    o.f_through_high[...], o.f_through_low[...] = halves(product)
    product = dot(high, o.g_high[...]) + dot(high, o.g_low[...]) + dot(low, o.g_high[...])
    o.g_through_high[...], o.g_through_low[...] = halves(product)


def make_last(step, scale, ring):
    def last(i, o):
        rows, nodes = i.part.shape
        lhs = split_halos(i, rows)
        for start in range(0, nodes, WIDE):
            here = slice(start, start + WIDE)
            o.result[:, here] = i.part[:, here] + halo_product(i, lhs, rows, here, nodes)
        if not ring:
            return

        def got(kind, index):
            return carried(i, step, rows, kind, index)

        def put(k, chunk):
            size = chunk.shape[0] // 2
            o.grads[k] = scale * jnp.concatenate([chunk[:size], chunk[size:]], axis=1)

        size = i.eight.shape[0]
        one, two = joined(i.one[...], got(1, 1)), joined(i.two[...], got(1, 0))
        for k in range(4):
            put(k, one[k * size : (k + 1) * size])
        for k in range(3):
            put(4 + k, two[k * size : (k + 1) * size])
        put(7, added(i.seven[...], got(3, 0), got(2, 0)))
        m2, p2 = from_pairs({2: got(2, 1), 3: got(3, 1)})
        put(8, i.eight[...] + m2 + p2 + got(0, 0))

    return last


def local(features, cotangent, weights, tile_values, tile_cols, send_list):
    top = weights.shape[0] - 1
    channels, nodes = features.shape
    tile = tile_values.shape[-1]
    every = weights.shape[2]
    wide = nodes + SLOTS * tile
    parts = lax.axis_size("dom")
    ring = parts == RING and top == RING and channels * every == tile * tile and tile == 128
    scale = float(parts * nodes) ** (-0.5)
    sent_shape = ((channels, SLOTS * tile), F32, True)
    whole = ((every, nodes), BF16, True)
    turned = ((nodes, every), BF16, True)
    chunk = ((2 * channels, every // 2), F32, True)
    along = ((SLOTS * tile, every), BF16, True)

    stacked = call(
        stack,
        dict(upper=(cotangent, "hbm"), lower=(features, "hbm")),
        dict(both=((2 * channels, nodes), BF16, True)),
        [pltpu.SemaphoreType.DMA((2,))],
    )["both"]
    ready = call(
        prepare,
        dict(
            cols=(tile_cols, "smem"),
            lists=(send_list, "load"),
            tiles=(tile_values, "hbm"),
            stacked=stacked,
        ),
        dict(
            high=((wide, nodes), BF16, True),
            low=((wide, nodes), BF16, True),
            pick=((nodes, SLOTS * tile), BF16, True),
            back=sent_shape,
            sent=sent_shape,
        ),
        [
            pltpu.VMEM((wide, nodes), F32),
            pltpu.VMEM(tile_values.shape, F32),
            pltpu.SemaphoreType.DMA((nodes // tile,)),
        ],
        flops=10**10,
    )
    matrix = dict(high=ready["high"], low=ready["low"])
    pick = dict(pick=ready["pick"])
    blocks = gather((stacked, hop(stacked, lax.axis_size("chan") // 2)), ready["back"])

    def messages(rows, step):
        extra = LAYOUT.get(step, {}) if ring else {}
        return {
            f"send{k}": ((rows + sum(extra.get(kind, ())), tile), F32, False) for k, kind in enumerate(KINDS)
        }

    def state_outs(chains):
        rows = chains * channels
        return dict(state=((rows, nodes), F32, True), both=((2 * rows, nodes), BF16, True))

    named = {f"block{k}": (block, "") for k, block in enumerate(blocks[1:])}
    got = call(
        begin,
        dict(
            stacked=stacked,
            weight=(weights[top], ""),
            **pick,
            sent=ready["sent"],
            back=ready["back"],
            **named,
        ),
        dict(gathered=whole, **state_outs(2), **messages(3 * channels, 1)),
    )
    gathered = got["gathered"]

    def pass_through(i, o):
        for matrix, out in ((i.high, o.through_high), (i.low, o.through_low)):
            out[...] = dot(matrix[nodes:, :], i.pick[...]).astype(BF16)

    through = ((SLOTS * tile, SLOTS * tile), BF16, True)
    through = call(pass_through, dict(**matrix, **pick), dict(through_high=through, through_low=through))

    def opening(i, o):
        rows = [ref[channels:, :] for name, ref in vars(i).items() if name.startswith("block")]
        collect([i.stacked[channels:]] + rows, o.whole)
        o.feat_t[...] = transposed(o.whole[...])
        o.grad0[...] = correlate(i.stacked[:channels], None, o.feat_t[...])
        for ref, out in ((i.both1, o.grad1), (i.both2, o.grad2)):
            out[...] = correlate(ref[channels : 2 * channels], ref[3 * channels :], o.feat_t[...])

    before, boths, grads, back = None, {}, {}, None
    for step in range(1, top + 1):
        chains = 2 if step <= top - 2 else 1
        following = 2 if step + 1 <= top - 2 else 1
        halos = {f"halo{k}": (x, "") for k, x in enumerate(exchange([got[f"send{k}"] for k in range(SLOTS)]))}
        ins = dict(both=got["both"], weight=(weights[top - step], ""), gathered=gathered, **matrix)
        outs = dict(part=((chains * channels, nodes), F32, True))
        if step > 1:
            ins["before"] = before
        if step in QUICK:
            ins.update(pick)
            outs["picked"] = ((chains * channels, SLOTS * tile), F32, True)
        if step in (5, 6):
            ins.update(g_high=back["g_high"], g_low=back["g_low"])
            outs["base"] = chunk
        if step == 1:
            outs["back"] = sent_shape
        if step <= 2:
            ins["stacked"] = stacked
            outs["fpart"] = ((channels, nodes), F32, True)
        if step == 2:
            ins["fboth"] = got["fboth"]
        inside = call(
            make_inner(step, top, chains), ins, outs, flops=2 * chains * channels * nodes * nodes * 3
        )
        part = inside["part"]
        if step == 3:
            opened = call(
                opening,
                dict(stacked=stacked, **named, both1=boths[1], both2=boths[2]),
                dict(whole=whole, feat_t=turned, **{f"grad{k}": chunk for k in range(3)}),
            )
            feat_t, grads = opened["feat_t"], {k: opened[f"grad{k}"] for k in range(3)}
        if step == 3:
            back_blocks = got["fboth"], hop(got["fboth"], lax.axis_size("chan") // 2)
        if step == 4:
            back = call(
                settle,
                dict(
                    **{f"block{k}": (x, "") for k, x in enumerate(gather(back_blocks, got["send0"]))}, both=boths[3],
                    grad1=grads[1],
                    part=part,
                    feat_t=feat_t,
                    **matrix,
                ),
                dict(
                    g_high=turned, g_low=turned, whole=whole, fifth=chunk, base4=chunk, base6=chunk,
                    **{f"{name}_through_{half}": along for name in "fg" for half in ("high", "low")},
                ),
            )
        ins = dict(part=part, **matrix, **halos)
        if step == top:
            outs = dict(result=((channels, nodes), F32, False))
            if ring:
                ins.update({k: got[k] for k in ("one", "two", "seven", "eight")})
                outs["grads"] = ((top + 1, channels, every), F32, False)
            got = call(make_last(step, scale, ring), ins, outs)
            break
        ins.update(pick)
        outs = state_outs(chains)
        if step <= 2:
            ins["fpart"] = inside["fpart"]
            outs["fboth"] = ((2 * channels, nodes), BF16, True)
        if ring and step == 3:
            ins.update(feat_t=feat_t, **{f"grad{k}": grads[k] for k in range(3)})
            outs.update(one=((4 * channels, every // 2), F32, True), third=chunk)
        sent = following + (1 if step == 1 else 0)
        sends = messages(sent * channels, step + 1)
        ready = {}
        if step in QUICK:
            told = dict(picked=inside["picked"], **through, **halos)
            if step == 1:
                told["back"] = inside["back"]
            if ring and step >= 4:
                told["one"] = got["one"]
                if step < 7:
                    sends["one"] = ((4 * channels, every // 2), F32, True)
                else:
                    ready["one"] = got["one"]
                sends["two"] = ((3 * channels, every // 2), F32, True)
                if step >= 5:
                    told["two"] = got["two"]
                    sends["seven"] = chunk
                if step >= 6:
                    told["seven"] = got["seven"]
                    sends["eight"] = chunk
                if step in (4, 5, 6):
                    told.update({k: back[k] for k in ("g_through_high", "g_through_low")})
                if step == 4:
                    told.update(grad2=grads[2], **{k: x for k, x in back.items() if k in BESIDE})
                    sends["fourth"] = chunk
                if step == 5:
                    told.update(base=inside["base"], third=third)
                if step == 6:
                    told.update(base=inside["base"], fourth=fourth)
                if step == 7:
                    told["eight"] = got["eight"]
            ready.update(call(make_quick(step, chains, following, ring), told, sends))
        else:
            outs.update(sends)
        before = got["state"]
        weight = 2 * chains * channels * nodes * nodes * 3 if step in QUICK else 0
        got = call(make_outer(step, chains, following, ring and step == 3), ins, outs, flops=weight)
        got.update(ready)
        if ring and step == 3:
            third = got["third"]
        if ring and step == 4:
            fourth = got["fourth"]
        boths[step] = got["both"]
    if ring:
        return got["result"], jnp.swapaxes(got["grads"], 1, 2)

    def rest(i, o):
        for k in range(3):
            o.out[k] = getattr(i, f"grad{k}")[...]
        o.out[5] = i.fifth[...]
        for k in range(3, 7):
            ref = getattr(i, f"both{k}")
            state = ref[channels : 2 * channels], ref[3 * channels :]
            if k <= 4:
                o.out[k] = correlate(*state, i.feat_t[...])
            if k >= 4:
                o.out[k + 2] = 2.0 * correlate(*state, i.g_high[...], i.g_low[...]) - o.out[k - 2]

    total = call(
        rest,
        dict(
            feat_t=feat_t,
            fifth=back["fifth"],
            g_high=back["g_high"],
            g_low=back["g_low"],
            **{f"grad{k}": grads[k] for k in range(3)},
            **{f"both{k}": boths[k] for k in range(3, 7)},
        ),
        dict(out=((top + 1, 2 * channels, every // 2), F32, True)),
    )["out"]
    total = lax.psum(total, "dom").reshape(top + 1, 2, channels, every // 2)
    return got["result"], total.transpose(0, 1, 3, 2).reshape(top + 1, every, channels) * scale


def solution(mesh):
    placed = (
        P("chan", "dom"),
        P("chan", "dom"),
        P(None, "chan", None),
        P("dom", None, None),
        P("dom", None, None),
        P("dom", None, None),
    )
    return jax.shard_map(
        local,
        mesh=mesh,
        in_specs=placed,
        out_specs=(P("chan", "dom"), P(None, None, "chan")),
        check_vma=False,
    )
```

```python
import types

import jax
import jax.numpy as jnp
from jax import lax
from jax.experimental import pallas as pl
from jax.experimental.pallas import tpu as pltpu
from jax.sharding import PartitionSpec as P

F32, BF16 = jnp.float32, jnp.bfloat16
SLOTS = 4
WIDE = 256
MIB = 1 << 20
RING = 8
QUICK = (1, 2, 4, 5, 6, 7)
BESIDE = ("base4", "base6", "fifth", "f_through_high", "f_through_low")
KINDS = (2, 0, 3, 1)


def dot(a, b, contract=(1, 0)):
    return lax.dot_general(
        a, b, (((contract[0],), (contract[1],)), ((), ())), preferred_element_type=F32
    )


def halves(x):
    high = x.astype(BF16)
    return high, (x - high.astype(F32)).astype(BF16)


def call(body, ins, outs, scratch=(), flops=0):
    specs, operands = [], []
    for value in ins.values():
        x, place = value if isinstance(value, tuple) else (value, "vmem")
        if place:
            x = pltpu.with_memory_space_constraint(x, pltpu.VMEM if place == "vmem" else pltpu.HBM)
        specs.append(pl.BlockSpec(memory_space={"smem": pltpu.SMEM, "hbm": pltpu.HBM}.get(place, pltpu.VMEM)))
        operands.append(x)
    shapes = [
        pltpu.VMEM(shape, dtype) if kept else jax.ShapeDtypeStruct(shape, dtype)
        for shape, dtype, kept in outs.values()
    ]

    def kernel(*refs):
        n, m = len(ins), len(outs)
        i = types.SimpleNamespace(**dict(zip(ins, refs[:n])))
        o = types.SimpleNamespace(**dict(zip(outs, refs[n : n + m])))
        body(i, o, *refs[n + m :])

    got = pl.pallas_call(
        kernel,
        out_shape=shapes,
        in_specs=specs,
        out_specs=[pl.BlockSpec(memory_space=pltpu.VMEM)] * len(outs),
        scratch_shapes=list(scratch),
        compiler_params=pltpu.CompilerParams(vmem_limit_bytes=32 * MIB),
        cost_estimate=pl.CostEstimate(flops=flops, bytes_accessed=MIB, transcendentals=0),
    )(*operands)
    return dict(zip(outs, got))


def exchange(blocks):
    size = lax.axis_size("dom")
    pairs = [[], [], [], []]
    for p in range(size):
        odd, far = p % 2, (p // 2) % 2
        pairs[0].append((p, (p + 1) % size if odd else (p - 1) % size))
        pairs[1].append((p, (p - 1) % size if odd else (p + 1) % size))
        pairs[2].append((p, (p - 2) % size if far else (p + 2) % size))
        pairs[3].append((p, (p + 2) % size if far else (p - 2) % size))
    return [lax.ppermute(block, "dom", pairs[kind]) for block, kind in zip(blocks, KINDS)]


def sides():
    me = lax.axis_index("dom")
    return lax.rem(me, 2), lax.rem(lax.div(me, 2), 2)


def pairs_of_two(forth, back):
    far = sides()[1] == 1
    return {2: jnp.where(far, back, forth), 3: jnp.where(far, forth, back)}


def from_pairs(got):
    far = sides()[1] == 1
    return jnp.where(far, got[2], got[3]), jnp.where(far, got[3], got[2])


LAYOUT = {
    4: {1: (256,)},
    5: {1: (192,), 2: (128,), 3: (128,)},
    6: {1: (128,), 2: (128, 96), 3: (128, 96)},
    7: {1: (128,), 2: (96, 64, 128), 3: (96, 64, 128)},
    8: {0: (128,), 1: (192, 256), 2: (64, 128), 3: (64, 128)},
}


def carried(i, step, base, kind, index):
    rows = LAYOUT[step][kind]
    start = base + sum(rows[:index])
    return getattr(i, f"halo{KINDS.index(kind)}")[start : start + rows[index], :]


def parted(group):
    odd = sides()[0] == 1
    half = group.shape[0] // 2
    return jnp.where(odd, group[half:], group[:half]), jnp.where(odd, group[:half], group[half:])


def joined(own, other):
    odd = sides()[0] == 1
    return jnp.concatenate([jnp.where(odd, other, own), jnp.where(odd, own, other)], axis=0)


def added(rows, first, second):
    half = rows.shape[0] // 2
    return jnp.concatenate([rows[:half] + first, rows[half:] + second], axis=0)


def hop(block, bit):
    return lax.ppermute(block, "chan", [(c, c ^ bit) for c in range(lax.axis_size("chan"))])


def gather(blocks, marker):
    bit = lax.axis_size("chan") // 4
    blocks = [*lax.optimization_barrier((*blocks, marker))[:2]]
    while bit:
        blocks = blocks + [hop(block, bit) for block in blocks]
        bit //= 2
    return blocks


def collect(blocks, out):
    masks, bit = [0], len(blocks) // 2
    while bit:
        masks = masks + [m ^ bit for m in masks]
        bit //= 2
    place = lax.axis_index("chan")
    for mask, block in zip(masks, blocks):
        rows = block.shape[0]
        out[pl.ds(pl.multiple_of((place ^ mask) * rows, rows), rows), :] = block


def stack(i, o, sems):
    local = i.upper.shape[0]
    copies = [
        pltpu.make_async_copy(i.upper, o.both.at[pl.ds(0, local)], sems.at[0]),
        pltpu.make_async_copy(i.lower, o.both.at[pl.ds(local, local)], sems.at[1]),
    ]
    for copy in copies:
        copy.start()
    for copy in copies:
        copy.wait()


def prepare(i, o, total, held, sems):
    count, tile, _ = held.shape
    nodes = o.pick.shape[0]
    blocks = nodes // tile
    per_row = count // blocks
    copies = [
        pltpu.make_async_copy(
            i.tiles.at[pl.ds(r * per_row, per_row)], held.at[pl.ds(r * per_row, per_row)], sems.at[r]
        )
        for r in range(blocks)
    ]
    for copy in copies:
        copy.start()
    odd, far = sides()
    rows = lax.broadcasted_iota(jnp.int32, (nodes, tile), 0)
    lists = i.lists[0]
    near = jnp.where(odd == 1, lists[0:1], lists[1:2]), jnp.where(odd == 1, lists[1:2], lists[0:1])
    order = [*near, *pairs_of_two(lists[2:3], lists[3:4]).values()]
    for k, kind in enumerate(KINDS):
        hit = rows == jnp.broadcast_to(order[kind], rows.shape)
        o.pick[:, k * tile : (k + 1) * tile] = hit.astype(F32).astype(BF16)
    total[...] = jnp.zeros_like(total)
    for r, copy in enumerate(copies):
        copy.wait()
        here = slice(r * tile, (r + 1) * tile)
        for j in range(per_row):
            col = i.cols[0, r, j]
            slot = col - blocks
            kind = jnp.where(slot < 2, slot ^ odd, slot ^ (1 - far))
            place = sum(jnp.where(kind == k, KINDS.index(k), 0) for k in range(SLOTS))
            col = jnp.where(slot >= 0, blocks + place, col)
            at = pl.ds(pl.multiple_of(col * tile, tile), tile)
            total[at, here] += held[r * per_row + j]
        high, low = halves(total[:, here])
        o.high[:, here] = high
        o.low[:, here] = low
    channels = i.stacked.shape[0] // 2
    feat = i.stacked[channels:]
    o.back[...] = dot(feat, o.high[nodes:, :], (1, 1)) + dot(feat, o.low[nodes:, :], (1, 1))
    o.sent[...] = dot(i.stacked[:channels], o.pick[...])


def summed(both):
    rows = both.shape[0] // 2
    return both[:rows] + both[rows:]


def write_sends(o, parts, extra=None):
    for k, kind in enumerate(KINDS):
        ref = getattr(o, f"send{k}")
        at, width = 0, ref.shape[1]
        for part in parts:
            ref[at : at + part.shape[0], :] = part[:, k * width : (k + 1) * width]
            at += part.shape[0]
        for block in (extra or {}).get(kind, ()):
            ref[at : at + block.shape[0], :] = block
            at += block.shape[0]


def back_halo(both, i, nodes):
    rows = both.shape[0] // 2
    return summed(dot(both, i.high[nodes:, :], (1, 1))) + dot(both[:rows], i.low[nodes:, :], (1, 1))


def correlate(u_high, u_low, g_high, g_low=None):
    if u_low is None:
        total = dot(u_high, g_high)
    else:
        total = summed(dot(jnp.concatenate([u_high, u_low], axis=0), g_high))
    if g_low is not None:
        total += dot(u_high, g_low)
    half = total.shape[1] // 2
    return jnp.concatenate([total[:, :half], total[:, half:]], axis=0)


def transposed(x):
    return x.astype(F32).T.astype(BF16)


def begin(i, o):
    local = i.weight.shape[0]
    own = i.stacked[:local]
    collect([own] + [ref[:local, :] for name, ref in vars(i).items() if name.startswith("block")], o.gathered)
    first = dot(i.weight[...], o.gathered[...])
    o.state[:local] = first
    o.state[local:] = own.astype(F32)
    high, low = halves(first)
    o.both[:local] = high
    o.both[local : 2 * local] = own
    o.both[2 * local : 3 * local] = low
    o.both[3 * local :] = jnp.zeros_like(low)
    parts = summed(dot(jnp.concatenate([high, low], axis=0), i.pick[...])), i.sent[...], i.back[...]
    write_sends(o, parts)


def make_inner(step, top, chains):
    def inner(i, o):
        rows, nodes = o.part.shape
        local = rows // chains
        scale = 1.0 if step == top else 2.0
        width = i.both.shape[0] // 2
        lhs = jnp.concatenate([i.both[:rows], i.both[width : width + rows]], axis=0)
        for start in range(0, nodes, WIDE):
            here = slice(start, start + WIDE)
            total = summed(dot(lhs, i.high[:nodes, here])) + dot(lhs[:rows], i.low[:nodes, here])
            mixed = dot(i.weight[...], i.gathered[:, here])
            value = scale * total[:local] + mixed
            if step > 1:
                value -= i.before[:local, here]
            o.part[:local, here] = value
            if chains > 1:
                value = (1.0 if step == 1 else 2.0) * total[local:]
                if step > 1:
                    value -= i.before[local:, here]
                o.part[local:, here] = value
        if step == 1:
            feat = i.stacked[local:]
            for start in range(0, nodes, WIDE):
                here = slice(start, start + WIDE)
                o.fpart[:, here] = dot(feat, i.high[here, :], (1, 1)) + dot(feat, i.low[here, :], (1, 1))
        if step == 2:
            for start in range(0, nodes, WIDE):
                here = slice(start, start + WIDE)
                total = summed(dot(i.fboth[...], i.high[here, :], (1, 1)))
                total += dot(i.fboth[:local], i.low[here, :], (1, 1))
                o.fpart[:, here] = 2.0 * total - i.stacked[local:, here].astype(F32)
        if step in QUICK:
            o.picked[...] = summed(dot(jnp.concatenate(halves(o.part[...]), axis=0), i.pick[...]))
        if step == 1:
            o.back[...] = back_halo(jnp.concatenate(halves(o.fpart[...]), axis=0), i, nodes)
        if step in (5, 6):
            o.base[...] = correlate(*halves(o.part[local:, :]), i.g_high[...], i.g_low[...])

    return inner


def make_quick(step, chains, following, ring):
    def quick(i, o):
        rows = i.picked.shape[0]
        local = rows // chains
        both = split_halos(i, rows)
        total = summed(dot(both, i.through_high[...])) + dot(both[:rows], i.through_low[...])
        if step == 1:
            total = jnp.concatenate([2.0 * total[:local], total[local:]], axis=0)
        else:
            total = 2.0 * total
        parts = [(i.picked[...] + total)[: following * local]]
        if step == 1:
            got = [getattr(i, f"halo{k}")[rows : rows + local, :] for k in range(SLOTS)]
            back = jnp.concatenate(halves(jnp.concatenate(got, axis=1)), axis=0)
            total = summed(dot(back, i.through_high[...], (1, 1)))
            parts.append(i.back[...] + total + dot(back[:local], i.through_low[...], (1, 1)))
        if not ring or step <= 2:
            write_sends(o, parts)
            return
        if chains > 1:
            arrived = both[local : 2 * local], both[rows + local :]

        def got(kind, index):
            return carried(i, step, rows, kind, index)

        def newest(base, old):
            return 2.0 * (base + 2.0 * correlate(*arrived, i.g_through_high[...], i.g_through_low[...])) - old

        if step == 4:
            one = i.one[...] + got(1, 0)
            half = one.shape[0] // 2
            o.one[...] = one
            o.fourth[...] = i.base4[...] + 2.0 * correlate(*arrived, i.f_through_high[...], i.f_through_low[...])
            group = [o.fourth[...], i.fifth[...], newest(i.base6[...], i.grad2[...])]
            o.two[...], away = parted(jnp.concatenate(group, axis=0))
            extra = {1: [away], 2: [one[:half]], 3: [one[half:]]}
        if step == 5:
            one = added(i.one[...], got(2, 0), got(3, 0))
            two = i.two[...] + got(1, 0)
            half, quarter = one.shape[0] // 2, two.shape[0] // 2
            o.one[...], o.two[...] = one, two
            o.seven[...] = newest(i.base[...], i.third[...])
            extra = {1: [o.seven[...]], 2: [one[half:], two[:quarter]], 3: [one[:half], two[quarter:]]}
        if step == 6:
            one = added(i.one[...], got(3, 0), got(2, 0))
            two = added(i.two[...], got(2, 1), got(3, 1))
            seven = i.seven[...] + got(1, 0)
            eight = newest(i.base[...], i.fourth[...])
            half, quarter = seven.shape[0] // 2, two.shape[0] // 2
            o.one[...], o.two[...], o.seven[...], o.eight[...] = one, two, seven, eight
            extra = {
                1: [eight],
                2: [two[quarter:], seven[:half], eight],
                3: [two[:quarter], seven[half:], eight],
            }
        if step == 7:
            two = added(i.two[...], got(3, 0), got(2, 0))
            seven = added(i.seven[...], got(2, 1), got(3, 1))
            near, (m2, p2) = got(1, 0), from_pairs({2: got(2, 2), 3: got(3, 2)})
            half = seven.shape[0] // 2
            o.two[...], o.seven[...] = two, seven
            o.eight[...] = i.eight[...] + near + m2 + p2
            on = pairs_of_two(near, near + p2)
            across = jnp.where(sides()[0] == 1, m2, p2)
            extra = {0: [across], 1: [two, i.one[...]], 2: [seven[half:], on[2]], 3: [seven[:half], on[3]]}
        write_sends(o, parts, extra)

    return quick


def halo_product(i, lhs, rows, here, nodes):
    return summed(dot(lhs, i.high[nodes:, here])) + dot(lhs[:rows], i.low[nodes:, here])


def split_halos(i, rows):
    got = [getattr(i, f"halo{k}") for k in range(SLOTS)]
    high, low = halves(jnp.concatenate([ref[:rows, :] for ref in got], axis=1))
    return jnp.concatenate([high, low], axis=0)


def make_outer(step, chains, following, ring):
    def outer(i, o):
        rows, nodes = i.part.shape
        local = rows // chains
        lhs = split_halos(i, rows)
        for start in range(0, nodes, WIDE):
            here = slice(start, start + WIDE)
            total = halo_product(i, lhs, rows, here, nodes)
            for chain in range(chains):
                mine = slice(chain * local, (chain + 1) * local)
                state = i.part[mine, here] + (1.0 if chain == 1 and step == 1 else 2.0) * total[mine]
                o.state[mine, here] = state
                high, low = halves(state)
                o.both[mine, here] = high
                o.both[rows + chain * local : rows + (chain + 1) * local, here] = low
        live = following * local
        moving = o.both[...]
        if following < chains:
            moving = jnp.concatenate([o.both[:live], o.both[rows : rows + live]], axis=0)
        if step not in QUICK:
            parts = [summed(dot(moving, i.pick[...]))]
        if step <= 2:
            got = [getattr(i, f"halo{k}")[rows : rows + local, :] for k in range(SLOTS)]
            high, low = halves(jnp.concatenate(got, axis=1))
            lhs = jnp.concatenate([high, low], axis=0)
            for start in range(0, nodes, WIDE):
                here = slice(start, start + WIDE)
                total = summed(dot(lhs, i.pick[here, :], (1, 1)))
                high, low = halves(i.fpart[:, here] + (1.0 if step == 1 else 2.0) * total)
                o.fboth[:local, here] = high
                o.fboth[local:, here] = low
        if step in QUICK:
            return
        extra = None
        if ring:
            if chains > 1:
                state = o.both[local : 2 * local], o.both[rows + local : rows + 2 * local]

            def got(kind, index):
                return carried(i, step, rows, kind, index)

            def newest(old):
                return 2.0 * correlate(*state, i.g_high[...], i.g_low[...]) - old

            if step == 3:
                o.third[...] = correlate(*state, i.feat_t[...])
                group = jnp.concatenate([i.grad0[...], i.grad1[...], i.grad2[...], o.third[...]], axis=0)
                o.one[...], away = parted(group)
                extra = {1: [away]}
        write_sends(o, parts, extra)

    return outer


def settle(i, o):
    blocks = [ref for name, ref in vars(i).items() if name.startswith("block")]
    rows = blocks[0].shape[0] // 2
    for half, out in ((slice(0, rows), o.g_high), (slice(rows, None), o.g_low)):
        collect([ref[half, :] for ref in blocks], o.whole)
        out[...] = transposed(o.whole[...])
    local = i.both.shape[0] // 4
    o.fifth[...] = 2.0 * correlate(
        i.both[local : 2 * local], i.both[3 * local :], o.g_high[...], o.g_low[...]
    ) - i.grad1[...]
    nodes = i.part.shape[1]
    part = halves(i.part[local:, :])
    o.base4[...] = correlate(*part, i.feat_t[...])
    o.base6[...] = correlate(*part, o.g_high[...], o.g_low[...])
    high, low = i.high[nodes:, :], i.low[nodes:, :]
    product = dot(high, i.feat_t[...]) + dot(low, i.feat_t[...])
    o.f_through_high[...], o.f_through_low[...] = halves(product)
    product = dot(high, o.g_high[...]) + dot(high, o.g_low[...]) + dot(low, o.g_high[...])
    o.g_through_high[...], o.g_through_low[...] = halves(product)


def make_last(step, scale, ring):
    def last(i, o):
        rows, nodes = i.part.shape
        lhs = split_halos(i, rows)
        for start in range(0, nodes, WIDE):
            here = slice(start, start + WIDE)
            o.result[:, here] = i.part[:, here] + halo_product(i, lhs, rows, here, nodes)
        if not ring:
            return

        def got(kind, index):
            return carried(i, step, rows, kind, index)

        def put(k, chunk):
            size = chunk.shape[0] // 2
            o.grads[k] = scale * jnp.concatenate([chunk[:size], chunk[size:]], axis=1)

        size = i.eight.shape[0]
        one, two = joined(i.one[...], got(1, 1)), joined(i.two[...], got(1, 0))
        for k in range(4):
            put(k, one[k * size : (k + 1) * size])
        for k in range(3):
            put(4 + k, two[k * size : (k + 1) * size])
        put(7, added(i.seven[...], got(3, 0), got(2, 0)))
        m2, p2 = from_pairs({2: got(2, 1), 3: got(3, 1)})
        put(8, i.eight[...] + m2 + p2 + got(0, 0))

    return last


def local(features, cotangent, weights, tile_values, tile_cols, send_list):
    top = weights.shape[0] - 1
    channels, nodes = features.shape
    tile = tile_values.shape[-1]
    every = weights.shape[2]
    wide = nodes + SLOTS * tile
    parts = lax.axis_size("dom")
    ring = parts == RING and top == RING and channels * every == tile * tile and tile == 128
    scale = float(parts * nodes) ** (-0.5)
    sent_shape = ((channels, SLOTS * tile), F32, True)
    whole = ((every, nodes), BF16, True)
    turned = ((nodes, every), BF16, True)
    chunk = ((2 * channels, every // 2), F32, True)
    along = ((SLOTS * tile, every), BF16, True)

    stacked = call(
        stack,
        dict(upper=(cotangent, "hbm"), lower=(features, "hbm")),
        dict(both=((2 * channels, nodes), BF16, True)),
        [pltpu.SemaphoreType.DMA((2,))],
    )["both"]
    ready = call(
        prepare,
        dict(
            cols=(tile_cols, "smem"),
            lists=(send_list, "load"),
            tiles=(tile_values, "hbm"),
            stacked=stacked,
        ),
        dict(
            high=((wide, nodes), BF16, True),
            low=((wide, nodes), BF16, True),
            pick=((nodes, SLOTS * tile), BF16, True),
            back=sent_shape,
            sent=sent_shape,
        ),
        [
            pltpu.VMEM((wide, nodes), F32),
            pltpu.VMEM(tile_values.shape, F32),
            pltpu.SemaphoreType.DMA((nodes // tile,)),
        ],
        flops=10**10,
    )
    matrix = dict(high=ready["high"], low=ready["low"])
    pick = dict(pick=ready["pick"])
    blocks = gather((stacked, hop(stacked, lax.axis_size("chan") // 2)), ready["back"])

    def messages(rows, step):
        extra = LAYOUT.get(step, {}) if ring else {}
        return {
            f"send{k}": ((rows + sum(extra.get(kind, ())), tile), F32, False) for k, kind in enumerate(KINDS)
        }

    def state_outs(chains):
        rows = chains * channels
        return dict(state=((rows, nodes), F32, True), both=((2 * rows, nodes), BF16, True))

    def pass_through(i, o):
        for matrix, out in ((i.high, o.through_high), (i.low, o.through_low)):
            out[...] = dot(matrix[nodes:, :], i.pick[...]).astype(BF16)

    through = ((SLOTS * tile, SLOTS * tile), BF16, True)
    through = call(pass_through, dict(**matrix, **pick), dict(through_high=through, through_low=through))

    sent_first = lax.optimization_barrier((ready["sent"], through["through_high"]))[0]
    named = {f"block{k}": (block, "") for k, block in enumerate(blocks[1:])}
    got = call(
        begin,
        dict(
            stacked=stacked,
            weight=(weights[top], ""),
            **pick,
            sent=sent_first,
            back=ready["back"],
            **named,
        ),
        dict(gathered=whole, **state_outs(2), **messages(3 * channels, 1)),
    )
    gathered = got["gathered"]

    def opening(i, o):
        rows = [ref[channels:, :] for name, ref in vars(i).items() if name.startswith("block")]
        collect([i.stacked[channels:]] + rows, o.whole)
        o.feat_t[...] = transposed(o.whole[...])
        o.grad0[...] = correlate(i.stacked[:channels], None, o.feat_t[...])
        for ref, out in ((i.both1, o.grad1), (i.both2, o.grad2)):
            out[...] = correlate(ref[channels : 2 * channels], ref[3 * channels :], o.feat_t[...])

    before, boths, grads, back = None, {}, {}, None
    for step in range(1, top + 1):
        chains = 2 if step <= top - 2 else 1
        following = 2 if step + 1 <= top - 2 else 1
        halos = {f"halo{k}": (x, "") for k, x in enumerate(exchange([got[f"send{k}"] for k in range(SLOTS)]))}
        ins = dict(both=got["both"], weight=(weights[top - step], ""), gathered=gathered, **matrix)
        outs = dict(part=((chains * channels, nodes), F32, True))
        if step > 1:
            ins["before"] = before
        if step in QUICK:
            ins.update(pick)
            outs["picked"] = ((chains * channels, SLOTS * tile), F32, True)
        if step in (5, 6):
            ins.update(g_high=back["g_high"], g_low=back["g_low"])
            outs["base"] = chunk
        if step == 1:
            outs["back"] = sent_shape
        if step <= 2:
            ins["stacked"] = stacked
            outs["fpart"] = ((channels, nodes), F32, True)
        if step == 2:
            ins["fboth"] = got["fboth"]
        inside = call(
            make_inner(step, top, chains), ins, outs, flops=2 * chains * channels * nodes * nodes * 3
        )
        part = inside["part"]
        if step == 3:
            opened = call(
                opening,
                dict(stacked=stacked, **named, both1=boths[1], both2=boths[2]),
                dict(whole=whole, feat_t=turned, **{f"grad{k}": chunk for k in range(3)}),
            )
            feat_t, grads = opened["feat_t"], {k: opened[f"grad{k}"] for k in range(3)}
        if step == 3:
            back_blocks = got["fboth"], hop(got["fboth"], lax.axis_size("chan") // 2)
        if step == 4:
            back = call(
                settle,
                dict(
                    **{f"block{k}": (x, "") for k, x in enumerate(gather(back_blocks, got["send0"]))}, both=boths[3],
                    grad1=grads[1],
                    part=part,
                    feat_t=feat_t,
                    **matrix,
                ),
                dict(
                    g_high=turned, g_low=turned, whole=whole, fifth=chunk, base4=chunk, base6=chunk,
                    **{f"{name}_through_{half}": along for name in "fg" for half in ("high", "low")},
                ),
            )
        ins = dict(part=part, **matrix, **halos)
        if step == top:
            outs = dict(result=((channels, nodes), F32, False))
            if ring:
                ins.update({k: got[k] for k in ("one", "two", "seven", "eight")})
                outs["grads"] = ((top + 1, channels, every), F32, False)
            got = call(make_last(step, scale, ring), ins, outs)
            break
        ins.update(pick)
        outs = state_outs(chains)
        if step <= 2:
            ins["fpart"] = inside["fpart"]
            outs["fboth"] = ((2 * channels, nodes), BF16, True)
        if ring and step == 3:
            ins.update(feat_t=feat_t, **{f"grad{k}": grads[k] for k in range(3)})
            outs.update(one=((4 * channels, every // 2), F32, True), third=chunk)
        sent = following + (1 if step == 1 else 0)
        sends = messages(sent * channels, step + 1)
        ready = {}
        if step in QUICK:
            told = dict(picked=inside["picked"], **through, **halos)
            if step == 1:
                told["back"] = inside["back"]
            if ring and step >= 4:
                told["one"] = got["one"]
                if step < 7:
                    sends["one"] = ((4 * channels, every // 2), F32, True)
                else:
                    ready["one"] = got["one"]
                sends["two"] = ((3 * channels, every // 2), F32, True)
                if step >= 5:
                    told["two"] = got["two"]
                    sends["seven"] = chunk
                if step >= 6:
                    told["seven"] = got["seven"]
                    sends["eight"] = chunk
                if step in (4, 5, 6):
                    told.update({k: back[k] for k in ("g_through_high", "g_through_low")})
                if step == 4:
                    told.update(grad2=grads[2], **{k: x for k, x in back.items() if k in BESIDE})
                    sends["fourth"] = chunk
                if step == 5:
                    told.update(base=inside["base"], third=third)
                if step == 6:
                    told.update(base=inside["base"], fourth=fourth)
                if step == 7:
                    told["eight"] = got["eight"]
            ready.update(call(make_quick(step, chains, following, ring), told, sends))
        else:
            outs.update(sends)
        before = got["state"]
        weight = 2 * chains * channels * nodes * nodes * 3 if step in QUICK else 0
        got = call(make_outer(step, chains, following, ring and step == 3), ins, outs, flops=weight)
        got.update(ready)
        if ring and step == 3:
            third = got["third"]
        if ring and step == 4:
            fourth = got["fourth"]
        boths[step] = got["both"]
    if ring:
        return got["result"], jnp.swapaxes(got["grads"], 1, 2)

    def rest(i, o):
        for k in range(3):
            o.out[k] = getattr(i, f"grad{k}")[...]
        o.out[5] = i.fifth[...]
        for k in range(3, 7):
            ref = getattr(i, f"both{k}")
            state = ref[channels : 2 * channels], ref[3 * channels :]
            if k <= 4:
                o.out[k] = correlate(*state, i.feat_t[...])
            if k >= 4:
                o.out[k + 2] = 2.0 * correlate(*state, i.g_high[...], i.g_low[...]) - o.out[k - 2]

    total = call(
        rest,
        dict(
            feat_t=feat_t,
            fifth=back["fifth"],
            g_high=back["g_high"],
            g_low=back["g_low"],
            **{f"grad{k}": grads[k] for k in range(3)},
            **{f"both{k}": boths[k] for k in range(3, 7)},
        ),
        dict(out=((top + 1, 2 * channels, every // 2), F32, True)),
    )["out"]
    total = lax.psum(total, "dom").reshape(top + 1, 2, channels, every // 2)
    return got["result"], total.transpose(0, 1, 3, 2).reshape(top + 1, every, channels) * scale


def solution(mesh):
    placed = (
        P("chan", "dom"),
        P("chan", "dom"),
        P(None, "chan", None),
        P("dom", None, None),
        P("dom", None, None),
        P("dom", None, None),
    )
    return jax.shard_map(
        local,
        mesh=mesh,
        in_specs=placed,
        out_specs=(P("chan", "dom"), P(None, None, "chan")),
        check_vma=False,
    )
```
